32 devices in a mesh: lat: 8 (over z, core), lon: 4 (over y, x).
Axes of the slice: x: 2, y: 2, z: 4, core: 2. Of those that a mesh axis runs over, the one named last changes fastest.
Arguments:
- fields: bfloat16 [512, 16, 16, 128], P(None, 'lat', 'lon'), may hold values from -6 to 6
- chan_mean: float32 [128], replicated, may hold values from -1 to 1
- chan_std: float32 [128], replicated, may hold values from 0.5 to 2
- sea_mask: int32 [512, 16, 16], P(None, 'lat', 'lon'), may hold values from 0 to 1, as said below
- missing: int32 [512, 16, 16], P(None, 'lat', 'lon'), may hold values from 0 to 1, as said below
- cotangent: bfloat16 [512, 16, 16, 128], P(None, 'lat', 'lon'), may hold values from -6 to 6
- w_master: float32 [2, 1152, 128], P(None, 'lat', 'lon'), may hold values from -0.1875 to 0.1875
- w_first: float32 [2, 1152, 128], P(None, 'lat', 'lon'), may hold values from -0.0012207031 to 0.0012207031
- w_second: float32 [2, 1152, 128], P(None, 'lat', 'lon'), may hold values from 3.3864327e-09 to 1.3545731e-08
- vec_master: float32 [3, 128], replicated, may hold values from -1 to 2.16
- vec_first: float32 [3, 128], replicated, may hold values from -0.0012207031 to 0.0012207031
- vec_second: float32 [3, 128], replicated, may hold values from 3.3864327e-09 to 1.3545731e-08
Outputs:
- block_out: bfloat16 [512, 16, 16, 128], P(None, 'lat', 'lon')
- field_grad: float32 [512, 16, 16, 128], P(None, 'lat', 'lon')
- grad_norm: float32 [], replicated
- w_new: float32 [2, 1152, 128], P(None, 'lat', 'lon')
- w_first_new: float32 [2, 1152, 128], P(None, 'lat', 'lon')
- w_second_new: float32 [2, 1152, 128], P(None, 'lat', 'lon')
- w_low: bfloat16 [2, 1152, 128], P(None, 'lat', 'lon')
- vec_new: float32 [3, 128], replicated
- vec_first_new: float32 [3, 128], replicated
- vec_second_new: float32 [3, 128], replicated
The draws below stay inside these ranges and needn't reach their ends.
Inputs may be any that keep to these rules, and one draw needn't show every extreme that they name: `sea_mask`: 1 marks sea; in every sample the pixel in the last latitude row and last longitude column is sea. `missing`: 1 marks a pixel without data; in every sample the pixel in the last latitude row and last longitude column has data.
All inputs are finite; a program needn't handle non-finite values.
Results may differ from the reference program's by a relative error of at most 0.0053.
Values may be sent and summed in bfloat16 or wider, within the bound.
A program may use at most 128 MiB of HBM per device.

```python
import math
import jax
import jax.numpy as jnp
from jax import lax

C = 128
B = 512
STEP = 10
NLAT = 16
NLON = 16


def draw_sea_mask(key, part):
    sub_key = jax.random.fold_in(key, 11)
    lat_pos = jnp.arange(NLAT, dtype=jnp.int32)[:, None]
    lon_pos = jnp.arange(NLON, dtype=jnp.int32)[None, :]
    threshold = 1000 * (NLAT - 1 + 2 * lat_pos) * (NLON - 1 + 2 * lon_pos) // (9 * (NLAT - 1) * (NLON - 1))
    dice_rolls = jax.random.randint(sub_key, (B, NLAT, NLON), 0, 1000)
    sea_cells = (dice_rolls < threshold[None]).astype(jnp.int32)
    return sea_cells.at[:, NLAT - 1, NLON - 1].set(1)


def draw_missing(key, part):
    sub_key = jax.random.fold_in(key, 17)
    dice_rolls = jax.random.randint(sub_key, (B, NLAT, NLON), 0, 100)
    gaps = (dice_rolls < 15).astype(jnp.int32)
    return gaps.at[:, NLAT - 1, NLON - 1].set(0)


def draw_vec_master(key, part):
    sub_keys = jax.random.split(jax.random.fold_in(key, 29), 2)
    channel_ramp = 0.6 + 1.2 * jnp.arange(C, dtype=jnp.float32) / (C - 1)
    biases = jnp.clip(0.4 * jax.random.normal(sub_keys[0], (2, C), jnp.float32), -1.0, 1.0)
    wobble = jax.random.uniform(sub_keys[1], (C,), jnp.float32, 0.8, 1.2)
    gain_row = channel_ramp * wobble
    return jnp.stack([gain_row, biases[0], biases[1]]).astype(jnp.float32)


def levels(stream_key, shape, cuts, smallest, high):
    factor_of = 1.0
    for position, shards_of in cuts:
        heights = jax.random.uniform(jax.random.fold_in(jax.random.fold_in(stream_key, 6), position), (shards_of,), jnp.float32, smallest / len(cuts), high / len(cuts))
        factor_of = factor_of * jnp.repeat(jnp.exp(heights), shape[position] // shards_of).reshape((-1,) + (1,) * (len(shape) - 1 - position))
    return factor_of


def noise(stream_key, dims, scale, bound, shards=(), held_as=jnp.bfloat16):
    entries = scale * jax.random.normal(stream_key, dims, jnp.float32)
    if shards:
        entries = entries * levels(stream_key, dims, shards, -0.22, 0.18)
    return jnp.clip(entries, -bound, bound).astype(held_as)


def setup_inputs(seed: int = 0) -> dict:
    key_of = jax.random.split(jax.random.key(seed), 13)
    fields = noise(key_of[0], (B, NLAT, NLON, C), 1.0, 6.0, ((1, 8), (2, 4)))
    chan_mean = jnp.clip(jax.random.uniform(key_of[1], (C,), jnp.float32, -1.0, 1.0), -1.0, 1.0)
    chan_std = jnp.clip(jnp.exp(jax.random.uniform(key_of[2], (C,), jnp.float32, math.log(0.5), math.log(2.0))), 0.5, 2.0)
    sea_mask = draw_sea_mask(jax.random.fold_in(key_of[12], 71), 0)
    missing = draw_missing(jax.random.fold_in(key_of[12], 71), 0)
    cotangent = noise(key_of[5], (B, NLAT, NLON, C), 1.0, 6.0, ((1, 8), (2, 4)))
    w_master = noise(key_of[6], (2, 9 * C, C), (9 * C) ** -0.5, 0.1875, ((1, 8), (2, 4)), jnp.float32)
    w_first = noise(key_of[7], (2, 9 * C, C), (0.111 / (18 * C * C + 3 * C) ** 0.5), 0.0012207031, ((1, 8), (2, 4)), jnp.float32)
    w_second = jnp.clip(jnp.exp(math.log(1.3545730759290109e-08) - 1.3862944 * jax.random.uniform(key_of[8], (2, 9 * C, C), jnp.float32) ** levels(key_of[8], (2, 9 * C, C), ((1, 8), (2, 4)), -0.2, 0.2)), 3.3864326898225272e-09, 1.3545730759290109e-08)
    vec_master = draw_vec_master(jax.random.fold_in(key_of[12], 71), 0)
    vec_first = noise(key_of[10], (3, C), (0.111 / (18 * C * C + 3 * C) ** 0.5), 0.0012207031, (), jnp.float32)
    vec_second = jnp.clip(jnp.exp(jax.random.uniform(key_of[11], (3, C), jnp.float32, math.log(3.3864326898225272e-09), math.log(1.3545730759290109e-08))), 3.3864326898225272e-09, 1.3545730759290109e-08)
    return {"fields": fields, "chan_mean": chan_mean, "chan_std": chan_std, "sea_mask": sea_mask, "missing": missing, "cotangent": cotangent, "w_master": w_master, "w_first": w_first, "w_second": w_second, "vec_master": vec_master, "vec_first": vec_first, "vec_second": vec_second}


EPS = 1e-05
MAX_NORM = 1.0
BETA_ONE = 0.9
BETA_TWO = 0.999
ADAM_EPS = 1e-08
RATE_KERNEL = 0.02
RATE_VECTOR = 0.1
DECAY = 0.01

@jax.custom_vjp
def low(v):
    return lax.optimization_barrier(v.astype(jnp.bfloat16)).astype(jnp.float32)

@jax.custom_vjp
def low_back(v):
    return v

def low_keep(v):
    return (low(v), None)

def low_pass(kept, grad):
    return (grad,)

def back_keep(v):
    return (v, None)

def back_low(kept, grad):
    return (low(grad),)
low.defvjp(low_keep, low_pass)
low_back.defvjp(back_keep, back_low)

def smooth_leaky(values):
    return 0.3 * values + 0.7 * jax.nn.softplus(values)

def pad_field(values):
    wrapped = jnp.concatenate([values[:, :, -1:], values, values[:, :, :1]], axis=2)
    return jnp.pad(wrapped, ((0, 0), (1, 1), (0, 0), (0, 0)))

def convolve(values, kernel):
    channels = kernel.shape[1]
    taps = kernel.reshape(3, 3, channels, channels)
    return lax.conv_general_dilated(pad_field(values), taps, (1, 1), 'VALID', dimension_numbers=('NHWC', 'HWIO', 'NHWC'), precision=lax.Precision.HIGHEST)

def forward(field_values, kernels, vectors, chan_mean, chan_std, present, counted):
    standard = (field_values - chan_mean) / chan_std * present
    first_pre = low_back(convolve(low(standard), low(kernels[0])))
    first_act = smooth_leaky(first_pre)
    total = jnp.sum(counted)
    center = lax.optimization_barrier(jnp.sum(counted * first_act, axis=(0, 1, 2))) / total
    offset = first_act - center
    spread = lax.optimization_barrier(jnp.sum(counted * offset * offset, axis=(0, 1, 2))) / total
    normed = offset * lax.rsqrt(spread + EPS)
    scaled = normed * vectors[0] + vectors[1]
    second_pre = low_back(convolve(low(scaled), low(kernels[1])) + vectors[2])
    return standard + smooth_leaky(second_pre)

def adam_step(master, first, second, grads, rate, decay):
    first_new = BETA_ONE * first + (1.0 - BETA_ONE) * grads
    second_new = BETA_TWO * second + (1.0 - BETA_TWO) * grads * grads
    first_hat = first_new / (1.0 - BETA_ONE ** STEP)
    second_hat = second_new / (1.0 - BETA_TWO ** STEP)
    master_new = master - rate * (first_hat / (jnp.sqrt(second_hat) + ADAM_EPS) + decay * master)
    return (master_new, first_new, second_new)

def reference(fields, chan_mean, chan_std, sea_mask, missing, cotangent, w_master, w_first, w_second, vec_master, vec_first, vec_second):
    present = (1 - missing).astype(jnp.float32)[..., None]
    counted = (sea_mask * (1 - missing)).astype(jnp.float32)[..., None]

    def forward_of(field_values, kernels, vectors):
        return forward(field_values, kernels, vectors, chan_mean, chan_std, present, counted)
    block_value, pullback = jax.vjp(forward_of, fields.astype(jnp.float32), w_master, vec_master)
    field_grad, kernel_grad, vector_grad = pullback(cotangent.astype(jnp.float32))
    grad_norm = jnp.sqrt(jnp.sum(kernel_grad * kernel_grad) + jnp.sum(vector_grad * vector_grad))
    factor = jnp.minimum(1.0, MAX_NORM / grad_norm)
    w_new, w_first_new, w_second_new = adam_step(w_master, w_first, w_second, kernel_grad * factor, RATE_KERNEL, DECAY)
    vec_new, vec_first_new, vec_second_new = adam_step(vec_master, vec_first, vec_second, vector_grad * factor, RATE_VECTOR, 0.0)
    return (block_value.astype(jnp.bfloat16), field_grad, grad_norm, w_new, w_first_new, w_second_new, w_new.astype(jnp.bfloat16), vec_new, vec_first_new, vec_second_new)
```

```python
import functools

import jax
import jax.numpy as jnp
from jax import lax
from jax.experimental import pallas as pl
from jax.experimental.pallas import tpu as pltpu
from jax.sharding import PartitionSpec as P

STEP = 10
EPS = 1e-05
MAX_NORM = 1.0
BETA_ONE = 0.9
BETA_TWO = 0.999
ADAM_EPS = 1e-08
RATE_KERNEL = 0.02
RATE_VECTOR = 0.1
DECAY = 0.01

MESH = pl.DeviceIdType.MESH
BF = jnp.bfloat16
F32 = jnp.float32
C = 128
R = 2
W = R * C
FIRST, SECOND = 0, 1


def cols_of(i):
    return slice(i * C, (i + 1) * C)


def twice(row):
    return jnp.concatenate([row, row], axis=1)


def fold(row):
    return row[:, :C] + row[:, C:]


def to_eight(block):
    rows, width = block.shape
    return jnp.sum(block.reshape(rows // 8, 8, width), axis=0)


def total_row(block):
    return jnp.sum(block, axis=0, keepdims=True)


def both_masks(missing, sea):
    have = (1 - missing).astype(F32)
    present = jnp.concatenate([have[0], have[1]], axis=0)
    counted = None
    if sea is not None:
        land = have * sea.astype(F32)
        counted = jnp.concatenate([land[0], land[1]], axis=0)
    return present, counted


def smooth(value):
    small = jnp.exp(-jnp.abs(value))
    one = 1.0 + small
    soft = jnp.maximum(value, 0.0) + jnp.log(one)
    sigmoid = jnp.where(value >= 0.0, 1.0, small) / one
    return 0.3 * value + 0.7 * soft, 0.3 + 0.7 * sigmoid


class Sizes:
    def __init__(self, nla, nlo, samples, quads, wrows, wcols):
        self.nla, self.nlo = nla, nlo
        self.n = nla * nlo
        self.B, self.Q = samples, quads
        self.PX = R * quads
        self.S = samples // nlo
        self.L = quads * nlo
        self.CH = self.S // 4 if self.S % 64 == 0 else 16
        self.nch = self.S // self.CH
        self.wr, self.wc = wrows, wcols
        self.LP = -(-wrows // 128) * 128


def main_kernel(
    z,
    fields, cot, sea, missing, mean, std, wt, vec,
    ob, fo, gw, gv, gn,
    fin, cin, fb, pres, cm, cnt, sb, cb,
    X, H, G, F, act, slope, sg, ct, pre, bo, fs,
    w1, w2, t1, t2, acc1, acc2,
    ws, wg, kg_in, kf, kl,
    rsb, rr, kform, ssum, ts, lb, lr,
    y1, y2, y3,
    load_sem, mask_s, mask_r, f_s, f_r, c_s, c_r, halo_s, halo_r,
    bo_s, bo_r, fo_s, fo_r, wg_s, wg_r, kz_s, kz_r, kc_s, kc_r,
    ra_s, ra_r, ro_s, ro_r, y_s, y_r,
):
    nla, nlo, n = z.nla, z.nlo, z.n
    S, L, Q, CH, nch = z.S, z.L, z.Q, z.CH, z.nch
    la = lax.axis_index("lat")
    lo = lax.axis_index("lon")
    me = la * nlo + lo

    def remote(src, dst, ss, rs, lat_to, lon_to):
        return pltpu.make_async_remote_copy(
            src, dst, ss, rs, device_id=(lat_to, lon_to), device_id_type=MESH
        )

    def loop(low, high, body):
        def step(k, carry):
            body(k)
            return carry
        lax.fori_loop(low, high, step, 0)

    def others(body):
        def row(i):
            def one(j):
                @pl.when(jnp.logical_or(i != la, j != lo))
                def _():
                    body(i, j)
            loop(0, nlo, one)
        loop(0, nla, row)

    def chunk(c):
        return pl.ds(pl.multiple_of(c * CH, CH), CH)

    def peer(k):
        return lax.rem(lo + k, nlo)

    barrier = pltpu.get_barrier_semaphore()
    others(lambda i, j: pl.semaphore_signal(barrier, inc=1, device_id=(i, j), device_id_type=MESH))
    load_f = pltpu.make_async_copy(fields, fin, load_sem.at[0])
    load_c = pltpu.make_async_copy(cot, cin, load_sem.at[1])
    load_f.start()
    load_c.start()

    present, counted = both_masks(missing[...], sea[...])
    pres[...] = present.T
    cm[lo] = counted
    pad = z.LP - z.wr
    for k in range(2):
        block = wt[k].astype(BF)
        if pad:
            block = jnp.concatenate([block, jnp.zeros((z.wc, pad), BF)], axis=1)
        ws[k] = block
        wg[lo, k] = block
    for ref in (X, H, G, F):
        @pl.when(la == 0)
        def _():
            ref[:, :, cols_of(0)] = jnp.zeros((L + 2, S, C), BF)

        @pl.when(la == nla - 1)
        def _():
            ref[:, :, cols_of(3)] = jnp.zeros((L + 2, S, C), BF)

    pl.semaphore_wait(barrier, n - 1)

    def w_copy(k):
        m = peer(k)
        return remote(ws, wg.at[lo], wg_s.at[k], wg_r.at[k], la, m)

    def mask_copy(k):
        return remote(cm.at[lo], cm.at[lo], mask_s.at[k], mask_r.at[k], la, peer(k))

    loop(1, nlo, lambda k: w_copy(k).start())
    load_f.wait()

    rstd = 1.0 / std[...]
    center_in = mean[...]

    def place(src, t, c, put, standardize):
        first = pl.multiple_of((t * S + c * CH) * z.PX, CH * z.PX)
        fb[...] = src[pl.ds(first, CH * z.PX), :].astype(F32)
        here = pres[pl.ds(pl.multiple_of(t * S + c * CH, CH), CH), :]
        for p in range(z.PX):
            value = fb[pl.ds(p, CH, stride=z.PX), :]
            if standardize:
                value = (value - center_in) * rstd * here[:, p : p + 1]
            put(p // Q, p % Q, value.astype(BF))

    def f_copy(c, k):
        return remote(
            sb.at[c, k], X.at[pl.ds(1 + Q * lo, Q), chunk(c), pl.ds(C, W)],
            f_s.at[c, k], f_r.at[c, k], la, peer(k),
        )

    def c_copy(c, k):
        return remote(
            cb.at[c, k], ct.at[pl.ds(Q * lo, Q), chunk(c), :],
            c_s.at[c, k], c_r.at[c, k], la, peer(k),
        )

    def send_fields(c):
        def one(k):
            def put(i, q, value):
                sb[c, k, q, :, cols_of(i)] = value
            place(fin, peer(k), c, put, True)
            f_copy(c, k).start()
        loop(1, nlo, one)

    def own_fields(c):
        def put(i, q, value):
            X[1 + Q * lo + q, chunk(c), cols_of(i + 1)] = value
        place(fin, lo, c, put, True)

    def own_cot(c):
        def put(i, q, value):
            ct[Q * lo + q, chunk(c), cols_of(i)] = value
        place(cin, lo, c, put, False)

    def prep_cot(c):
        def one(k):
            def put(i, q, value):
                cb[c, k, q, :, cols_of(i)] = value
            place(cin, peer(k), c, put, False)
        loop(1, nlo, one)

    loop(0, nch, send_fields)
    loop(1, nlo, lambda k: mask_copy(k).start())
    loop(0, nch, own_fields)

    loop(1, nlo, lambda k: w_copy(k).wait_recv())
    for k in range(2):
        gathered = jnp.concatenate([wg[m, k].astype(F32) for m in range(nlo)], axis=0)
        kl[k] = gathered.T[: z.wr].astype(BF)
        kg_in[k, la] = kl[k]
    core = lax.rem(la, 2)
    sibling = la + 1 - 2 * core

    def kz_copy(k, d):
        to = lax.rem(la + 2 * d, nla)
        return remote(kl.at[k], kg_in.at[k, la], kz_s.at[k, d], kz_r.at[k, d], to, lo)

    def kc_copy(k, d):
        row = lax.rem(la + nla - 2 * d, nla)
        return remote(kg_in.at[k, row], kg_in.at[k, row], kc_s.at[k, d], kc_r.at[k, d], sibling, lo)

    def start_kernel(k):
        loop(1, nla // 2, lambda d: kz_copy(k, d).start())
        kc_copy(k, 0).start()

    def forward_kernel(k):
        def one(d):
            kz_copy(k, d).wait_recv()
            kc_copy(k, d).start()
        loop(1, nla // 2, one)

    def finish_kernel(k):
        loop(0, nla // 2, lambda d: kc_copy(k, d).wait_recv())
        for i in range(nla):
            kf[pl.ds(i * z.wr, z.wr), :] = kg_in[k, i].astype(F32)

    def tap(a, b):
        return kf[pl.ds((3 * a + b) * C, C), :]

    def build_forward(ref):
        for b in range(3):
            for r in range(4):
                for i in range(R):
                    a = r - i
                    good = 0 <= a <= 2
                    block = tap(a, b).astype(BF) if good else jnp.zeros((C, C), BF)
                    ref[pl.ds((b * 4 + r) * C, C), cols_of(i)] = block

    def build_turned(ref):
        for b in range(3):
            for a in range(3):
                block = tap(2 - a, 2 - b).T.astype(BF)
                for i in range(R):
                    ref[pl.ds((b * 4 + a + i) * C, C), cols_of(i)] = block
            for i, r in ((0, 3), (1, 0)):
                ref[pl.ds((b * 4 + r) * C, C), cols_of(i)] = jnp.zeros((C, C), BF)

    start_kernel(FIRST)
    start_kernel(SECOND)

    load_c.wait()
    loop(0, nch, own_cot)
    loop(0, nch, prep_cot)
    loop(1, nlo, lambda k: mask_copy(k).wait_recv())
    rows = jnp.concatenate([cm[m] for m in range(nlo)], axis=0)
    back = z.B - lo * S
    mine = pltpu.roll(rows, lax.rem(back, z.B), 1)[:, : min(z.B, 128)].T
    for j in range(L):
        for i in range(R):
            col = (j // Q) * z.PX + i * Q + j % Q
            cnt[j, :, cols_of(i)] = jnp.broadcast_to(mine[:S, col : col + 1], (S, C))

    forward_kernel(FIRST)
    finish_kernel(FIRST)
    build_forward(w1)

    def halo_copies(ref, h, c):
        north = remote(
            ref.at[pl.ds(1, L), chunk(c), pl.ds(C, C)], ref.at[pl.ds(1, L), chunk(c), pl.ds(3 * C, C)],
            halo_s.at[h, c, 0], halo_r.at[h, c, 0], jnp.maximum(la - 1, 0), lo,
        )
        south = remote(
            ref.at[pl.ds(1, L), chunk(c), pl.ds(2 * C, C)], ref.at[pl.ds(1, L), chunk(c), pl.ds(0, C)],
            halo_s.at[h, c, 1], halo_r.at[h, c, 1], jnp.minimum(la + 1, nla - 1), lo,
        )
        return north, south

    def halo_send(ref, h, c):
        north, south = halo_copies(ref, h, c)
        pl.when(la > 0)(north.start)
        pl.when(la < nla - 1)(south.start)

    def halo_wait(ref, h, c):
        north, south = halo_copies(ref, h, c)
        pl.when(la < nla - 1)(north.wait_recv)
        pl.when(la > 0)(south.wait_recv)
        ref[0, chunk(c), :] = ref[L, chunk(c), :]
        ref[L + 1, chunk(c), :] = ref[1, chunk(c), :]

    def halo_done(ref, h, c):
        north, south = halo_copies(ref, h, c)
        pl.when(la > 0)(north.wait_send)
        pl.when(la < nla - 1)(south.wait_send)

    def taps(ref, c):
        parts = [ref[b : b + L, chunk(c), :].reshape(L * CH, 4 * C) for b in range(3)]
        return jnp.concatenate(parts, axis=1)

    def conv(lhs, kernel):
        out = jnp.dot(lhs, kernel[...], preferred_element_type=F32)
        pre[...] = out.reshape(L, CH, W)

    def kernel_grad(lhs, grad, acc):
        acc[...] += lax.dot_general(
            lhs, grad, (((0,), (0,)), ((), ())), preferred_element_type=F32
        )

    def columns(body, carry):
        return lax.fori_loop(0, L, body, carry)

    zero8 = jnp.zeros((8, W), F32)

    def arrive(c):
        loop(1, nlo, lambda k: f_copy(c, k).wait_recv())
        halo_send(X, 0, c)

    def first_chunk(c, stats):
        halo_wait(X, 0, c)
        conv(taps(X, c), w1)

        def one(j, carry):
            s, m = carry
            value, grad = smooth(pre[j])
            act[j, chunk(c), :] = value
            slope[j, chunk(c), :] = grad
            here = cnt[j, chunk(c), :]
            return s + to_eight(here * value), m + to_eight(here)

        s8, n8 = columns(one, (zero8, zero8))
        s_c, n_c = fold(total_row(s8)), fold(total_row(n8))
        mean_c = s_c / jnp.maximum(n_c, 1.0)
        mean_w = twice(mean_c)

        def two(j, m2):
            off = act[j, chunk(c), :] - mean_w
            return m2 + to_eight(cnt[j, chunk(c), :] * off * off)

        m_c = fold(total_row(columns(two, zero8)))
        n_0, s_0, m_0 = stats
        delta = mean_c - s_0 / jnp.maximum(n_0, 1.0)
        n_1 = n_0 + n_c
        m_1 = m_0 + m_c + delta * delta * (n_0 * n_c / jnp.maximum(n_1, 1.0))
        return n_1, s_0 + s_c, m_1

    def send_cot():
        def one(c):
            loop(1, nlo, lambda k: c_copy(c, k).start())
        loop(0, nch, one)

    arrive(0)
    zero1 = jnp.zeros((1, C), F32)

    def first_step(c, stats):
        @pl.when(c + 1 < nch)
        def _():
            arrive(c + 1)
            pl.when(c + 2 == nch)(send_cot)
        return first_chunk(c, stats)

    n_d, s_d, m_d = lax.fori_loop(0, nch, first_step, (zero1, zero1, zero1))

    def share(buf, which, value):
        buf[me] = value
        others(lambda i, j: remote(buf.at[me], buf.at[me], y_s.at[which], y_r.at[which], i, j).start())

    def shared(buf, which):
        block = remote(buf.at[pl.ds(0, n - 1)], buf.at[pl.ds(0, n - 1)], y_s.at[which], y_r.at[which], la, lo)
        block.wait_recv()
        block.wait_send()
        return buf[...]

    share(y1, 0, jnp.concatenate([n_d, s_d, m_d], axis=1))
    build_turned(t1)
    forward_kernel(SECOND)
    finish_kernel(SECOND)
    build_forward(w2)
    build_turned(t2)
    acc1[...] = jnp.zeros_like(acc1)
    acc2[...] = jnp.zeros_like(acc2)

    parts = shared(y1, 0)
    n_all, s_all, m_all = parts[:, :, :C], parts[:, :, C : 2 * C], parts[:, :, 2 * C :]
    total = jnp.sum(n_all, axis=0)
    center = jnp.sum(s_all, axis=0) / total
    apart = s_all / jnp.maximum(n_all, 1.0) - center[None]
    spread = jnp.sum(m_all + n_all * apart * apart, axis=0) / total
    inverse = lax.rsqrt(spread + EPS)
    gain, shift, bias = vec[0:1, :], vec[1:2, :], vec[2:3, :]
    center_w, inverse_w = twice(center), twice(inverse)
    gain_w, shift_w, bias_w = twice(gain), twice(shift), twice(bias)

    def hidden(c):
        def one(j, carry):
            normed = (act[j, chunk(c), :] - center_w) * inverse_w
            H[1 + j, chunk(c), pl.ds(C, W)] = (normed * gain_w + shift_w).astype(BF)
            return carry
        columns(one, 0)
        halo_send(H, 1, c)

    loop(0, nch, hidden)

    def out_copy(src, dst, ss, rs, c, k):
        m = peer(k)
        return remote(
            src.at[pl.ds(Q * m, Q), chunk(c), :],
            dst.at[:, pl.ds(pl.multiple_of(lo * S + c * CH, CH), CH), :],
            ss.at[c, k], rs.at[c, k], la, m,
        )

    def own_out(src, dst, ss, c):
        return pltpu.make_async_copy(
            src.at[pl.ds(Q * lo, Q), chunk(c), :],
            dst.at[:, pl.ds(pl.multiple_of(lo * S + c * CH, CH), CH), :],
            ss.at[c, 0],
        )

    def send_out(src, dst, ss, rs, c):
        loop(1, nlo, lambda k: out_copy(src, dst, ss, rs, c, k).start())
        own_out(src, dst, ss, c).start()

    def second_chunk(c, b8):
        halo_wait(H, 1, c)
        loop(1, nlo, lambda k: c_copy(c, k).wait_recv())
        lhs = taps(H, c)
        conv(lhs, w2)

        def one(j, carry):
            value, grad = smooth(pre[j] + bias_w)
            standard = X[1 + j, chunk(c), pl.ds(C, W)].astype(F32)
            bo[j, chunk(c), :] = (standard + value).astype(BF)
            low = (ct[j, chunk(c), :].astype(F32) * grad).astype(BF)
            G[1 + j, chunk(c), pl.ds(C, W)] = low
            return carry + to_eight(low.astype(F32))

        b8 = columns(one, b8)
        halo_send(G, 2, c)
        send_out(bo, ob, bo_s, bo_r, c)
        grad = G[1 : 1 + L, chunk(c), pl.ds(C, W)].reshape(L * CH, W)
        kernel_grad(taps(H, c), grad, acc2)
        return b8

    def back_chunk(c, carry):
        halo_wait(G, 2, c)
        conv(taps(G, c), t2)

        def one(j, carry):
            g8, s8 = carry
            value = pre[j]
            sg[j, chunk(c), :] = value
            normed = (act[j, chunk(c), :] - center_w) * inverse_w
            return g8 + to_eight(value * normed), s8 + to_eight(value)

        return columns(one, carry)

    b8 = second_chunk(0, zero8)

    def second_step(c, carry):
        b8, g8, s8 = carry
        b8 = second_chunk(c + 1, b8)
        g8, s8 = back_chunk(c, (g8, s8))
        return b8, g8, s8

    b8, g8, s8 = lax.fori_loop(0, nch - 1, second_step, (b8, zero8, zero8))
    g8, s8 = back_chunk(nch - 1, (g8, s8))
    sums = [fold(total_row(v)) for v in (g8, s8, b8)]
    share(y2, 1, jnp.concatenate(sums, axis=1))

    def lat_copy(k, i):
        return remote(rsb.at[k, i], rr.at[k, la], ra_s.at[k, i], ra_r.at[k, la], i, lo)

    def lat_wait(k, i):
        return remote(rsb.at[k, i], rr.at[k, i], ra_s.at[k, i], ra_r.at[k, i], i, lo)

    def lat_start(k, acc):
        for a in range(3):
            for b in range(3):
                top, low = (b * 4 + a) * C, (b * 4 + a + 1) * C
                kform[k, pl.ds((3 * a + b) * C, C), :] = (
                    acc[pl.ds(top, C), cols_of(0)] + acc[pl.ds(low, C), cols_of(1)]
                )

        def one(i):
            rows = kform[k, pl.ds(pl.multiple_of(i * z.wr, 8), z.wr), :]
            rsb[k, i] = rows.astype(BF)
            pl.when(i != la)(lambda: lat_copy(k, i).start())
        loop(0, nla, one)

    def lon_copy(k, m):
        return remote(lb.at[k, m], lr.at[k, lo], ro_s.at[k, m], ro_r.at[k, lo], la, m)

    def lon_wait(k, m):
        return remote(lb.at[k, m], lr.at[k, m], ro_s.at[k, m], ro_r.at[k, m], la, m)

    def lon_start(k):
        ssum[...] = jnp.zeros_like(ssum)
        ssum[0 : z.wr, :] = kform[k, pl.ds(pl.multiple_of(la * z.wr, 8), z.wr), :]

        def one(i):
            @pl.when(i != la)
            def _():
                lat_wait(k, i).wait_recv()
                ssum[0 : z.wr, :] += rr[k, i].astype(F32)
        loop(0, nla, one)
        ts[k] = ssum[...].T

        def two(m):
            lb[k, m] = ts[k, pl.ds(pl.multiple_of(m * z.wc, z.wc), z.wc), :].astype(BF)
            pl.when(m != lo)(lambda: lon_copy(k, m).start())
        loop(0, nlo, two)

    def lon_finish(k):
        gw[k] = ts[k, pl.ds(pl.multiple_of(lo * z.wc, z.wc), z.wc), :]

        def one(m):
            @pl.when(m != lo)
            def _():
                lon_wait(k, m).wait_recv()
                gw[k] += lr[k, m].astype(F32)
        loop(0, nlo, one)

    lat_start(SECOND, acc2)

    sums = jnp.sum(shared(y2, 1), axis=0)
    gain_grad, shift_grad = sums[:, :C], sums[:, C : 2 * C]
    gv[...] = sums

    scale_w = twice(inverse * gain)
    shift_part = twice(shift_grad / total)
    gain_part = twice(gain_grad / total)

    def first_grad(c):
        def one(j, carry):
            normed = (act[j, chunk(c), :] - center_w) * inverse_w
            here = cnt[j, chunk(c), :]
            value = sg[j, chunk(c), :] - here * shift_part - here * normed * gain_part
            low = (scale_w * value * slope[j, chunk(c), :]).astype(BF)
            F[1 + j, chunk(c), pl.ds(C, W)] = low
            return carry
        columns(one, 0)
        halo_send(F, 3, c)

    def first_kernel(c):
        grad = F[1 : 1 + L, chunk(c), pl.ds(C, W)].reshape(L * CH, W)
        kernel_grad(taps(X, c), grad, acc1)

    def field_chunk(c):
        halo_wait(F, 3, c)
        out = jnp.dot(taps(F, c), t1[...], preferred_element_type=F32)
        fs[:, chunk(c), :] = out.astype(BF).reshape(L, CH, W)
        send_out(fs, fo, fo_s, fo_r, c)

    loop(0, nch, first_grad)
    loop(0, nch, first_kernel)
    lat_start(FIRST, acc1)
    loop(0, nch, field_chunk)
    lon_start(SECOND)
    lon_start(FIRST)
    lon_finish(SECOND)
    lon_finish(FIRST)
    square = gw[0] * gw[0] + gw[1] * gw[1]
    square = total_row(square)
    share(y3, 2, sum(square[:, cols_of(t)] for t in range(z.LP // C)))
    squares = jnp.sum(shared(y3, 2), axis=0)
    mine2 = total_row((sums * sums).reshape(3, C)) if False else sum(
        sums[:, cols_of(t)] * sums[:, cols_of(t)] for t in range(3)
    )
    norm = jnp.sqrt(jnp.sum(squares + mine2, axis=1, keepdims=True))
    gn[...] = jnp.broadcast_to(norm, (1, C))

    def drain(c):
        def one(k):
            f_copy(c, k).wait_send()
            c_copy(c, k).wait_send()
            out_copy(bo, ob, bo_s, bo_r, c, k).wait()
            out_copy(fs, fo, fo_s, fo_r, c, k).wait()
        loop(1, nlo, one)
        own_out(bo, ob, bo_s, c).wait()
        own_out(fs, fo, fo_s, c).wait()
        for h, ref in enumerate((X, H, G, F)):
            halo_done(ref, h, c)

    loop(0, nch, drain)

    def drain_lon(k):
        w_copy(k).wait_send()
        mask_copy(k).wait_send()
    loop(1, nlo, drain_lon)
    for k in range(2):
        loop(1, nla // 2, lambda d: kz_copy(k, d).wait_send())
        loop(0, nla // 2, lambda d: kc_copy(k, d).wait_send())
        loop(0, nla, lambda i: pl.when(i != la)(lambda: lat_copy(k, i).wait_send()))
        loop(0, nlo, lambda m: pl.when(m != lo)(lambda: lon_copy(k, m).wait_send()))


def adam_step(master, first, second, grads, rate, decay):
    first_new = BETA_ONE * first + (1.0 - BETA_ONE) * grads
    second_new = BETA_TWO * second + (1.0 - BETA_TWO) * grads * grads
    first_hat = first_new / (1.0 - BETA_ONE**STEP)
    second_hat = second_new / (1.0 - BETA_TWO**STEP)
    master_new = master - rate * (first_hat / (jnp.sqrt(second_hat) + ADAM_EPS) + decay * master)
    return master_new, first_new, second_new


def last_kernel(
    z, step,
    ob, fo, cot, missing, std, gw, gv, gn, wm, wf, wsec, vm, vf, vs,
    block_out, field_grad, norm, w_new, w_first, w_second, w_low, v_new, v_first, v_second,
    cf, bf,
):
    Q = z.Q
    present, _ = both_masks(missing[...], None)
    have = present.T
    rstd = 1.0 / std[...]
    cf[...] = cot[...].astype(F32)
    for p in range(z.PX):
        i, q = p // Q, p % Q
        here = pl.ds(p, step, stride=z.PX)
        grad = cf[here, :] + fo[q, :, cols_of(i)].astype(F32)
        field_grad[here, :] = grad * have[:, p : p + 1] * rstd
        bf[here, :] = ob[q, :, cols_of(i)].astype(F32)
    block_out[...] = bf[...].astype(BF)

    @pl.when(pl.program_id(0) == 0)
    def _():
        size = gn[...]
        norm[...] = size[:, 0:1]
        factor = jnp.minimum(1.0, MAX_NORM / size)
        wide = factor[:, 0:1]
        for k in range(2):
            grads = gw[k, :, 0 : z.wr] * wide
            new, first, second = adam_step(wm[k], wf[k], wsec[k], grads, RATE_KERNEL, DECAY)
            w_new[k], w_first[k], w_second[k] = new, first, second
            w_low[k] = new.astype(BF)
        for k in range(3):
            grads = gv[:, cols_of(k)] * factor
            row = slice(k, k + 1)
            new, first, second = adam_step(vm[row, :], vf[row, :], vs[row, :], grads, RATE_VECTOR, 0.0)
            v_new[row, :], v_first[row, :], v_second[row, :] = new, first, second


def body(nla, nlo, fields, chan_mean, chan_std, sea_mask, missing, cotangent,
         w_master, w_first, w_second, vec_master, vec_first, vec_second):
    samples, rows, quads, channels = fields.shape
    z = Sizes(nla, nlo, samples, quads, w_master.shape[1], w_master.shape[2])
    S, L, Q, CH, nch, n, B = z.S, z.L, z.Q, z.CH, z.nch, z.n, z.B
    flat = (samples * rows * quads, channels)
    fields = fields.reshape(flat)
    cotangent = cotangent.reshape(flat)
    sea = jnp.transpose(sea_mask, (1, 2, 0))
    miss = jnp.transpose(missing, (1, 2, 0))
    wm, wf, wsec = (jnp.transpose(w, (0, 2, 1)) for w in (w_master, w_first, w_second))
    mean, std = chan_mean.reshape(1, C), chan_std.reshape(1, C)

    vmem = pl.BlockSpec(memory_space=pltpu.VMEM)
    hbm = pl.BlockSpec(memory_space=pl.ANY)
    V = pltpu.VMEM
    dma = pltpu.SemaphoreType.DMA
    shape = jax.ShapeDtypeStruct
    padded = V((L + 2, S, 4 * C), BF)
    wide = V((L, S, W), F32)
    scratch = [
        V(flat, BF), V(flat, BF), V((CH * z.PX, C), F32), V((B, z.PX), F32),
        V((nlo, z.PX, B), F32), wide,
        V((nch, nlo, Q, CH, W), BF), V((nch, nlo, Q, CH, W), BF),
        padded, padded, padded, padded, wide, wide, wide,
        V((L, S, W), BF), V((L, CH, W), F32), V((L, S, W), BF), V((L, S, W), BF),
        V((12 * C, W), BF), V((12 * C, W), BF), V((12 * C, W), BF), V((12 * C, W), BF),
        V((12 * C, W), F32), V((12 * C, W), F32),
        V((2, z.wc, z.LP), BF), V((nlo, 2, z.wc, z.LP), BF), V((2, nla, z.wr, C), BF),
        V((9 * C, C), F32), V((2, z.wr, C), BF),
        V((2, nla, z.wr, C), BF), V((2, nla, z.wr, C), BF), V((2, 9 * C, C), F32),
        V((z.LP, C), F32), V((2, C, z.LP), F32), V((2, nlo, z.wc, z.LP), BF), V((2, nlo, z.wc, z.LP), BF),
        V((n, 1, 3 * C), F32), V((n, 1, 3 * C), F32), V((n, 1, C), F32),
        dma((2,)), dma((nlo,)), dma((nlo,)), dma((nch, nlo)), dma((nch, nlo)),
        dma((nch, nlo)), dma((nch, nlo)), dma((4, nch, 2)), dma((4, nch, 2)),
        dma((nch, nlo)), dma((nch, nlo)), dma((nch, nlo)), dma((nch, nlo)),
        dma((nlo,)), dma((nlo,)), dma((2, nla)), dma((2, nla)), dma((2, nla)), dma((2, nla)),
        dma((2, nla)), dma((2, nla)), dma((2, nlo)), dma((2, nlo)), dma((3,)), dma((3,)),
    ]
    ob, fo, gw, gv, gn = pl.pallas_call(
        functools.partial(main_kernel, z),
        out_shape=(
            shape((Q, B, W), BF), shape((Q, B, W), BF),
            shape((2, z.wc, z.LP), F32), shape((1, 3 * C), F32), shape((1, C), F32),
        ),
        in_specs=[hbm, hbm] + [vmem] * 6,
        out_specs=(hbm, hbm, vmem, vmem, vmem),
        scratch_shapes=scratch,
        compiler_params=pltpu.CompilerParams(
            collective_id=0, has_side_effects=True, vmem_limit_bytes=56 * 2**20
        ),
        name="block",
    )(fields, cotangent, sea, miss, mean, std, wm, vec_master)

    step = min(128, B)
    whole = lambda s: pl.BlockSpec(s, lambda t: (0,) * len(s))
    native = pl.BlockSpec((step * z.PX, C), lambda t: (t, 0))
    spread = pl.BlockSpec((Q, step, W), lambda t: (0, t, 0))
    w_spec, v_spec = whole(wm.shape), whole((3, C))
    outs = pl.pallas_call(
        functools.partial(last_kernel, z, step),
        grid=(B // step,),
        out_shape=(
            shape(flat, BF), shape(flat, F32), shape((1, 1), F32),
            shape(wm.shape, F32), shape(wm.shape, F32), shape(wm.shape, F32), shape(wm.shape, BF),
            shape((3, C), F32), shape((3, C), F32), shape((3, C), F32),
        ),
        in_specs=[
            spread, spread, native, pl.BlockSpec((R, Q, step), lambda t: (0, 0, t)), whole((1, C)),
            whole(gw.shape), whole(gv.shape), whole(gn.shape),
            w_spec, w_spec, w_spec, v_spec, v_spec, v_spec,
        ],
        out_specs=(native, native, whole((1, 1)), w_spec, w_spec, w_spec, w_spec, v_spec, v_spec, v_spec),
        scratch_shapes=[V((step * z.PX, C), F32), V((step * z.PX, C), F32)],
        compiler_params=pltpu.CompilerParams(vmem_limit_bytes=32 * 2**20),
        name="update",
    )(ob, fo, cotangent, miss, std, gw, gv, gn, wm, wf, wsec, vec_master, vec_first, vec_second)
    block_out, field_grad, norm, w_new, w_f, w_s, w_low, v_new, v_f, v_s = outs
    like = (samples, rows, quads, channels)
    w_new, w_f, w_s, w_low = (jnp.transpose(w, (0, 2, 1)) for w in (w_new, w_f, w_s, w_low))
    return (
        block_out.reshape(like), field_grad.reshape(like), norm.reshape(()),
        w_new, w_f, w_s, w_low, v_new, v_f, v_s,
    )


def solution(mesh):
    tile, kernel = P(None, "lat", "lon", None), P(None, "lat", "lon")
    return jax.shard_map(
        functools.partial(body, mesh.shape["lat"], mesh.shape["lon"]),
        mesh=mesh,
        in_specs=(tile, P(), P(), kernel, kernel, tile, kernel, kernel, kernel, P(), P(), P()),
        out_specs=(tile, tile, P(), kernel, kernel, kernel, kernel, P(), P(), P()),
        check_vma=False,
    )
```

```python
import functools

import jax
import jax.numpy as jnp
from jax import lax
from jax.experimental import pallas as pl
from jax.experimental.pallas import tpu as pltpu
from jax.sharding import PartitionSpec as P

STEP = 10
EPS = 1e-05
MAX_NORM = 1.0
BETA_ONE = 0.9
BETA_TWO = 0.999
ADAM_EPS = 1e-08
RATE_KERNEL = 0.02
RATE_VECTOR = 0.1
DECAY = 0.01

MESH = pl.DeviceIdType.MESH
BF = jnp.bfloat16
F32 = jnp.float32
C = 128
R = 2
W = R * C
FIRST, SECOND = 0, 1


def cols_of(i):
    return slice(i * C, (i + 1) * C)


def twice(row):
    return jnp.concatenate([row, row], axis=1)


def fold(row):
    return row[:, :C] + row[:, C:]


def to_eight(block):
    rows, width = block.shape
    return jnp.sum(block.reshape(rows // 8, 8, width), axis=0)


def total_row(block):
    return jnp.sum(block, axis=0, keepdims=True)


def both_masks(missing, sea):
    have = (1 - missing).astype(F32)
    present = jnp.concatenate([have[0], have[1]], axis=0)
    counted = None
    if sea is not None:
        land = have * sea.astype(F32)
        counted = jnp.concatenate([land[0], land[1]], axis=0)
    return present, counted


def smooth(value):
    small = jnp.exp(-jnp.abs(value))
    one = 1.0 + small
    soft = jnp.maximum(value, 0.0) + jnp.log(one)
    sigmoid = jnp.where(value >= 0.0, 1.0, small) / one
    return 0.3 * value + 0.7 * soft, 0.3 + 0.7 * sigmoid


class Sizes:
    def __init__(self, nla, nlo, samples, quads, wrows, wcols):
        self.nla, self.nlo = nla, nlo
        self.n = nla * nlo
        self.B, self.Q = samples, quads
        self.PX = R * quads
        self.S = samples // nlo
        self.L = quads * nlo
        self.CH = self.S // 4 if self.S % 64 == 0 else 16
        self.nch = self.S // self.CH
        self.wr, self.wc = wrows, wcols
        self.LP = -(-wrows // 128) * 128


def main_kernel(
    z,
    fields, cot, sea_h, missing_h, mean_h, std_h, wt_h, vec_h,
    ob, fo, grads,
    fin, cin, sea, missing, mean, std, wt, vec, fb, pres, cm, cnt, sb, cb,
    X, H, G, F, act, slope, sg, ct, pre, bo, fs,
    w1, w2, t1, t2, acc1, acc2,
    ws, wg, kg_in, kf, kl,
    ca, cr, za, zr, kform, ssum, ts, lb, lr,
    y1, y2, y3,
    load_sem, mask_s, mask_r, f_s, f_r, c_s, c_r, halo_s, halo_r,
    bo_s, bo_r, bo_o, fo_s, fo_r, fo_o, wg_s, wg_r, kz_s, kz_r, kc_s, kc_r,
    rc_s, rc_r, rz_s, rz_r, ro_s, ro_r, y_s, y_r,
):
    nla, nlo, n = z.nla, z.nlo, z.n
    S, L, Q, CH, nch = z.S, z.L, z.Q, z.CH, z.nch
    la = lax.axis_index("lat")
    lo = lax.axis_index("lon")
    me = la * nlo + lo

    def remote(src, dst, ss, rs, lat_to, lon_to):
        return pltpu.make_async_remote_copy(
            src, dst, ss, rs, device_id=(lat_to, lon_to), device_id_type=MESH
        )

    def received(ref, sem):
        remote(ref, ref, sem, sem, la, lo).wait_recv()

    def sent(ref, sem):
        remote(ref, ref, sem, sem, la, lo).wait_send()

    def loop(low, high, body):
        def step(k, carry):
            body(k)
            return carry
        lax.fori_loop(low, high, step, 0)

    def others(body):
        upper = la // (nla // 2)

        def row(t):
            i = upper * t + (1 - upper) * (nla - 1 - t)

            def one(j):
                @pl.when(jnp.logical_or(i != la, j != lo))
                def _():
                    body(i, j)
            loop(0, nlo, one)
        loop(0, nla, row)

    own = pl.ds(C, W)

    def chunk(c):
        return pl.ds(pl.multiple_of(c * CH, CH), CH)

    def peer(k):
        return lax.rem(lo + k, nlo)

    barrier = pltpu.get_barrier_semaphore()
    others(lambda i, j: pl.semaphore_signal(barrier, inc=1, device_id=(i, j), device_id_type=MESH))
    pairs = (
        (missing_h, missing), (sea_h, sea), (mean_h, mean), (std_h, std), (wt_h, wt), (vec_h, vec),
        (fields, fin), (cot, cin),
    )
    loads = [pltpu.make_async_copy(src, dst, load_sem.at[i]) for i, (src, dst) in enumerate(pairs)]
    for load in loads:
        load.start()
    for load in loads[:-2]:
        load.wait()
    load_f, load_c = loads[-2:]

    present, counted = both_masks(missing[...], sea[...])
    pres[...] = present.T
    cm[lo] = counted
    pad = z.LP - z.wr
    for k in range(2):
        block = wt[k].astype(BF)
        if pad:
            block = jnp.concatenate([block, jnp.zeros((z.wc, pad), BF)], axis=1)
        ws[k] = block
        wg[lo, k] = block
    north_pole, south_pole = la == 0, la == nla - 1
    for ref in (X, H, G, F):
        @pl.when(north_pole)
        def _():
            ref[:, :, cols_of(0)] = jnp.zeros((L + 2, S, C), BF)

        @pl.when(south_pole)
        def _():
            ref[:, :, cols_of(3)] = jnp.zeros((L + 2, S, C), BF)

    def w_copy(k):
        m = peer(k)
        return remote(ws, wg.at[lo], wg_s.at[0], wg_r.at[0], la, m)

    def mask_copy(k):
        return remote(cm.at[lo], cm.at[lo], mask_s.at[0], mask_r.at[0], la, peer(k))

    load_f.wait()

    rstd = 1.0 / std[...]
    center_in = mean[...]

    def place(src, t, c, put, standardize):
        first = pl.multiple_of((t * S + c * CH) * z.PX, CH * z.PX)
        fb[...] = src[pl.ds(first, CH * z.PX), :].astype(F32)
        here = pres[pl.ds(pl.multiple_of(t * S + c * CH, CH), CH), :]
        for p in range(z.PX):
            value = fb[pl.ds(p, CH, stride=z.PX), :]
            if standardize:
                value = (value - center_in) * rstd * here[:, p : p + 1]
            put(p // Q, p % Q, value.astype(BF))

    def f_copy(c, k):
        return remote(
            sb.at[c, k], X.at[pl.ds(1 + Q * lo, Q), chunk(c), own],
            f_s.at[0], f_r.at[c], la, peer(k),
        )

    def c_copy(c, k):
        return remote(
            cb.at[c, k], ct.at[pl.ds(Q * lo, Q), chunk(c), :],
            c_s.at[0], c_r.at[c], la, peer(k),
        )

    def prep_fields(c):
        def one(k):
            def put(i, q, value):
                sb[c, k, q, :, cols_of(i)] = value
            place(fin, peer(k), c, put, True)
        loop(1, nlo, one)

    def send_fields(c):
        loop(1, nlo, lambda k: f_copy(c, k).start())

    def next_fields(c):
        prep_fields(c)
        send_fields(c)

    def own_fields(c):
        def put(i, q, value):
            X[1 + Q * lo + q, chunk(c), cols_of(i + 1)] = value
        place(fin, lo, c, put, True)

    def own_cot(c):
        def put(i, q, value):
            ct[Q * lo + q, chunk(c), cols_of(i)] = value
        place(cin, lo, c, put, False)

    def prep_cot(c):
        def one(k):
            def put(i, q, value):
                cb[c, k, q, :, cols_of(i)] = value
            place(cin, peer(k), c, put, False)
        loop(1, nlo, one)

    prep_fields(0)
    pl.semaphore_wait(barrier, n - 1)
    loop(1, nlo, lambda k: w_copy(k).start())
    loop(1, nlo, lambda k: mask_copy(k).start())
    send_fields(0)
    loop(1, nch, next_fields)

    received(wg.at[pl.ds(0, nlo - 1)], wg_r.at[0])
    for k in range(2):
        gathered = jnp.concatenate([wg[m, k].astype(F32) for m in range(nlo)], axis=0)
        kl[k] = gathered.T[: z.wr].astype(BF)
        kg_in[k, la] = kl[k]
    core = lax.rem(la, 2)
    sibling = la + 1 - 2 * core

    def kz_copy(k, d):
        to = lax.rem(la + 2 * d, nla)
        return remote(kl.at[k], kg_in.at[k, la], kz_s.at[k], kz_r.at[k], to, lo)

    def kc_copy(k, d):
        row = lax.rem(la + nla - 2 * d, nla)
        return remote(kg_in.at[k, row], kg_in.at[k, row], kc_s.at[k], kc_r.at[k], sibling, lo)

    def start_kernel(k):
        loop(1, nla // 2, lambda d: kz_copy(k, d).start())
        kc_copy(k, 0).start()

    def forward_kernel(k):
        received(kg_in.at[k, pl.ds(0, nla // 2 - 1)], kz_r.at[k])
        loop(1, nla // 2, lambda d: kc_copy(k, d).start())

    def finish_kernel(k):
        received(kg_in.at[k, pl.ds(0, nla // 2)], kc_r.at[k])
        for i in range(nla):
            kf[pl.ds(i * z.wr, z.wr), :] = kg_in[k, i].astype(F32)

    def tap(a, b):
        return kf[pl.ds((3 * a + b) * C, C), :]

    def build_forward(ref):
        for b in range(3):
            for r in range(4):
                for i in range(R):
                    a = r - i
                    good = 0 <= a <= 2
                    block = tap(a, b).astype(BF) if good else jnp.zeros((C, C), BF)
                    ref[pl.ds((b * 4 + r) * C, C), cols_of(i)] = block

    def build_turned(ref):
        for b in range(3):
            for a in range(3):
                block = tap(2 - a, 2 - b).T.astype(BF)
                for i in range(R):
                    ref[pl.ds((b * 4 + a + i) * C, C), cols_of(i)] = block
            for i, r in ((0, 3), (1, 0)):
                ref[pl.ds((b * 4 + r) * C, C), cols_of(i)] = jnp.zeros((C, C), BF)

    start_kernel(FIRST)
    start_kernel(SECOND)

    loop(0, nch, own_fields)
    load_c.wait()
    loop(0, nch, own_cot)
    loop(0, nch, prep_cot)

    def spread_mask():
        rows = jnp.concatenate([cm[m] for m in range(nlo)], axis=0)
        back = z.B - lo * S
        mine = pltpu.roll(rows, lax.rem(back, z.B), 1)[:, : min(z.B, 128)].T
        for j in range(L):
            for i in range(R):
                col = (j // Q) * z.PX + i * Q + j % Q
                cnt[j, :, cols_of(i)] = jnp.broadcast_to(mine[:S, col : col + 1], (S, C))

    def halo_copies(ref, h, c):
        def lanes(r):
            return ref.at[pl.ds(1, L), chunk(c), pl.ds(r * C, C)]

        north = remote(lanes(1), lanes(3), halo_s.at[h], halo_r.at[h, c], jnp.maximum(la - 1, 0), lo)
        south = remote(lanes(2), lanes(0), halo_s.at[h], halo_r.at[h, c], jnp.minimum(la + 1, nla - 1), lo)
        return north, south

    def halo_send(ref, h, c):
        north, south = halo_copies(ref, h, c)
        pl.when(la > 0)(north.start)
        pl.when(la < nla - 1)(south.start)

    at_pole = jnp.logical_or(north_pole, south_pole)

    def halo_wait(ref, h, c):
        def both(width):
            received(ref.at[pl.ds(1, L), chunk(c), pl.ds(0, width)], halo_r.at[h, c])
        pl.when(at_pole)(lambda: both(C))
        pl.when(jnp.logical_not(at_pole))(lambda: both(W))
        ref[0, chunk(c), :] = ref[L, chunk(c), :]
        ref[L + 1, chunk(c), :] = ref[1, chunk(c), :]

    def halo_done(ref, h):
        def both(width):
            sent(ref.at[pl.ds(1, L), :, pl.ds(0, width)], halo_s.at[h])
        pl.when(at_pole)(lambda: both(C))
        pl.when(jnp.logical_not(at_pole))(lambda: both(W))

    def taps(ref, c):
        parts = [ref[b : b + L, chunk(c), :].reshape(L * CH, 4 * C) for b in range(3)]
        return jnp.concatenate(parts, axis=1)

    def conv(lhs, kernel):
        out = jnp.dot(lhs, kernel[...], preferred_element_type=F32)
        pre[...] = out.reshape(L, CH, W)

    def kernel_grad(lhs, grad, acc):
        acc[...] += lax.dot_general(
            lhs, grad, (((0,), (0,)), ((), ())), preferred_element_type=F32
        )

    def columns(body, carry):
        return lax.fori_loop(0, L, body, carry, unroll=min(L, 16))

    zero8 = jnp.zeros((8, W), F32)

    def arrive(c):
        received(X.at[pl.ds(1, Q * (nlo - 1)), chunk(c), own], f_r.at[c])
        halo_send(X, 0, c)

    def first_chunk(c, stats):
        halo_wait(X, 0, c)
        conv(taps(X, c), w1)

        def one(j, carry):
            s, m = carry
            value, grad = smooth(pre[j])
            act[j, chunk(c), :] = value
            slope[j, chunk(c), :] = grad
            here = cnt[j, chunk(c), :]
            return s + to_eight(here * value), m + to_eight(here)

        s8, n8 = columns(one, (zero8, zero8))
        s_c, n_c = fold(total_row(s8)), fold(total_row(n8))
        mean_c = s_c / jnp.maximum(n_c, 1.0)
        mean_w = twice(mean_c)

        def two(j, m2):
            off = act[j, chunk(c), :] - mean_w
            return m2 + to_eight(cnt[j, chunk(c), :] * off * off)

        m_c = fold(total_row(columns(two, zero8)))
        n_0, s_0, m_0 = stats
        delta = mean_c - s_0 / jnp.maximum(n_0, 1.0)
        n_1 = n_0 + n_c
        m_1 = m_0 + m_c + delta * delta * (n_0 * n_c / jnp.maximum(n_1, 1.0))
        return n_1, s_0 + s_c, m_1

    def send_cot(c):
        loop(1, nlo, lambda k: c_copy(c, k).start())

    arrive(0)
    forward_kernel(FIRST)
    received(cm.at[pl.ds(0, nlo - 1)], mask_r.at[0])
    spread_mask()
    finish_kernel(FIRST)
    build_forward(w1)
    build_turned(t1)
    zero1 = jnp.zeros((1, C), F32)

    def first_step(c, stats):
        pl.when(c + 1 < nch)(lambda: arrive(c + 1))
        pl.when(c + 2 == nch)(lambda: send_cot(0))
        return first_chunk(c, stats)

    n_d, s_d, m_d = lax.fori_loop(0, nch, first_step, (zero1, zero1, zero1))

    def share(buf, which, value):
        buf[me] = value
        others(lambda i, j: remote(buf.at[me], buf.at[me], y_s.at[which], y_r.at[which], i, j).start())

    def shared(buf, which):
        block = remote(buf.at[pl.ds(0, n - 1)], buf.at[pl.ds(0, n - 1)], y_s.at[which], y_r.at[which], la, lo)
        block.wait_recv()
        block.wait_send()
        return buf[...]

    share(y1, 0, jnp.concatenate([n_d, s_d, m_d], axis=1))
    loop(1, nch, send_cot)
    forward_kernel(SECOND)
    finish_kernel(SECOND)
    build_forward(w2)
    build_turned(t2)
    acc1[...] = jnp.zeros_like(acc1)
    acc2[...] = jnp.zeros_like(acc2)

    parts = shared(y1, 0)
    n_all, s_all, m_all = parts[:, :, :C], parts[:, :, C : 2 * C], parts[:, :, 2 * C :]
    total = jnp.sum(n_all, axis=0)
    center = jnp.sum(s_all, axis=0) / total
    apart = s_all / jnp.maximum(n_all, 1.0) - center[None]
    spread = jnp.sum(m_all + n_all * apart * apart, axis=0) / total
    inverse = lax.rsqrt(spread + EPS)
    gain, shift, bias = vec[0:1, :], vec[1:2, :], vec[2:3, :]
    center_w, inverse_w = twice(center), twice(inverse)
    gain_w, shift_w, bias_w = twice(gain), twice(shift), twice(bias)

    def hidden(c):
        def one(j, carry):
            normed = (act[j, chunk(c), :] - center_w) * inverse_w
            H[1 + j, chunk(c), own] = (normed * gain_w + shift_w).astype(BF)
            return carry
        columns(one, 0)
        halo_send(H, 1, c)

    def out_copy(src, dst, ss, rs, c, k):
        m = peer(k)
        return remote(
            src.at[pl.ds(Q * m, Q), chunk(c), :],
            dst.at[:, pl.ds(pl.multiple_of(lo * S + c * CH, CH), CH), :],
            ss.at[0], rs.at[0], la, m,
        )

    def own_out(src, dst, os, c):
        return pltpu.make_async_copy(
            src.at[pl.ds(Q * lo, Q), chunk(c), :],
            dst.at[:, pl.ds(pl.multiple_of(lo * S + c * CH, CH), CH), :],
            os.at[0],
        )

    def send_out(src, dst, ss, rs, os, c):
        loop(1, nlo, lambda k: out_copy(src, dst, ss, rs, c, k).start())
        own_out(src, dst, os, c).start()

    def out_done(src, dst, ss, rs, os):
        sent(src.at[pl.ds(0, Q * (nlo - 1))], ss.at[0])
        received(dst.at[:, pl.ds(0, S * (nlo - 1)), :], rs.at[0])
        pltpu.make_async_copy(src.at[pl.ds(0, Q)], dst.at[:, pl.ds(0, S), :], os.at[0]).wait()

    block_out = (bo, ob, bo_s, bo_r, bo_o)
    field_out = (fs, fo, fo_s, fo_r, fo_o)
    early = min(1, nch - 1)

    def second_chunk(c, b8):
        halo_wait(H, 1, c)
        received(ct.at[pl.ds(0, Q * (nlo - 1)), chunk(c), :], c_r.at[c])
        conv(taps(H, c), w2)

        def one(j, carry):
            value, grad = smooth(pre[j] + bias_w)
            standard = X[1 + j, chunk(c), own].astype(F32)
            bo[j, chunk(c), :] = (standard + value).astype(BF)
            low = (ct[j, chunk(c), :].astype(F32) * grad).astype(BF)
            G[1 + j, chunk(c), own] = low
            return carry + to_eight(low.astype(F32))

        b8 = columns(one, b8)
        halo_send(G, 2, c)
        return b8

    def second_kernel(c):
        grad = G[1 : 1 + L, chunk(c), own].reshape(L * CH, W)
        kernel_grad(taps(H, c), grad, acc2)

    def back_chunk(c, carry):
        halo_wait(G, 2, c)
        conv(taps(G, c), t2)

        def one(j, carry):
            g8, s8 = carry
            value = pre[j]
            sg[j, chunk(c), :] = value
            normed = (act[j, chunk(c), :] - center_w) * inverse_w
            return g8 + to_eight(value * normed), s8 + to_eight(value)

        return columns(one, carry)

    loop(0, nch, hidden)
    b8 = second_chunk(0, zero8)

    def second_step(c, carry):
        b8, g8, s8 = carry
        b8 = second_chunk(c + 1, b8)
        pl.when(c < early)(lambda: send_out(*block_out, c))
        second_kernel(c)
        g8, s8 = back_chunk(c, (g8, s8))
        return b8, g8, s8

    b8, g8, s8 = lax.fori_loop(0, nch - 1, second_step, (b8, zero8, zero8))
    second_kernel(nch - 1)
    g8, s8 = back_chunk(nch - 1, (g8, s8))
    sums = [fold(total_row(v)) for v in (g8, s8, b8)]
    share(y2, 1, jnp.concatenate(sums, axis=1))
    loop(early, nch, lambda c: send_out(*block_out, c))

    chip, chips = la // 2, nla // 2

    def rows_of(k, i):
        return kform[k, pl.ds(pl.multiple_of(i * z.wr, 8), z.wr), :]

    def core_copy(k):
        return remote(ca.at[k], cr.at[k], rc_s.at[k], rc_r.at[k], sibling, lo)

    def core_start(k, acc):
        for a in range(3):
            for b in range(3):
                top, low = (b * 4 + a) * C, (b * 4 + a + 1) * C
                kform[k, pl.ds((3 * a + b) * C, C), :] = (
                    acc[pl.ds(top, C), cols_of(0)] + acc[pl.ds(low, C), cols_of(1)]
                )

        def one(t):
            ca[k, t] = rows_of(k, 2 * t + 1 - core).astype(BF)
        loop(0, chips, one)
        core_copy(k).start()

    def chip_copy(k, t, slot):
        return remote(za.at[k, t], zr.at[k, slot], rz_s.at[k], rz_r.at[k], 2 * t + core, lo)

    def chip_start(k):
        core_copy(k).wait_recv()
        ssum[k] = jnp.zeros_like(ssum[k])
        ssum[k, 0 : z.wr, :] = rows_of(k, la) + cr[k, chip].astype(F32)

        def one(t):
            @pl.when(t != chip)
            def _():
                za[k, t] = (rows_of(k, 2 * t + core) + cr[k, t].astype(F32)).astype(BF)
                chip_copy(k, t, chip).start()
        loop(0, chips, one)

    def lon_copy(k, m):
        return remote(lb.at[k, m], lr.at[k, lo], ro_s.at[k], ro_r.at[k], la, m)

    def lon_start(k):
        received(zr.at[k, pl.ds(0, chips - 1)], rz_r.at[k])

        def one(t):
            @pl.when(t != chip)
            def _():
                ssum[k, 0 : z.wr, :] += zr[k, t].astype(F32)
        loop(0, chips, one)
        ts[k] = ssum[k].T

        def two(m):
            lb[k, m] = ts[k, pl.ds(pl.multiple_of(m * z.wc, z.wc), z.wc), :].astype(BF)
            pl.when(m != lo)(lambda: lon_copy(k, m).start())
        loop(0, nlo, two)

    def lon_finish(k):
        received(lr.at[k, pl.ds(0, nlo - 1)], ro_r.at[k])
        grads[k, 0 : z.wc] = ts[k, pl.ds(pl.multiple_of(lo * z.wc, z.wc), z.wc), :]

        def one(m):
            @pl.when(m != lo)
            def _():
                grads[k, 0 : z.wc] += lr[k, m].astype(F32)
        loop(0, nlo, one)

    core_start(SECOND, acc2)
    chip_start(SECOND)
    sums = jnp.sum(shared(y2, 1), axis=0)
    gain_grad, shift_grad = sums[:, :C], sums[:, C : 2 * C]

    scale_w = twice(inverse * gain)
    shift_part = twice(shift_grad / total)
    gain_part = twice(gain_grad / total)

    def first_grad(c):
        def one(j, carry):
            normed = (act[j, chunk(c), :] - center_w) * inverse_w
            here = cnt[j, chunk(c), :]
            value = sg[j, chunk(c), :] - here * shift_part - here * normed * gain_part
            F[1 + j, chunk(c), own] = (scale_w * value * slope[j, chunk(c), :]).astype(BF)
            return carry
        columns(one, 0)
        halo_send(F, 3, c)

    def first_kernel(c):
        grad = F[1 : 1 + L, chunk(c), own].reshape(L * CH, W)
        kernel_grad(taps(X, c), grad, acc1)

    def field_chunk(c):
        halo_wait(F, 3, c)
        out = jnp.dot(taps(F, c), t1[...], preferred_element_type=F32)
        fs[:, chunk(c), :] = out.astype(BF).reshape(L, CH, W)

    def send_field(c):
        send_out(*field_out, c)

    held = max(nch - 2, 1)
    loop(0, nch, first_grad)
    first_kernel(0)
    field_chunk(0)
    send_field(0)
    loop(1, nch, first_kernel)
    core_start(FIRST, acc1)
    loop(1, held, field_chunk)
    loop(1, held, send_field)
    chip_start(FIRST)
    loop(held, nch, field_chunk)
    lon_start(SECOND)
    lon_start(FIRST)
    loop(held, nch - 1, send_field)
    lon_finish(SECOND)
    lon_finish(FIRST)
    first_w, second_w = grads[0, 0 : z.wc], grads[1, 0 : z.wc]
    square = total_row(first_w * first_w + second_w * second_w)
    share(y3, 2, sum(square[:, cols_of(t)] for t in range(z.LP // C)))
    loop(max(held, nch - 1), nch, send_field)
    squares = jnp.sum(shared(y3, 2), axis=0)
    mine2 = sum(sums[:, cols_of(t)] * sums[:, cols_of(t)] for t in range(3))
    norm = jnp.sqrt(jnp.sum(squares + mine2, axis=1, keepdims=True))
    for k in range(3):
        grads[0, z.wc + k : z.wc + k + 1, 0:C] = sums[:, cols_of(k)]
    grads[0, z.wc + 3 : z.wc + 4, 0:C] = jnp.broadcast_to(norm, (1, C))

    sent(sb.at[:, pl.ds(1, nlo - 1)], f_s.at[0])
    sent(cb.at[:, pl.ds(1, nlo - 1)], c_s.at[0])
    sent(wg.at[pl.ds(0, nlo - 1)], wg_s.at[0])
    sent(cm.at[pl.ds(0, nlo - 1)], mask_s.at[0])
    for h, ref in enumerate((X, H, G, F)):
        halo_done(ref, h)
    for k in range(2):
        sent(kg_in.at[k, pl.ds(0, nla // 2 - 1)], kz_s.at[k])
        sent(kg_in.at[k, pl.ds(0, nla // 2)], kc_s.at[k])
        core_copy(k).wait_send()
        sent(zr.at[k, pl.ds(0, chips - 1)], rz_s.at[k])
        sent(lr.at[k, pl.ds(0, nlo - 1)], ro_s.at[k])
    out_done(*block_out)
    out_done(*field_out)


def adam_step(master, first, second, grads, rate, decay):
    first_new = BETA_ONE * first + (1.0 - BETA_ONE) * grads
    second_new = BETA_TWO * second + (1.0 - BETA_TWO) * grads * grads
    first_hat = first_new / (1.0 - BETA_ONE**STEP)
    second_hat = second_new / (1.0 - BETA_TWO**STEP)
    master_new = master - rate * (first_hat / (jnp.sqrt(second_hat) + ADAM_EPS) + decay * master)
    return master_new, first_new, second_new


def last_kernel(
    z, step,
    ob, fo, cot, missing, std, grads, wm, wf, wsec, vm, vf, vs,
    block_out, field_grad, norm, w_new, w_first, w_second, w_low, v_new, v_first, v_second,
    cf, bf,
):
    Q = z.Q
    present, _ = both_masks(missing[...], None)
    have = present.T
    rstd = 1.0 / std[...]
    cf[...] = cot[...].astype(F32)
    for p in range(z.PX):
        i, q = p // Q, p % Q
        here = pl.ds(p, step, stride=z.PX)
        grad = cf[here, :] + fo[q, :, cols_of(i)].astype(F32)
        field_grad[here, :] = grad * have[:, p : p + 1] * rstd
        bf[here, :] = ob[q, :, cols_of(i)].astype(F32)
    block_out[...] = bf[...].astype(BF)

    @pl.when(pl.program_id(0) == 0)
    def _():
        size = grads[0, z.wc + 3 : z.wc + 4, 0:C]
        norm[...] = size[:, 0:1]
        factor = jnp.minimum(1.0, MAX_NORM / size)
        wide = factor[:, 0:1]
        for k in range(2):
            own = grads[k, 0 : z.wc, 0 : z.wr] * wide
            new, first, second = adam_step(wm[k], wf[k], wsec[k], own, RATE_KERNEL, DECAY)
            w_new[k], w_first[k], w_second[k] = new, first, second
            w_low[k] = new.astype(BF)
        for k in range(3):
            own = grads[0, z.wc + k : z.wc + k + 1, 0:C] * factor
            row = slice(k, k + 1)
            new, first, second = adam_step(vm[row, :], vf[row, :], vs[row, :], own, RATE_VECTOR, 0.0)
            v_new[row, :], v_first[row, :], v_second[row, :] = new, first, second


def body(nla, nlo, fields, chan_mean, chan_std, sea_mask, missing, cotangent,
         w_master, w_first, w_second, vec_master, vec_first, vec_second):
    samples, rows, quads, channels = fields.shape
    z = Sizes(nla, nlo, samples, quads, w_master.shape[1], w_master.shape[2])
    S, L, Q, CH, nch, n, B = z.S, z.L, z.Q, z.CH, z.nch, z.n, z.B
    flat = (samples * rows * quads, channels)
    fields = fields.reshape(flat)
    cotangent = cotangent.reshape(flat)
    sea = jnp.transpose(sea_mask, (1, 2, 0))
    miss = jnp.transpose(missing, (1, 2, 0))
    wm, wf, wsec = (jnp.transpose(w, (0, 2, 1)) for w in (w_master, w_first, w_second))
    mean, std = chan_mean.reshape(1, C), chan_std.reshape(1, C)

    vmem = pl.BlockSpec(memory_space=pltpu.VMEM)
    hbm = pl.BlockSpec(memory_space=pl.ANY)
    V = pltpu.VMEM
    dma = pltpu.SemaphoreType.DMA
    shape = jax.ShapeDtypeStruct
    padded = V((L + 2, S, 2 * W), BF)
    wide = V((L, S, W), F32)
    scratch = [
        V(flat, BF), V(flat, BF), V(sea.shape, sea.dtype), V(miss.shape, miss.dtype),
        V((1, C), F32), V((1, C), F32), V(wm.shape, F32), V((3, C), F32),
        V((CH * z.PX, C), F32), V((B, z.PX), F32),
        V((nlo, z.PX, B), F32), wide,
        V((nch, nlo, Q, CH, W), BF), V((nch, nlo, Q, CH, W), BF),
        padded, padded, padded, padded, wide, wide, wide,
        V((L, S, W), BF), V((L, CH, W), F32), V((L, S, W), BF), V((L, S, W), BF),
        V((12 * C, W), BF), V((12 * C, W), BF), V((12 * C, W), BF), V((12 * C, W), BF),
        V((12 * C, W), F32), V((12 * C, W), F32),
        V((2, z.wc, z.LP), BF), V((nlo, 2, z.wc, z.LP), BF), V((2, nla, z.wr, C), BF),
        V((9 * C, C), F32), V((2, z.wr, C), BF),
        V((2, nla // 2, z.wr, C), BF), V((2, nla // 2, z.wr, C), BF),
        V((2, nla // 2, z.wr, C), BF), V((2, nla // 2, z.wr, C), BF), V((2, 9 * C, C), F32),
        V((2, z.LP, C), F32), V((2, C, z.LP), F32), V((2, nlo, z.wc, z.LP), BF), V((2, nlo, z.wc, z.LP), BF),
        V((n, 1, 3 * C), F32), V((n, 1, 3 * C), F32), V((n, 1, C), F32),
        dma((8,)), dma((1,)), dma((1,)), dma((1,)), dma((nch,)), dma((1,)), dma((nch,)),
        dma((4,)), dma((4, nch)),
        dma((1,)), dma((1,)), dma((1,)), dma((1,)), dma((1,)), dma((1,)), dma((1,)), dma((1,)),
        dma((2,)), dma((2,)), dma((2,)), dma((2,)),
        dma((2,)), dma((2,)), dma((2,)), dma((2,)), dma((2,)), dma((2,)), dma((3,)), dma((3,)),
    ]
    ob, fo, grads = pl.pallas_call(
        functools.partial(main_kernel, z),
        out_shape=(
            shape((Q, B, W), BF), shape((Q, B, W), BF),
            shape((2, z.wc + 8, z.LP), F32),
        ),
        in_specs=[hbm] * 8,
        out_specs=(hbm, hbm, vmem),
        scratch_shapes=scratch,
        compiler_params=pltpu.CompilerParams(
            collective_id=0, has_side_effects=True, vmem_limit_bytes=56 * 2**20
        ),
        name="block",
    )(fields, cotangent, sea, miss, mean, std, wm, vec_master)

    step = min(128, B)
    whole = lambda s: pl.BlockSpec(s, lambda t: (0,) * len(s))
    native = pl.BlockSpec((step * z.PX, C), lambda t: (t, 0))
    spread = pl.BlockSpec((Q, step, W), lambda t: (0, t, 0))
    w_spec, v_spec = whole(wm.shape), whole((3, C))
    outs = pl.pallas_call(
        functools.partial(last_kernel, z, step),
        grid=(B // step,),
        out_shape=(
            shape(flat, BF), shape(flat, F32), shape((1, 1), F32),
            shape(wm.shape, F32), shape(wm.shape, F32), shape(wm.shape, F32), shape(wm.shape, BF),
            shape((3, C), F32), shape((3, C), F32), shape((3, C), F32),
        ),
        in_specs=[
            spread, spread, native, pl.BlockSpec((R, Q, step), lambda t: (0, 0, t)), whole((1, C)),
            whole(grads.shape),
            w_spec, w_spec, w_spec, v_spec, v_spec, v_spec,
        ],
        out_specs=(native, native, whole((1, 1)), w_spec, w_spec, w_spec, w_spec, v_spec, v_spec, v_spec),
        scratch_shapes=[V((step * z.PX, C), F32), V((step * z.PX, C), F32)],
        compiler_params=pltpu.CompilerParams(vmem_limit_bytes=60 * 2**20),
        name="update",
    )(ob, fo, cotangent, miss, std, grads, wm, wf, wsec, vec_master, vec_first, vec_second)
    block_out, field_grad, norm, w_new, w_f, w_s, w_low, v_new, v_f, v_s = outs
    like = (samples, rows, quads, channels)
    w_new, w_f, w_s, w_low = (jnp.transpose(w, (0, 2, 1)) for w in (w_new, w_f, w_s, w_low))
    return (
        block_out.reshape(like), field_grad.reshape(like), norm.reshape(()),
        w_new, w_f, w_s, w_low, v_new, v_f, v_s,
    )


def solution(mesh):
    tile, kernel = P(None, "lat", "lon", None), P(None, "lat", "lon")
    return jax.shard_map(
        functools.partial(body, mesh.shape["lat"], mesh.shape["lon"]),
        mesh=mesh,
        in_specs=(tile, P(), P(), kernel, kernel, tile, kernel, kernel, kernel, P(), P(), P()),
        out_specs=(tile, tile, P(), kernel, kernel, kernel, kernel, P(), P(), P()),
        check_vma=False,
    )
```

```python
import functools

import jax
import jax.numpy as jnp
from jax import lax
from jax.experimental import pallas as pl
from jax.experimental.pallas import tpu as pltpu
from jax.sharding import PartitionSpec as P

STEP = 10
EPS = 1e-05
MAX_NORM = 1.0
BETA_ONE = 0.9
BETA_TWO = 0.999
ADAM_EPS = 1e-08
RATE_KERNEL = 0.02
RATE_VECTOR = 0.1
DECAY = 0.01

MESH = pl.DeviceIdType.MESH
BF = jnp.bfloat16
F32 = jnp.float32
C = 128
R = 2
W = R * C
FIRST, SECOND = 0, 1


def cols_of(i):
    return slice(i * C, (i + 1) * C)


def twice(row):
    return jnp.concatenate([row, row], axis=1)


def fold(row):
    return row[:, :C] + row[:, C:]


def to_eight(block):
    rows, width = block.shape
    return jnp.sum(block.reshape(rows // 8, 8, width), axis=0)


def total_row(block):
    return jnp.sum(block, axis=0, keepdims=True)


def both_masks(missing, sea):
    have = (1 - missing).astype(F32)
    present = jnp.concatenate([have[0], have[1]], axis=0)
    counted = None
    if sea is not None:
        land = have * sea.astype(F32)
        counted = jnp.concatenate([land[0], land[1]], axis=0)
    return present, counted


def smooth(value):
    small = jnp.exp(-jnp.abs(value))
    one = 1.0 + small
    soft = jnp.maximum(value, 0.0) + jnp.log(one)
    sigmoid = jnp.where(value >= 0.0, 1.0, small) / one
    return 0.3 * value + 0.7 * soft, 0.3 + 0.7 * sigmoid


class Sizes:
    def __init__(self, nla, nlo, samples, quads, wrows, wcols):
        self.nla, self.nlo = nla, nlo
        self.n = nla * nlo
        self.B, self.Q = samples, quads
        self.PX = R * quads
        self.S = samples // nlo
        self.L = quads * nlo
        self.CH = self.S // 4 if self.S % 64 == 0 else 16
        self.nch = self.S // self.CH
        self.wr, self.wc = wrows, wcols
        self.LP = -(-wrows // 128) * 128


def main_kernel(
    z,
    fields, cot, sea_h, missing_h, mean_h, std_h, wt_h, vec_h,
    ob, fo, grads,
    fin, cin, sea, missing, mean, std, wt, vec, fb, pres, cm, cnt, sb, cb,
    X, H, G, F, act, slope, sg, ct, pre, bo, fs, red,
    w1, w2, t1, t2, acc1, acc2,
    ws, wg, kg_in, kf, kl,
    ca, cr, za, zr, kform, ssum, ts, lb, lr,
    y1, y2, y3,
    load_sem, mask_s, mask_r, f_s, f_r, c_s, c_r, halo_s, halo_r,
    bo_s, bo_r, bo_o, fo_s, fo_r, fo_o, wg_s, wg_r, kz_s, kz_r, kc_s, kc_r,
    rc_s, rc_r, rz_s, rz_r, ro_s, ro_r, y_s, y_r,
):
    nla, nlo, n = z.nla, z.nlo, z.n
    S, L, Q, CH, nch = z.S, z.L, z.Q, z.CH, z.nch
    la = lax.axis_index("lat")
    lo = lax.axis_index("lon")
    me = la * nlo + lo

    def remote(src, dst, ss, rs, lat_to, lon_to):
        return pltpu.make_async_remote_copy(
            src, dst, ss, rs, device_id=(lat_to, lon_to), device_id_type=MESH
        )

    def received(ref, sem):
        remote(ref, ref, sem, sem, la, lo).wait_recv()

    def sent(ref, sem):
        remote(ref, ref, sem, sem, la, lo).wait_send()

    def loop(low, high, body):
        def step(k, carry):
            body(k)
            return carry
        lax.fori_loop(low, high, step, 0)

    def others(body):
        upper = la // (nla // 2)

        def row(t):
            i = upper * t + (1 - upper) * (nla - 1 - t)

            def one(j):
                @pl.when(jnp.logical_or(i != la, j != lo))
                def _():
                    body(i, j)
            loop(0, nlo, one)
        loop(0, nla, row)

    own = pl.ds(C, W)

    def chunk(c):
        return pl.ds(pl.multiple_of(c * CH, CH), CH)

    def peer(k):
        return lax.rem(lo + k, nlo)

    barrier = pltpu.get_barrier_semaphore()
    others(lambda i, j: pl.semaphore_signal(barrier, inc=1, device_id=(i, j), device_id_type=MESH))
    pairs = (
        (missing_h, missing), (sea_h, sea), (mean_h, mean), (std_h, std), (wt_h, wt), (vec_h, vec),
        (fields, fin), (cot, cin),
    )
    loads = [pltpu.make_async_copy(src, dst, load_sem.at[i]) for i, (src, dst) in enumerate(pairs)]
    for load in loads:
        load.start()
    for load in loads[:-2]:
        load.wait()
    load_f, load_c = loads[-2:]

    present, counted = both_masks(missing[...], sea[...])
    pres[...] = present.T
    cm[lo] = counted
    pad = z.LP - z.wr
    for k in range(2):
        block = wt[k].astype(BF)
        if pad:
            block = jnp.concatenate([block, jnp.zeros((z.wc, pad), BF)], axis=1)
        ws[k] = block
        wg[lo, k] = block
    north_pole, south_pole = la == 0, la == nla - 1
    for ref in (X, H, G, F):
        @pl.when(north_pole)
        def _():
            ref[:, :, cols_of(0)] = jnp.zeros((L + 2, S, C), BF)

        @pl.when(south_pole)
        def _():
            ref[:, :, cols_of(3)] = jnp.zeros((L + 2, S, C), BF)

    def w_copy(k):
        m = peer(k)
        return remote(ws, wg.at[lo], wg_s.at[0], wg_r.at[0], la, m)

    def mask_copy(k):
        return remote(cm.at[lo], cm.at[lo], mask_s.at[0], mask_r.at[0], la, peer(k))

    load_f.wait()

    rstd = 1.0 / std[...]
    center_in = mean[...]

    def place(src, t, c, put, standardize):
        first = pl.multiple_of((t * S + c * CH) * z.PX, CH * z.PX)
        fb[...] = src[pl.ds(first, CH * z.PX), :].astype(F32)
        here = pres[pl.ds(pl.multiple_of(t * S + c * CH, CH), CH), :]
        for p in range(z.PX):
            value = fb[pl.ds(p, CH, stride=z.PX), :]
            if standardize:
                value = (value - center_in) * rstd * here[:, p : p + 1]
            put(p // Q, p % Q, value.astype(BF))

    def f_copy(c, k):
        return remote(
            sb.at[c, k], X.at[pl.ds(1 + Q * lo, Q), chunk(c), own],
            f_s.at[0], f_r.at[c], la, peer(k),
        )

    def c_copy(c, k):
        return remote(
            cb.at[c, k], ct.at[pl.ds(Q * lo, Q), chunk(c), :],
            c_s.at[0], c_r.at[c], la, peer(k),
        )

    def prep_fields(c):
        def one(k):
            def put(i, q, value):
                sb[c, k, q, :, cols_of(i)] = value
            place(fin, peer(k), c, put, True)
        loop(1, nlo, one)

    def send_fields(c):
        loop(1, nlo, lambda k: f_copy(c, k).start())

    def next_fields(c):
        prep_fields(c)
        send_fields(c)

    def own_fields(c):
        def put(i, q, value):
            X[1 + Q * lo + q, chunk(c), cols_of(i + 1)] = value
        place(fin, lo, c, put, True)

    def own_cot(c):
        def put(i, q, value):
            ct[Q * lo + q, chunk(c), cols_of(i)] = value
        place(cin, lo, c, put, False)

    def prep_cot(c):
        def one(k):
            def put(i, q, value):
                cb[c, k, q, :, cols_of(i)] = value
            place(cin, peer(k), c, put, False)
        loop(1, nlo, one)

    prep_fields(0)
    pl.semaphore_wait(barrier, n - 1)
    loop(1, nlo, lambda k: w_copy(k).start())
    loop(1, nlo, lambda k: mask_copy(k).start())
    send_fields(0)
    loop(1, nch, next_fields)

    received(wg.at[pl.ds(0, nlo - 1)], wg_r.at[0])
    for k in range(2):
        gathered = jnp.concatenate([wg[m, k].astype(F32) for m in range(nlo)], axis=0)
        kl[k] = gathered.T[: z.wr].astype(BF)
        kg_in[k, la] = kl[k]
    core = lax.rem(la, 2)
    sibling = la + 1 - 2 * core

    def kz_copy(k, d):
        to = lax.rem(la + 2 * d, nla)
        return remote(kl.at[k], kg_in.at[k, la], kz_s.at[k], kz_r.at[k], to, lo)

    def kc_copy(k, d):
        row = lax.rem(la + nla - 2 * d, nla)
        return remote(kg_in.at[k, row], kg_in.at[k, row], kc_s.at[k], kc_r.at[k], sibling, lo)

    def start_kernel(k):
        loop(1, nla // 2, lambda d: kz_copy(k, d).start())
        kc_copy(k, 0).start()

    def forward_kernel(k):
        received(kg_in.at[k, pl.ds(0, nla // 2 - 1)], kz_r.at[k])
        loop(1, nla // 2, lambda d: kc_copy(k, d).start())

    def finish_kernel(k):
        received(kg_in.at[k, pl.ds(0, nla // 2)], kc_r.at[k])
        for i in range(nla):
            kf[pl.ds(i * z.wr, z.wr), :] = kg_in[k, i].astype(F32)

    def tap(a, b):
        return kf[pl.ds((3 * a + b) * C, C), :]

    def build_forward(ref):
        for b in range(3):
            for r in range(4):
                for i in range(R):
                    a = r - i
                    good = 0 <= a <= 2
                    block = tap(a, b).astype(BF) if good else jnp.zeros((C, C), BF)
                    ref[pl.ds((b * 4 + r) * C, C), cols_of(i)] = block

    def build_turned(ref):
        for b in range(3):
            for a in range(3):
                block = tap(2 - a, 2 - b).T.astype(BF)
                for i in range(R):
                    ref[pl.ds((b * 4 + a + i) * C, C), cols_of(i)] = block
            for i, r in ((0, 3), (1, 0)):
                ref[pl.ds((b * 4 + r) * C, C), cols_of(i)] = jnp.zeros((C, C), BF)

    start_kernel(FIRST)
    start_kernel(SECOND)

    loop(0, nch, own_fields)
    load_c.wait()
    loop(0, nch, own_cot)
    loop(0, nch, prep_cot)

    def spread_mask():
        rows = jnp.concatenate([cm[m] for m in range(nlo)], axis=0)
        back = z.B - lo * S
        mine = pltpu.roll(rows, lax.rem(back, z.B), 1)[:, : min(z.B, 128)].T
        for j in range(L):
            for i in range(R):
                col = (j // Q) * z.PX + i * Q + j % Q
                cnt[j, :, cols_of(i)] = jnp.broadcast_to(mine[:S, col : col + 1], (S, C))

    def halo_copies(ref, h, c):
        def lanes(r):
            return ref.at[pl.ds(1, L), chunk(c), pl.ds(r * C, C)]

        north = remote(lanes(1), lanes(3), halo_s.at[h], halo_r.at[h, c], jnp.maximum(la - 1, 0), lo)
        south = remote(lanes(2), lanes(0), halo_s.at[h], halo_r.at[h, c], jnp.minimum(la + 1, nla - 1), lo)
        return north, south

    def halo_send(ref, h, c):
        north, south = halo_copies(ref, h, c)
        pl.when(la > 0)(north.start)
        pl.when(la < nla - 1)(south.start)

    at_pole = jnp.logical_or(north_pole, south_pole)

    def halo_wait(ref, h, c):
        def both(width):
            received(ref.at[pl.ds(1, L), chunk(c), pl.ds(0, width)], halo_r.at[h, c])
        pl.when(at_pole)(lambda: both(C))
        pl.when(jnp.logical_not(at_pole))(lambda: both(W))
        ref[0, chunk(c), :] = ref[L, chunk(c), :]
        ref[L + 1, chunk(c), :] = ref[1, chunk(c), :]

    def halo_done(ref, h):
        def both(width):
            sent(ref.at[pl.ds(1, L), :, pl.ds(0, width)], halo_s.at[h])
        pl.when(at_pole)(lambda: both(C))
        pl.when(jnp.logical_not(at_pole))(lambda: both(W))

    def taps(ref, c):
        parts = [ref[b : b + L, chunk(c), :].reshape(L * CH, 4 * C) for b in range(3)]
        return jnp.concatenate(parts, axis=1)

    def conv(lhs, kernel):
        out = jnp.dot(lhs, kernel[...], preferred_element_type=F32)
        pre[...] = out.reshape(L, CH, W)

    def kernel_grad(lhs, grad, acc):
        acc[...] += lax.dot_general(
            lhs, grad, (((0,), (0,)), ((), ())), preferred_element_type=F32
        )

    def columns(body, carry):
        return lax.fori_loop(0, L, body, carry, unroll=min(L, 16))

    zero8 = jnp.zeros((8, W), F32)

    def arrive(c):
        received(X.at[pl.ds(1, Q * (nlo - 1)), chunk(c), own], f_r.at[c])
        halo_send(X, 0, c)

    def first_chunk(c, stats):
        halo_wait(X, 0, c)
        conv(taps(X, c), w1)

        def one(j, carry):
            s, m = carry
            value, grad = smooth(pre[j])
            act[j, chunk(c), :] = value
            slope[j, chunk(c), :] = grad
            here = cnt[j, chunk(c), :]
            return s + to_eight(here * value), m + to_eight(here)

        s8, n8 = columns(one, (zero8, zero8))
        s_c, n_c = fold(total_row(s8)), fold(total_row(n8))
        mean_c = s_c / jnp.maximum(n_c, 1.0)
        mean_w = twice(mean_c)

        def two(j, m2):
            off = act[j, chunk(c), :] - mean_w
            return m2 + to_eight(cnt[j, chunk(c), :] * off * off)

        m_c = fold(total_row(columns(two, zero8)))
        n_0, s_0, m_0 = stats
        delta = mean_c - s_0 / jnp.maximum(n_0, 1.0)
        n_1 = n_0 + n_c
        m_1 = m_0 + m_c + delta * delta * (n_0 * n_c / jnp.maximum(n_1, 1.0))
        return n_1, s_0 + s_c, m_1

    def send_cot(c):
        loop(1, nlo, lambda k: c_copy(c, k).start())

    arrive(0)
    forward_kernel(FIRST)
    received(cm.at[pl.ds(0, nlo - 1)], mask_r.at[0])
    spread_mask()
    finish_kernel(FIRST)
    build_forward(w1)
    build_turned(t1)
    zero1 = jnp.zeros((1, C), F32)

    def first_step(c, stats):
        pl.when(c + 1 < nch)(lambda: arrive(c + 1))
        pl.when(c + 2 == nch)(lambda: send_cot(0))
        return first_chunk(c, stats)

    n_d, s_d, m_d = lax.fori_loop(0, nch, first_step, (zero1, zero1, zero1))

    def share(buf, which, value):
        buf[me] = value
        others(lambda i, j: remote(buf.at[me], buf.at[me], y_s.at[which], y_r.at[which], i, j).start())

    def shared(buf, which):
        block = remote(buf.at[pl.ds(0, n - 1)], buf.at[pl.ds(0, n - 1)], y_s.at[which], y_r.at[which], la, lo)
        block.wait_recv()
        block.wait_send()
        return buf[...]

    share(y1, 0, jnp.concatenate([n_d, s_d, m_d], axis=1))
    loop(1, nch, send_cot)
    forward_kernel(SECOND)
    finish_kernel(SECOND)
    build_forward(w2)
    build_turned(t2)
    acc1[...] = jnp.zeros_like(acc1)
    acc2[...] = jnp.zeros_like(acc2)

    parts = shared(y1, 0)
    n_all, s_all, m_all = parts[:, :, :C], parts[:, :, C : 2 * C], parts[:, :, 2 * C :]
    total = jnp.sum(n_all, axis=0)
    center = jnp.sum(s_all, axis=0) / total
    apart = s_all / jnp.maximum(n_all, 1.0) - center[None]
    spread = jnp.sum(m_all + n_all * apart * apart, axis=0) / total
    inverse = lax.rsqrt(spread + EPS)
    gain, shift, bias = vec[0:1, :], vec[1:2, :], vec[2:3, :]
    center_w, inverse_w = twice(center), twice(inverse)
    gain_w, shift_w, bias_w = twice(gain), twice(shift), twice(bias)

    chip, chips = la // 2, nla // 2

    def rows_of(k, i):
        return kform[k, pl.ds(pl.multiple_of(i * z.wr, 8), z.wr), :]

    def core_copy(k):
        return remote(ca.at[k], cr.at[k], rc_s.at[k], rc_r.at[k], sibling, lo)

    def core_start(k, acc):
        for a in range(3):
            for b in range(3):
                top, low = (b * 4 + a) * C, (b * 4 + a + 1) * C
                kform[k, pl.ds((3 * a + b) * C, C), :] = (
                    acc[pl.ds(top, C), cols_of(0)] + acc[pl.ds(low, C), cols_of(1)]
                )

        def one(t):
            ca[k, t] = rows_of(k, 2 * t + 1 - core).astype(BF)
        loop(0, chips, one)
        core_copy(k).start()

    def chip_copy(k, t, slot):
        return remote(za.at[k, t], zr.at[k, slot], rz_s.at[k], rz_r.at[k], 2 * t + core, lo)

    def chip_start(k):
        core_copy(k).wait_recv()
        ssum[k] = jnp.zeros_like(ssum[k])
        ssum[k, 0 : z.wr, :] = rows_of(k, la) + cr[k, chip].astype(F32)

        def one(t):
            @pl.when(t != chip)
            def _():
                za[k, t] = (rows_of(k, 2 * t + core) + cr[k, t].astype(F32)).astype(BF)
                chip_copy(k, t, chip).start()
        loop(0, chips, one)

    def lon_copy(k, m):
        return remote(lb.at[k, m], lr.at[k, lo], ro_s.at[k], ro_r.at[k], la, m)

    def lon_start(k):
        received(zr.at[k, pl.ds(0, chips - 1)], rz_r.at[k])

        def one(t):
            @pl.when(t != chip)
            def _():
                ssum[k, 0 : z.wr, :] += zr[k, t].astype(F32)
        loop(0, chips, one)
        ts[k] = ssum[k].T

        def two(m):
            lb[k, m] = ts[k, pl.ds(pl.multiple_of(m * z.wc, z.wc), z.wc), :].astype(BF)
            pl.when(m != lo)(lambda: lon_copy(k, m).start())
        loop(0, nlo, two)

    def lon_finish(k):
        received(lr.at[k, pl.ds(0, nlo - 1)], ro_r.at[k])
        grads[k, 0 : z.wc] = ts[k, pl.ds(pl.multiple_of(lo * z.wc, z.wc), z.wc), :]

        def one(m):
            @pl.when(m != lo)
            def _():
                grads[k, 0 : z.wc] += lr[k, m].astype(F32)
        loop(0, nlo, one)

    def hidden(c):
        def one(j, carry):
            normed = (act[j, chunk(c), :] - center_w) * inverse_w
            H[1 + j, chunk(c), own] = (normed * gain_w + shift_w).astype(BF)
            return carry
        columns(one, 0)
        halo_send(H, 1, c)

    def out_copy(src, dst, ss, rs, c, k):
        m = peer(k)
        return remote(
            src.at[pl.ds(Q * m, Q), chunk(c), :],
            dst.at[:, pl.ds(pl.multiple_of(lo * S + c * CH, CH), CH), :],
            ss.at[0], rs.at[0], la, m,
        )

    def own_out(src, dst, os, c):
        return pltpu.make_async_copy(
            src.at[pl.ds(Q * lo, Q), chunk(c), :],
            dst.at[:, pl.ds(pl.multiple_of(lo * S + c * CH, CH), CH), :],
            os.at[0],
        )

    def send_out(src, dst, ss, rs, os, c):
        loop(1, nlo, lambda k: out_copy(src, dst, ss, rs, c, k).start())
        own_out(src, dst, os, c).start()

    def out_done(src, dst, ss, rs, os):
        sent(src.at[pl.ds(0, Q * (nlo - 1))], ss.at[0])
        received(dst.at[:, pl.ds(0, S * (nlo - 1)), :], rs.at[0])
        pltpu.make_async_copy(src.at[pl.ds(0, Q)], dst.at[:, pl.ds(0, S), :], os.at[0]).wait()

    block_out = (bo, ob, bo_s, bo_r, bo_o)
    field_out = (fs, fo, fo_s, fo_r, fo_o)
    early = min(1, nch - 1)

    def second_chunk(c):
        halo_wait(H, 1, c)
        received(ct.at[pl.ds(0, Q * (nlo - 1)), chunk(c), :], c_r.at[c])
        conv(taps(H, c), w2)

        def one(j, carry):
            value, grad = smooth(pre[j] + bias_w)
            standard = X[1 + j, chunk(c), own].astype(F32)
            bo[j, chunk(c), :] = (standard + value).astype(BF)
            low = (ct[j, chunk(c), :].astype(F32) * grad).astype(BF)
            G[1 + j, chunk(c), own] = low
            return carry + to_eight(low.astype(F32))

        red[0] += columns(one, zero8)
        halo_send(G, 2, c)

    def second_kernel(c):
        grad = G[1 : 1 + L, chunk(c), own].reshape(L * CH, W)
        kernel_grad(taps(H, c), grad, acc2)

    def back_chunk(c):
        halo_wait(G, 2, c)
        conv(taps(G, c), t2)

        def one(j, carry):
            g8, s8 = carry
            value = pre[j]
            sg[j, chunk(c), :] = value
            normed = (act[j, chunk(c), :] - center_w) * inverse_w
            return g8 + to_eight(value * normed), s8 + to_eight(value)

        g8, s8 = columns(one, (zero8, zero8))
        red[1] += g8
        red[2] += s8

    loop(0, nch, hidden)
    def second_step(c):
        second_chunk(c)
        pl.when(c < early)(lambda: send_out(*block_out, c))

    red[...] = jnp.zeros_like(red)
    loop(0, nch, second_step)
    loop(0, nch, second_kernel)
    core_start(SECOND, acc2)
    loop(0, nch, back_chunk)
    sums = [fold(total_row(red[k])) for k in (1, 2, 0)]
    share(y2, 1, jnp.concatenate(sums, axis=1))
    loop(early, nch, lambda c: send_out(*block_out, c))

    chip_start(SECOND)
    sums = jnp.sum(shared(y2, 1), axis=0)
    gain_grad, shift_grad = sums[:, :C], sums[:, C : 2 * C]

    scale_w = twice(inverse * gain)
    shift_part = twice(shift_grad / total)
    gain_part = twice(gain_grad / total)

    def first_grad(c):
        def one(j, carry):
            normed = (act[j, chunk(c), :] - center_w) * inverse_w
            here = cnt[j, chunk(c), :]
            value = sg[j, chunk(c), :] - here * shift_part - here * normed * gain_part
            F[1 + j, chunk(c), own] = (scale_w * value * slope[j, chunk(c), :]).astype(BF)
            return carry
        columns(one, 0)
        halo_send(F, 3, c)

    def first_kernel(c):
        grad = F[1 : 1 + L, chunk(c), own].reshape(L * CH, W)
        kernel_grad(taps(X, c), grad, acc1)

    def field_chunk(c):
        halo_wait(F, 3, c)
        out = jnp.dot(taps(F, c), t1[...], preferred_element_type=F32)
        fs[:, chunk(c), :] = out.astype(BF).reshape(L, CH, W)

    def send_field(c):
        send_out(*field_out, c)

    held = max(nch - 2, 1)
    def field_step(c):
        field_chunk(c)
        pl.when(c < held)(lambda: send_field(c))
        pl.when(c == 1)(lambda: chip_start(FIRST))

    loop(0, nch, first_grad)
    loop(0, nch, first_kernel)
    core_start(FIRST, acc1)
    loop(0, nch, field_step)
    lon_start(SECOND)
    lon_start(FIRST)
    loop(held, nch - 1, send_field)
    lon_finish(SECOND)
    lon_finish(FIRST)
    first_w, second_w = grads[0, 0 : z.wc], grads[1, 0 : z.wc]
    square = total_row(first_w * first_w + second_w * second_w)
    share(y3, 2, sum(square[:, cols_of(t)] for t in range(z.LP // C)))
    loop(max(held, nch - 1), nch, send_field)
    squares = jnp.sum(shared(y3, 2), axis=0)
    mine2 = sum(sums[:, cols_of(t)] * sums[:, cols_of(t)] for t in range(3))
    norm = jnp.sqrt(jnp.sum(squares + mine2, axis=1, keepdims=True))
    for k in range(3):
        grads[0, z.wc + k : z.wc + k + 1, 0:C] = sums[:, cols_of(k)]
    grads[0, z.wc + 3 : z.wc + 4, 0:C] = jnp.broadcast_to(norm, (1, C))

    sent(sb.at[:, pl.ds(1, nlo - 1)], f_s.at[0])
    sent(cb.at[:, pl.ds(1, nlo - 1)], c_s.at[0])
    sent(wg.at[pl.ds(0, nlo - 1)], wg_s.at[0])
    sent(cm.at[pl.ds(0, nlo - 1)], mask_s.at[0])
    for h, ref in enumerate((X, H, G, F)):
        halo_done(ref, h)
    for k in range(2):
        sent(kg_in.at[k, pl.ds(0, nla // 2 - 1)], kz_s.at[k])
        sent(kg_in.at[k, pl.ds(0, nla // 2)], kc_s.at[k])
        core_copy(k).wait_send()
        sent(zr.at[k, pl.ds(0, chips - 1)], rz_s.at[k])
        sent(lr.at[k, pl.ds(0, nlo - 1)], ro_s.at[k])
    out_done(*block_out)
    out_done(*field_out)


def adam_step(master, first, second, grads, rate, decay):
    first_new = BETA_ONE * first + (1.0 - BETA_ONE) * grads
    second_new = BETA_TWO * second + (1.0 - BETA_TWO) * grads * grads
    first_hat = first_new / (1.0 - BETA_ONE**STEP)
    second_hat = second_new / (1.0 - BETA_TWO**STEP)
    master_new = master - rate * (first_hat / (jnp.sqrt(second_hat) + ADAM_EPS) + decay * master)
    return master_new, first_new, second_new


def last_kernel(
    z, step,
    ob, fo, cot, missing, std, grads, wm, wf, wsec, vm, vf, vs,
    block_out, field_grad, norm, w_new, w_first, w_second, w_low, v_new, v_first, v_second,
    cf, bf,
):
    Q = z.Q
    present, _ = both_masks(missing[...], None)
    have = present.T
    rstd = 1.0 / std[...]
    cf[...] = cot[...].astype(F32)
    for p in range(z.PX):
        i, q = p // Q, p % Q
        here = pl.ds(p, step, stride=z.PX)
        grad = cf[here, :] + fo[q, :, cols_of(i)].astype(F32)
        field_grad[here, :] = grad * have[:, p : p + 1] * rstd
        bf[here, :] = ob[q, :, cols_of(i)].astype(F32)
    block_out[...] = bf[...].astype(BF)

    @pl.when(pl.program_id(0) == 0)
    def _():
        size = grads[0, z.wc + 3 : z.wc + 4, 0:C]
        norm[...] = size[:, 0:1]
        factor = jnp.minimum(1.0, MAX_NORM / size)
        wide = factor[:, 0:1]
        for k in range(2):
            own = grads[k, 0 : z.wc, 0 : z.wr] * wide
            new, first, second = adam_step(wm[k], wf[k], wsec[k], own, RATE_KERNEL, DECAY)
            w_new[k], w_first[k], w_second[k] = new, first, second
            w_low[k] = new.astype(BF)
        for k in range(3):
            own = grads[0, z.wc + k : z.wc + k + 1, 0:C] * factor
            row = slice(k, k + 1)
            new, first, second = adam_step(vm[row, :], vf[row, :], vs[row, :], own, RATE_VECTOR, 0.0)
            v_new[row, :], v_first[row, :], v_second[row, :] = new, first, second


def body(nla, nlo, fields, chan_mean, chan_std, sea_mask, missing, cotangent,
         w_master, w_first, w_second, vec_master, vec_first, vec_second):
    samples, rows, quads, channels = fields.shape
    z = Sizes(nla, nlo, samples, quads, w_master.shape[1], w_master.shape[2])
    S, L, Q, CH, nch, n, B = z.S, z.L, z.Q, z.CH, z.nch, z.n, z.B
    flat = (samples * rows * quads, channels)
    fields = fields.reshape(flat)
    cotangent = cotangent.reshape(flat)
    sea = jnp.transpose(sea_mask, (1, 2, 0))
    miss = jnp.transpose(missing, (1, 2, 0))
    wm, wf, wsec = (jnp.transpose(w, (0, 2, 1)) for w in (w_master, w_first, w_second))
    mean, std = chan_mean.reshape(1, C), chan_std.reshape(1, C)

    vmem = pl.BlockSpec(memory_space=pltpu.VMEM)
    hbm = pl.BlockSpec(memory_space=pl.ANY)
    V = pltpu.VMEM
    dma = pltpu.SemaphoreType.DMA
    shape = jax.ShapeDtypeStruct
    padded = V((L + 2, S, 2 * W), BF)
    wide = V((L, S, W), F32)
    scratch = [
        V(flat, BF), V(flat, BF), V(sea.shape, sea.dtype), V(miss.shape, miss.dtype),
        V((1, C), F32), V((1, C), F32), V(wm.shape, F32), V((3, C), F32),
        V((CH * z.PX, C), F32), V((B, z.PX), F32),
        V((nlo, z.PX, B), F32), wide,
        V((nch, nlo, Q, CH, W), BF), V((nch, nlo, Q, CH, W), BF),
        padded, padded, padded, padded, wide, wide, wide,
        V((L, S, W), BF), V((L, CH, W), F32), V((L, S, W), BF), V((L, S, W), BF), V((3, 8, W), F32),
        V((12 * C, W), BF), V((12 * C, W), BF), V((12 * C, W), BF), V((12 * C, W), BF),
        V((12 * C, W), F32), V((12 * C, W), F32),
        V((2, z.wc, z.LP), BF), V((nlo, 2, z.wc, z.LP), BF), V((2, nla, z.wr, C), BF),
        V((9 * C, C), F32), V((2, z.wr, C), BF),
        V((2, nla // 2, z.wr, C), BF), V((2, nla // 2, z.wr, C), BF),
        V((2, nla // 2, z.wr, C), BF), V((2, nla // 2, z.wr, C), BF), V((2, 9 * C, C), F32),
        V((2, z.LP, C), F32), V((2, C, z.LP), F32), V((2, nlo, z.wc, z.LP), BF), V((2, nlo, z.wc, z.LP), BF),
        V((n, 1, 3 * C), F32), V((n, 1, 3 * C), F32), V((n, 1, C), F32),
        dma((8,)), dma((1,)), dma((1,)), dma((1,)), dma((nch,)), dma((1,)), dma((nch,)),
        dma((4,)), dma((4, nch)),
        dma((1,)), dma((1,)), dma((1,)), dma((1,)), dma((1,)), dma((1,)), dma((1,)), dma((1,)),
        dma((2,)), dma((2,)), dma((2,)), dma((2,)),
        dma((2,)), dma((2,)), dma((2,)), dma((2,)), dma((2,)), dma((2,)), dma((3,)), dma((3,)),
    ]
    ob, fo, grads = pl.pallas_call(
        functools.partial(main_kernel, z),
        out_shape=(
            shape((Q, B, W), BF), shape((Q, B, W), BF),
            shape((2, z.wc + 8, z.LP), F32),
        ),
        in_specs=[hbm] * 8,
        out_specs=(hbm, hbm, vmem),
        scratch_shapes=scratch,
        compiler_params=pltpu.CompilerParams(
            collective_id=0, has_side_effects=True, vmem_limit_bytes=56 * 2**20
        ),
        name="block",
    )(fields, cotangent, sea, miss, mean, std, wm, vec_master)

    step = min(128, B)
    whole = lambda s: pl.BlockSpec(s, lambda t: (0,) * len(s))
    native = pl.BlockSpec((step * z.PX, C), lambda t: (t, 0))
    spread = pl.BlockSpec((Q, step, W), lambda t: (0, t, 0))
    w_spec, v_spec = whole(wm.shape), whole((3, C))
    outs = pl.pallas_call(
        functools.partial(last_kernel, z, step),
        grid=(B // step,),
        out_shape=(
            shape(flat, BF), shape(flat, F32), shape((1, 1), F32),
            shape(wm.shape, F32), shape(wm.shape, F32), shape(wm.shape, F32), shape(wm.shape, BF),
            shape((3, C), F32), shape((3, C), F32), shape((3, C), F32),
        ),
        in_specs=[
            spread, spread, native, pl.BlockSpec((R, Q, step), lambda t: (0, 0, t)), whole((1, C)),
            whole(grads.shape),
            w_spec, w_spec, w_spec, v_spec, v_spec, v_spec,
        ],
        out_specs=(native, native, whole((1, 1)), w_spec, w_spec, w_spec, w_spec, v_spec, v_spec, v_spec),
        scratch_shapes=[V((step * z.PX, C), F32), V((step * z.PX, C), F32)],
        compiler_params=pltpu.CompilerParams(vmem_limit_bytes=60 * 2**20),
        name="update",
    )(ob, fo, cotangent, miss, std, grads, wm, wf, wsec, vec_master, vec_first, vec_second)
    block_out, field_grad, norm, w_new, w_f, w_s, w_low, v_new, v_f, v_s = outs
    like = (samples, rows, quads, channels)
    w_new, w_f, w_s, w_low = (jnp.transpose(w, (0, 2, 1)) for w in (w_new, w_f, w_s, w_low))
    return (
        block_out.reshape(like), field_grad.reshape(like), norm.reshape(()),
        w_new, w_f, w_s, w_low, v_new, v_f, v_s,
    )


def solution(mesh):
    tile, kernel = P(None, "lat", "lon", None), P(None, "lat", "lon")
    return jax.shard_map(
        functools.partial(body, mesh.shape["lat"], mesh.shape["lon"]),
        mesh=mesh,
        in_specs=(tile, P(), P(), kernel, kernel, tile, kernel, kernel, kernel, P(), P(), P()),
        out_specs=(tile, tile, P(), kernel, kernel, kernel, kernel, P(), P(), P()),
        check_vma=False,
    )
```

```python
import functools

import jax
import jax.numpy as jnp
from jax import lax
from jax.experimental import pallas as pl
from jax.experimental.pallas import tpu as pltpu
from jax.sharding import PartitionSpec as P

STEP = 10
EPS = 1e-05
MAX_NORM = 1.0
BETA_ONE = 0.9
BETA_TWO = 0.999
ADAM_EPS = 1e-08
RATE_KERNEL = 0.02
RATE_VECTOR = 0.1
DECAY = 0.01

MESH = pl.DeviceIdType.MESH
BF = jnp.bfloat16
F32 = jnp.float32
C = 128
R = 2
W = R * C
FIRST, SECOND = 0, 1


def cols_of(i):
    return slice(i * C, (i + 1) * C)


def twice(row):
    return jnp.concatenate([row, row], axis=1)


def fold(row):
    return row[:, :C] + row[:, C:]


def to_eight(block):
    rows, width = block.shape
    return jnp.sum(block.reshape(rows // 8, 8, width), axis=0)


def total_row(block):
    return jnp.sum(block, axis=0, keepdims=True)


def both_masks(missing, sea):
    have = (1 - missing).astype(F32)
    present = jnp.concatenate([have[0], have[1]], axis=0)
    counted = None
    if sea is not None:
        land = have * sea.astype(F32)
        counted = jnp.concatenate([land[0], land[1]], axis=0)
    return present, counted


def smooth(value):
    small = jnp.exp(-jnp.abs(value))
    one = 1.0 + small
    soft = jnp.maximum(value, 0.0) + jnp.log(one)
    sigmoid = jnp.where(value >= 0.0, 1.0, small) / one
    return 0.3 * value + 0.7 * soft, 0.3 + 0.7 * sigmoid


class Sizes:
    def __init__(self, nla, nlo, samples, quads, wrows, wcols):
        self.nla, self.nlo = nla, nlo
        self.n = nla * nlo
        self.B, self.Q = samples, quads
        self.PX = R * quads
        self.S = samples // nlo
        self.L = quads * nlo
        self.CH = self.S // 4 if self.S % 64 == 0 else 16
        self.nch = self.S // self.CH
        self.wr, self.wc = wrows, wcols
        self.LP = -(-wrows // 128) * 128


def main_kernel(
    z,
    fields, cot, sea_h, missing_h, mean_h, std_h, wt_h, vec_h,
    out_low, out_grad, grads,
    ob, fo, fin, cin, sea, missing, mean, std, wt, vec, fb, pres, cm, cnt, sb, cb,
    X, H, G, F, act, slope, sg, ct, pre, bo, fs, red,
    w1, w2, t1, t2, acc1, acc2,
    ws, wg, kg_in, kf, kl,
    ca, cr, za, zr, kform, ssum, ts, lb, lr,
    y1, y2, y3,
    load_sem, mask_s, mask_r, f_s, f_r, c_s, c_r, halo_s, halo_r,
    bo_s, bo_r, bo_o, fo_s, fo_r, fo_o, wg_s, wg_r, kz_s, kz_r, kc_s, kc_r,
    rc_s, rc_r, rz_s, rz_r, ro_s, ro_r, y_s, y_r,
):
    nla, nlo, n = z.nla, z.nlo, z.n
    S, L, Q, CH, nch = z.S, z.L, z.Q, z.CH, z.nch
    la = lax.axis_index("lat")
    lo = lax.axis_index("lon")
    me = la * nlo + lo

    def remote(src, dst, ss, rs, lat_to, lon_to):
        return pltpu.make_async_remote_copy(
            src, dst, ss, rs, device_id=(lat_to, lon_to), device_id_type=MESH
        )

    def received(ref, sem):
        remote(ref, ref, sem, sem, la, lo).wait_recv()

    def sent(ref, sem):
        remote(ref, ref, sem, sem, la, lo).wait_send()

    def loop(low, high, body):
        def step(k, carry):
            body(k)
            return carry
        lax.fori_loop(low, high, step, 0)

    def others(body):
        upper = la // (nla // 2)

        def row(t):
            i = upper * t + (1 - upper) * (nla - 1 - t)

            def one(j):
                @pl.when(jnp.logical_or(i != la, j != lo))
                def _():
                    body(i, j)
            loop(0, nlo, one)
        loop(0, nla, row)

    own = pl.ds(C, W)

    def chunk(c):
        return pl.ds(pl.multiple_of(c * CH, CH), CH)

    def peer(k):
        return lax.rem(lo + k, nlo)

    barrier = pltpu.get_barrier_semaphore()
    others(lambda i, j: pl.semaphore_signal(barrier, inc=1, device_id=(i, j), device_id_type=MESH))
    pairs = (
        (missing_h, missing), (sea_h, sea), (mean_h, mean), (std_h, std), (wt_h, wt), (vec_h, vec),
        (fields, fin), (cot, cin),
    )
    loads = [pltpu.make_async_copy(src, dst, load_sem.at[i]) for i, (src, dst) in enumerate(pairs)]
    for load in loads:
        load.start()
    for load in loads[:-2]:
        load.wait()
    load_f, load_c = loads[-2:]

    present, counted = both_masks(missing[...], sea[...])
    pres[...] = present.T
    cm[lo] = counted
    pad = z.LP - z.wr
    for k in range(2):
        block = wt[k].astype(BF)
        if pad:
            block = jnp.concatenate([block, jnp.zeros((z.wc, pad), BF)], axis=1)
        ws[k] = block
        wg[lo, k] = block
    north_pole, south_pole = la == 0, la == nla - 1
    for ref in (X, H, G, F):
        @pl.when(north_pole)
        def _():
            ref[:, :, cols_of(0)] = jnp.zeros((L + 2, S, C), BF)

        @pl.when(south_pole)
        def _():
            ref[:, :, cols_of(3)] = jnp.zeros((L + 2, S, C), BF)

    def w_copy(k):
        m = peer(k)
        return remote(ws, wg.at[lo], wg_s.at[0], wg_r.at[0], la, m)

    def mask_copy(k):
        return remote(cm.at[lo], cm.at[lo], mask_s.at[0], mask_r.at[0], la, peer(k))

    load_f.wait()

    rstd = 1.0 / std[...]
    center_in = mean[...]

    def place(src, t, c, put, standardize):
        first = pl.multiple_of((t * S + c * CH) * z.PX, CH * z.PX)
        fb[...] = src[pl.ds(first, CH * z.PX), :].astype(F32)
        here = pres[pl.ds(pl.multiple_of(t * S + c * CH, CH), CH), :]
        for p in range(z.PX):
            value = fb[pl.ds(p, CH, stride=z.PX), :]
            if standardize:
                value = (value - center_in) * rstd * here[:, p : p + 1]
            put(p // Q, p % Q, value.astype(BF))

    def f_copy(c, k):
        return remote(
            sb.at[c, k], X.at[pl.ds(1 + Q * lo, Q), chunk(c), own],
            f_s.at[0], f_r.at[c], la, peer(k),
        )

    def c_copy(c, k):
        return remote(
            cb.at[c, k], ct.at[pl.ds(Q * lo, Q), chunk(c), :],
            c_s.at[0], c_r.at[c], la, peer(k),
        )

    def prep_fields(c):
        def one(k):
            def put(i, q, value):
                sb[c, k, q, :, cols_of(i)] = value
            place(fin, peer(k), c, put, True)
        loop(1, nlo, one)

    def send_fields(c):
        loop(1, nlo, lambda k: f_copy(c, k).start())

    def next_fields(c):
        prep_fields(c)
        send_fields(c)

    def own_fields(c):
        def put(i, q, value):
            X[1 + Q * lo + q, chunk(c), cols_of(i + 1)] = value
        place(fin, lo, c, put, True)

    def own_cot(c):
        def put(i, q, value):
            ct[Q * lo + q, chunk(c), cols_of(i)] = value
        place(cin, lo, c, put, False)

    def prep_cot(c):
        def one(k):
            def put(i, q, value):
                cb[c, k, q, :, cols_of(i)] = value
            place(cin, peer(k), c, put, False)
        loop(1, nlo, one)

    prep_fields(0)
    pl.semaphore_wait(barrier, n - 1)
    loop(1, nlo, lambda k: w_copy(k).start())
    loop(1, nlo, lambda k: mask_copy(k).start())
    send_fields(0)
    loop(1, nch, next_fields)

    received(wg.at[pl.ds(0, nlo - 1)], wg_r.at[0])
    for k in range(2):
        gathered = jnp.concatenate([wg[m, k].astype(F32) for m in range(nlo)], axis=0)
        kl[k] = gathered.T[: z.wr].astype(BF)
        kg_in[k, la] = kl[k]
    core = lax.rem(la, 2)
    sibling = la + 1 - 2 * core

    def kz_copy(k, d):
        to = lax.rem(la + 2 * d, nla)
        return remote(kl.at[k], kg_in.at[k, la], kz_s.at[k], kz_r.at[k], to, lo)

    def kc_copy(k, d):
        row = lax.rem(la + nla - 2 * d, nla)
        return remote(kg_in.at[k, row], kg_in.at[k, row], kc_s.at[k], kc_r.at[k], sibling, lo)

    def start_kernel(k):
        loop(1, nla // 2, lambda d: kz_copy(k, d).start())
        kc_copy(k, 0).start()

    def forward_kernel(k):
        received(kg_in.at[k, pl.ds(0, nla // 2 - 1)], kz_r.at[k])
        loop(1, nla // 2, lambda d: kc_copy(k, d).start())

    def finish_kernel(k):
        received(kg_in.at[k, pl.ds(0, nla // 2)], kc_r.at[k])
        for i in range(nla):
            kf[pl.ds(i * z.wr, z.wr), :] = kg_in[k, i].astype(F32)

    def tap(a, b):
        return kf[pl.ds((3 * a + b) * C, C), :]

    def build_forward(ref):
        for b in range(3):
            for r in range(4):
                for i in range(R):
                    a = r - i
                    good = 0 <= a <= 2
                    block = tap(a, b).astype(BF) if good else jnp.zeros((C, C), BF)
                    ref[pl.ds((b * 4 + r) * C, C), cols_of(i)] = block

    def build_turned(ref):
        for b in range(3):
            for a in range(3):
                block = tap(2 - a, 2 - b).T.astype(BF)
                for i in range(R):
                    ref[pl.ds((b * 4 + a + i) * C, C), cols_of(i)] = block
            for i, r in ((0, 3), (1, 0)):
                ref[pl.ds((b * 4 + r) * C, C), cols_of(i)] = jnp.zeros((C, C), BF)

    start_kernel(FIRST)
    start_kernel(SECOND)

    loop(0, nch, own_fields)
    load_c.wait()
    loop(0, nch, own_cot)
    loop(0, nch, prep_cot)

    def spread_mask():
        rows = jnp.concatenate([cm[m] for m in range(nlo)], axis=0)
        back = z.B - lo * S
        mine = pltpu.roll(rows, lax.rem(back, z.B), 1)[:, : min(z.B, 128)].T
        for j in range(L):
            for i in range(R):
                col = (j // Q) * z.PX + i * Q + j % Q
                cnt[j, :, cols_of(i)] = jnp.broadcast_to(mine[:S, col : col + 1], (S, C))

    def halo_copies(ref, h, c):
        def lanes(r):
            return ref.at[pl.ds(1, L), chunk(c), pl.ds(r * C, C)]

        north = remote(lanes(1), lanes(3), halo_s.at[h], halo_r.at[h, c], jnp.maximum(la - 1, 0), lo)
        south = remote(lanes(2), lanes(0), halo_s.at[h], halo_r.at[h, c], jnp.minimum(la + 1, nla - 1), lo)
        return north, south

    def halo_send(ref, h, c):
        north, south = halo_copies(ref, h, c)
        pl.when(la > 0)(north.start)
        pl.when(la < nla - 1)(south.start)

    at_pole = jnp.logical_or(north_pole, south_pole)

    def halo_wait(ref, h, c):
        def both(width):
            received(ref.at[pl.ds(1, L), chunk(c), pl.ds(0, width)], halo_r.at[h, c])
        pl.when(at_pole)(lambda: both(C))
        pl.when(jnp.logical_not(at_pole))(lambda: both(W))
        ref[0, chunk(c), :] = ref[L, chunk(c), :]
        ref[L + 1, chunk(c), :] = ref[1, chunk(c), :]

    def halo_done(ref, h):
        def both(width):
            sent(ref.at[pl.ds(1, L), :, pl.ds(0, width)], halo_s.at[h])
        pl.when(at_pole)(lambda: both(C))
        pl.when(jnp.logical_not(at_pole))(lambda: both(W))

    def taps(ref, c):
        parts = [ref[b : b + L, chunk(c), :].reshape(L * CH, 4 * C) for b in range(3)]
        return jnp.concatenate(parts, axis=1)

    def conv(lhs, kernel):
        out = jnp.dot(lhs, kernel[...], preferred_element_type=F32)
        pre[...] = out.reshape(L, CH, W)

    def kernel_grad(lhs, grad, acc):
        acc[...] += lax.dot_general(
            lhs, grad, (((0,), (0,)), ((), ())), preferred_element_type=F32
        )

    def columns(body, carry):
        return lax.fori_loop(0, L, body, carry, unroll=min(L, 16))

    zero8 = jnp.zeros((8, W), F32)

    def arrive(c):
        received(X.at[pl.ds(1, Q * (nlo - 1)), chunk(c), own], f_r.at[c])
        halo_send(X, 0, c)

    def first_chunk(c, stats):
        halo_wait(X, 0, c)
        conv(taps(X, c), w1)

        def one(j, carry):
            s, m = carry
            value, grad = smooth(pre[j])
            act[j, chunk(c), :] = value
            slope[j, chunk(c), :] = grad
            here = cnt[j, chunk(c), :]
            return s + to_eight(here * value), m + to_eight(here)

        s8, n8 = columns(one, (zero8, zero8))
        s_c, n_c = fold(total_row(s8)), fold(total_row(n8))
        mean_c = s_c / jnp.maximum(n_c, 1.0)
        mean_w = twice(mean_c)

        def two(j, m2):
            off = act[j, chunk(c), :] - mean_w
            return m2 + to_eight(cnt[j, chunk(c), :] * off * off)

        m_c = fold(total_row(columns(two, zero8)))
        n_0, s_0, m_0 = stats
        delta = mean_c - s_0 / jnp.maximum(n_0, 1.0)
        n_1 = n_0 + n_c
        m_1 = m_0 + m_c + delta * delta * (n_0 * n_c / jnp.maximum(n_1, 1.0))
        return n_1, s_0 + s_c, m_1

    def send_cot(c):
        loop(1, nlo, lambda k: c_copy(c, k).start())

    arrive(0)
    forward_kernel(FIRST)
    received(cm.at[pl.ds(0, nlo - 1)], mask_r.at[0])
    spread_mask()
    finish_kernel(FIRST)
    build_forward(w1)
    build_turned(t1)
    zero1 = jnp.zeros((1, C), F32)

    def first_step(c, stats):
        pl.when(c + 1 < nch)(lambda: arrive(c + 1))
        pl.when(c + 2 == nch)(lambda: send_cot(0))
        return first_chunk(c, stats)

    n_d, s_d, m_d = lax.fori_loop(0, nch, first_step, (zero1, zero1, zero1))

    def share(buf, which, value):
        buf[me] = value
        others(lambda i, j: remote(buf.at[me], buf.at[me], y_s.at[which], y_r.at[which], i, j).start())

    def shared(buf, which):
        block = remote(buf.at[pl.ds(0, n - 1)], buf.at[pl.ds(0, n - 1)], y_s.at[which], y_r.at[which], la, lo)
        block.wait_recv()
        block.wait_send()
        return buf[...]

    share(y1, 0, jnp.concatenate([n_d, s_d, m_d], axis=1))
    loop(1, nch, send_cot)
    forward_kernel(SECOND)
    finish_kernel(SECOND)
    build_forward(w2)
    build_turned(t2)
    acc1[...] = jnp.zeros_like(acc1)
    acc2[...] = jnp.zeros_like(acc2)

    parts = shared(y1, 0)
    n_all, s_all, m_all = parts[:, :, :C], parts[:, :, C : 2 * C], parts[:, :, 2 * C :]
    total = jnp.sum(n_all, axis=0)
    center = jnp.sum(s_all, axis=0) / total
    apart = s_all / jnp.maximum(n_all, 1.0) - center[None]
    spread = jnp.sum(m_all + n_all * apart * apart, axis=0) / total
    inverse = lax.rsqrt(spread + EPS)
    gain, shift, bias = vec[0:1, :], vec[1:2, :], vec[2:3, :]
    center_w, inverse_w = twice(center), twice(inverse)
    gain_w, shift_w, bias_w = twice(gain), twice(shift), twice(bias)

    chip, chips = la // 2, nla // 2

    def rows_of(k, i):
        return kform[k, pl.ds(pl.multiple_of(i * z.wr, 8), z.wr), :]

    def core_copy(k):
        return remote(ca.at[k], cr.at[k], rc_s.at[k], rc_r.at[k], sibling, lo)

    def core_start(k, acc):
        for a in range(3):
            for b in range(3):
                top, low = (b * 4 + a) * C, (b * 4 + a + 1) * C
                kform[k, pl.ds((3 * a + b) * C, C), :] = (
                    acc[pl.ds(top, C), cols_of(0)] + acc[pl.ds(low, C), cols_of(1)]
                )

        def one(t):
            ca[k, t] = rows_of(k, 2 * t + 1 - core).astype(BF)
        loop(0, chips, one)
        core_copy(k).start()

    def chip_copy(k, t, slot):
        return remote(za.at[k, t], zr.at[k, slot], rz_s.at[k], rz_r.at[k], 2 * t + core, lo)

    def chip_start(k):
        core_copy(k).wait_recv()
        ssum[k] = jnp.zeros_like(ssum[k])
        ssum[k, 0 : z.wr, :] = rows_of(k, la) + cr[k, chip].astype(F32)

        def one(t):
            @pl.when(t != chip)
            def _():
                za[k, t] = (rows_of(k, 2 * t + core) + cr[k, t].astype(F32)).astype(BF)
                chip_copy(k, t, chip).start()
        loop(0, chips, one)

    def lon_copy(k, m):
        return remote(lb.at[k, m], lr.at[k, lo], ro_s.at[k], ro_r.at[k], la, m)

    def lon_start(k):
        received(zr.at[k, pl.ds(0, chips - 1)], rz_r.at[k])

        def one(t):
            @pl.when(t != chip)
            def _():
                ssum[k, 0 : z.wr, :] += zr[k, t].astype(F32)
        loop(0, chips, one)
        ts[k] = ssum[k].T

        def two(m):
            lb[k, m] = ts[k, pl.ds(pl.multiple_of(m * z.wc, z.wc), z.wc), :].astype(BF)
            pl.when(m != lo)(lambda: lon_copy(k, m).start())
        loop(0, nlo, two)

    def lon_finish(k):
        received(lr.at[k, pl.ds(0, nlo - 1)], ro_r.at[k])
        grads[k, 0 : z.wc] = ts[k, pl.ds(pl.multiple_of(lo * z.wc, z.wc), z.wc), :]

        def one(m):
            @pl.when(m != lo)
            def _():
                grads[k, 0 : z.wc] += lr[k, m].astype(F32)
        loop(0, nlo, one)

    def hidden(c):
        def one(j, carry):
            normed = (act[j, chunk(c), :] - center_w) * inverse_w
            H[1 + j, chunk(c), own] = (normed * gain_w + shift_w).astype(BF)
            return carry
        columns(one, 0)
        halo_send(H, 1, c)

    def out_copy(src, dst, ss, rs, c, k):
        m = peer(k)
        return remote(
            src.at[pl.ds(Q * m, Q), chunk(c), :],
            dst.at[:, pl.ds(pl.multiple_of(lo * S + c * CH, CH), CH), :],
            ss.at[0], rs.at[c], la, m,
        )

    def own_out(src, dst, os, c):
        return pltpu.make_async_copy(
            src.at[pl.ds(Q * lo, Q), chunk(c), :],
            dst.at[:, pl.ds(pl.multiple_of(lo * S + c * CH, CH), CH), :],
            os.at[c],
        )

    def send_out(src, dst, ss, rs, os, c):
        loop(1, nlo, lambda k: out_copy(src, dst, ss, rs, c, k).start())
        own_out(src, dst, os, c).start()

    def out_arrived(src, dst, rs, os, c):
        received(dst.at[:, pl.ds(0, CH * (nlo - 1)), :], rs.at[c])
        pltpu.make_async_copy(src.at[pl.ds(0, Q), chunk(0), :], dst.at[:, chunk(0), :], os.at[c]).wait()

    def native_rows(t, c):
        first = pl.multiple_of((t * S + c * CH) * z.PX, CH * z.PX)
        return pl.ds(first, CH * z.PX), pl.ds(pl.multiple_of(t * S + c * CH, CH), CH)

    def finish_block(c):
        out_arrived(bo, ob, bo_r, bo_o, c)

        def one(t):
            rows, here = native_rows(t, c)
            for p in range(z.PX):
                fb[pl.ds(p, CH, stride=z.PX), :] = ob[p % Q, here, cols_of(p // Q)].astype(F32)
            out_low[rows, :] = fb[...].astype(BF)
        loop(0, nlo, one)

    def finish_field(c):
        out_arrived(fs, fo, fo_r, fo_o, c)

        def one(t):
            rows, here = native_rows(t, c)
            fb[...] = cin[rows, :].astype(F32)
            have = pres[here, :]
            for p in range(z.PX):
                pixel = pl.ds(p, CH, stride=z.PX)
                grad = fb[pixel, :] + fo[p % Q, here, cols_of(p // Q)].astype(F32)
                fb[pixel, :] = grad * have[:, p : p + 1] * rstd
            out_grad[rows, :] = fb[...]
        loop(0, nlo, one)

    block_out = (bo, ob, bo_s, bo_r, bo_o)
    field_out = (fs, fo, fo_s, fo_r, fo_o)
    early = min(1, nch - 1)

    def second_chunk(c):
        halo_wait(H, 1, c)
        received(ct.at[pl.ds(0, Q * (nlo - 1)), chunk(c), :], c_r.at[c])
        conv(taps(H, c), w2)

        def one(j, carry):
            value, grad = smooth(pre[j] + bias_w)
            standard = X[1 + j, chunk(c), own].astype(F32)
            bo[j, chunk(c), :] = (standard + value).astype(BF)
            low = (ct[j, chunk(c), :].astype(F32) * grad).astype(BF)
            G[1 + j, chunk(c), own] = low
            return carry + to_eight(low.astype(F32))

        red[0] += columns(one, zero8)
        halo_send(G, 2, c)

    def second_kernel(c):
        grad = G[1 : 1 + L, chunk(c), own].reshape(L * CH, W)
        kernel_grad(taps(H, c), grad, acc2)

    def back_chunk(c):
        halo_wait(G, 2, c)
        conv(taps(G, c), t2)

        def one(j, carry):
            g8, s8 = carry
            value = pre[j]
            sg[j, chunk(c), :] = value
            normed = (act[j, chunk(c), :] - center_w) * inverse_w
            return g8 + to_eight(value * normed), s8 + to_eight(value)

        g8, s8 = columns(one, (zero8, zero8))
        red[1] += g8
        red[2] += s8

    loop(0, nch, hidden)
    def second_step(c):
        second_chunk(c)
        pl.when(c < early)(lambda: send_out(*block_out, c))

    red[...] = jnp.zeros_like(red)
    loop(0, nch, second_step)
    loop(0, nch, second_kernel)
    core_start(SECOND, acc2)
    loop(0, nch, back_chunk)
    sums = [fold(total_row(red[k])) for k in (1, 2, 0)]
    share(y2, 1, jnp.concatenate(sums, axis=1))
    loop(early, nch, lambda c: send_out(*block_out, c))

    chip_start(SECOND)
    sums = jnp.sum(shared(y2, 1), axis=0)
    gain_grad, shift_grad = sums[:, :C], sums[:, C : 2 * C]

    scale_w = twice(inverse * gain)
    shift_part = twice(shift_grad / total)
    gain_part = twice(gain_grad / total)

    def first_grad(c):
        def one(j, carry):
            normed = (act[j, chunk(c), :] - center_w) * inverse_w
            here = cnt[j, chunk(c), :]
            value = sg[j, chunk(c), :] - here * shift_part - here * normed * gain_part
            F[1 + j, chunk(c), own] = (scale_w * value * slope[j, chunk(c), :]).astype(BF)
            return carry
        columns(one, 0)
        halo_send(F, 3, c)

    def first_kernel(c):
        grad = F[1 : 1 + L, chunk(c), own].reshape(L * CH, W)
        kernel_grad(taps(X, c), grad, acc1)

    def field_chunk(c):
        halo_wait(F, 3, c)
        out = jnp.dot(taps(F, c), t1[...], preferred_element_type=F32)
        fs[:, chunk(c), :] = out.astype(BF).reshape(L, CH, W)

    def send_field(c):
        send_out(*field_out, c)

    held = max(nch - 2, 1)
    def field_step(c):
        field_chunk(c)
        pl.when(c < held)(lambda: send_field(c))
        pl.when(c == 1)(lambda: chip_start(FIRST))

    loop(0, nch, first_grad)
    loop(0, nch, first_kernel)
    core_start(FIRST, acc1)
    loop(0, nch, field_step)
    lon_start(SECOND)
    lon_start(FIRST)
    loop(held, nch - 1, send_field)
    loop(0, nch, finish_block)
    lon_finish(SECOND)
    lon_finish(FIRST)
    first_w, second_w = grads[0, 0 : z.wc], grads[1, 0 : z.wc]
    square = total_row(first_w * first_w + second_w * second_w)
    share(y3, 2, sum(square[:, cols_of(t)] for t in range(z.LP // C)))
    loop(max(held, nch - 1), nch, send_field)
    loop(0, nch - 1, finish_field)
    squares = jnp.sum(shared(y3, 2), axis=0)
    mine2 = sum(sums[:, cols_of(t)] * sums[:, cols_of(t)] for t in range(3))
    norm = jnp.sqrt(jnp.sum(squares + mine2, axis=1, keepdims=True))
    for k in range(3):
        grads[0, z.wc + k : z.wc + k + 1, 0:C] = sums[:, cols_of(k)]
    grads[0, z.wc + 3 : z.wc + 4, 0:C] = jnp.broadcast_to(norm, (1, C))

    finish_field(nch - 1)

    sent(sb.at[:, pl.ds(1, nlo - 1)], f_s.at[0])
    sent(cb.at[:, pl.ds(1, nlo - 1)], c_s.at[0])
    sent(wg.at[pl.ds(0, nlo - 1)], wg_s.at[0])
    sent(cm.at[pl.ds(0, nlo - 1)], mask_s.at[0])
    for h, ref in enumerate((X, H, G, F)):
        halo_done(ref, h)
    for k in range(2):
        sent(kg_in.at[k, pl.ds(0, nla // 2 - 1)], kz_s.at[k])
        sent(kg_in.at[k, pl.ds(0, nla // 2)], kc_s.at[k])
        core_copy(k).wait_send()
        sent(zr.at[k, pl.ds(0, chips - 1)], rz_s.at[k])
        sent(lr.at[k, pl.ds(0, nlo - 1)], ro_s.at[k])
    sent(bo.at[pl.ds(0, Q * (nlo - 1))], bo_s.at[0])
    sent(fs.at[pl.ds(0, Q * (nlo - 1))], fo_s.at[0])


def adam_step(master, first, second, grads, rate, decay):
    first_new = BETA_ONE * first + (1.0 - BETA_ONE) * grads
    second_new = BETA_TWO * second + (1.0 - BETA_TWO) * grads * grads
    first_hat = first_new / (1.0 - BETA_ONE**STEP)
    second_hat = second_new / (1.0 - BETA_TWO**STEP)
    master_new = master - rate * (first_hat / (jnp.sqrt(second_hat) + ADAM_EPS) + decay * master)
    return master_new, first_new, second_new


def last_kernel(
    z,
    low, grad, grads, wm_h, wf_h, ws_h, vm_h, vf_h, vs_h,
    block_out, field_grad, norm_h, w_new_h, w_first_h, w_second_h, w_low_h, v_new_h, v_first_h, v_second_h,
    wm, wf, wsec, vm, vf, vs, norm, w_new, w_first, w_second, w_low, v_new, v_first, v_second,
    in_sem, out_sem,
):
    ins = ((wm_h, wm), (wf_h, wf), (ws_h, wsec), (vm_h, vm), (vf_h, vf), (vs_h, vs))
    loads = [pltpu.make_async_copy(src, dst, in_sem.at[i]) for i, (src, dst) in enumerate(ins)]
    for load in loads:
        load.start()
    outs = (
        (grad, field_grad), (low, block_out), (norm, norm_h), (w_new, w_new_h), (w_first, w_first_h),
        (w_second, w_second_h), (w_low, w_low_h), (v_new, v_new_h), (v_first, v_first_h), (v_second, v_second_h),
    )
    stores = [pltpu.make_async_copy(src, dst, out_sem.at[i]) for i, (src, dst) in enumerate(outs)]
    stores[0].start()
    stores[1].start()
    size = grads[0, z.wc + 3 : z.wc + 4, 0:C]
    norm[...] = size[:, 0:1]
    factor = jnp.minimum(1.0, MAX_NORM / size)
    wide = factor[:, 0:1]
    for load in loads:
        load.wait()
    for k in range(2):
        own = grads[k, 0 : z.wc, 0 : z.wr] * wide
        new, first, second = adam_step(wm[k], wf[k], wsec[k], own, RATE_KERNEL, DECAY)
        w_new[k], w_first[k], w_second[k] = new, first, second
        w_low[k] = new.astype(BF)
    for k in range(3):
        own = grads[0, z.wc + k : z.wc + k + 1, 0:C] * factor
        row = slice(k, k + 1)
        new, first, second = adam_step(vm[row, :], vf[row, :], vs[row, :], own, RATE_VECTOR, 0.0)
        v_new[row, :], v_first[row, :], v_second[row, :] = new, first, second
    for store in stores[2:]:
        store.start()
    for store in stores:
        store.wait()


def body(nla, nlo, fields, chan_mean, chan_std, sea_mask, missing, cotangent,
         w_master, w_first, w_second, vec_master, vec_first, vec_second):
    samples, rows, quads, channels = fields.shape
    z = Sizes(nla, nlo, samples, quads, w_master.shape[1], w_master.shape[2])
    S, L, Q, CH, nch, n, B = z.S, z.L, z.Q, z.CH, z.nch, z.n, z.B
    flat = (samples * rows * quads, channels)
    fields = fields.reshape(flat)
    cotangent = cotangent.reshape(flat)
    sea = jnp.transpose(sea_mask, (1, 2, 0))
    miss = jnp.transpose(missing, (1, 2, 0))
    wm, wf, wsec = (jnp.transpose(w, (0, 2, 1)) for w in (w_master, w_first, w_second))
    mean, std = chan_mean.reshape(1, C), chan_std.reshape(1, C)

    vmem = pl.BlockSpec(memory_space=pltpu.VMEM)
    hbm = pl.BlockSpec(memory_space=pl.ANY)
    V = pltpu.VMEM
    dma = pltpu.SemaphoreType.DMA
    shape = jax.ShapeDtypeStruct
    padded = V((L + 2, S, 2 * W), BF)
    wide = V((L, S, W), F32)
    scratch = [
        V((Q, B, W), BF), V((Q, B, W), BF), V(flat, BF), V(flat, BF), V(sea.shape, sea.dtype), V(miss.shape, miss.dtype),
        V((1, C), F32), V((1, C), F32), V(wm.shape, F32), V((3, C), F32),
        V((CH * z.PX, C), F32), V((B, z.PX), F32),
        V((nlo, z.PX, B), F32), wide,
        V((nch, nlo, Q, CH, W), BF), V((nch, nlo, Q, CH, W), BF),
        padded, padded, padded, padded, wide, wide, wide,
        V((L, S, W), BF), V((L, CH, W), F32), V((L, S, W), BF), V((L, S, W), BF), V((3, 8, W), F32),
        V((12 * C, W), BF), V((12 * C, W), BF), V((12 * C, W), BF), V((12 * C, W), BF),
        V((12 * C, W), F32), V((12 * C, W), F32),
        V((2, z.wc, z.LP), BF), V((nlo, 2, z.wc, z.LP), BF), V((2, nla, z.wr, C), BF),
        V((9 * C, C), F32), V((2, z.wr, C), BF),
        V((2, nla // 2, z.wr, C), BF), V((2, nla // 2, z.wr, C), BF),
        V((2, nla // 2, z.wr, C), BF), V((2, nla // 2, z.wr, C), BF), V((2, 9 * C, C), F32),
        V((2, z.LP, C), F32), V((2, C, z.LP), F32), V((2, nlo, z.wc, z.LP), BF), V((2, nlo, z.wc, z.LP), BF),
        V((n, 1, 3 * C), F32), V((n, 1, 3 * C), F32), V((n, 1, C), F32),
        dma((8,)), dma((1,)), dma((1,)), dma((1,)), dma((nch,)), dma((1,)), dma((nch,)),
        dma((4,)), dma((4, nch)),
        dma((1,)), dma((nch,)), dma((nch,)), dma((1,)), dma((nch,)), dma((nch,)), dma((1,)), dma((1,)),
        dma((2,)), dma((2,)), dma((2,)), dma((2,)),
        dma((2,)), dma((2,)), dma((2,)), dma((2,)), dma((2,)), dma((2,)), dma((3,)), dma((3,)),
    ]
    low, grad, grads = pl.pallas_call(
        functools.partial(main_kernel, z),
        out_shape=(V(flat, BF), V(flat, F32), V((2, z.wc + 8, z.LP), F32)),
        in_specs=[hbm] * 8,
        out_specs=(vmem, vmem, vmem),
        scratch_shapes=scratch,
        compiler_params=pltpu.CompilerParams(
            collective_id=0, has_side_effects=True, vmem_limit_bytes=59 * 2**20
        ),
        name="block",
    )(fields, cotangent, sea, miss, mean, std, wm, vec_master)

    shapes = [((1, 1), F32)] + [(wm.shape, F32)] * 3 + [(wm.shape, BF)] + [((3, C), F32)] * 3
    outs = pl.pallas_call(
        functools.partial(last_kernel, z),
        out_shape=[shape(flat, BF), shape(flat, F32)] + [shape(*v) for v in shapes],
        in_specs=[vmem] * 3 + [hbm] * 6,
        out_specs=[hbm] * 10,
        scratch_shapes=[V(wm.shape, F32)] * 3 + [V((3, C), F32)] * 3 + [V(*v) for v in shapes]
        + [dma((6,)), dma((10,))],
        compiler_params=pltpu.CompilerParams(vmem_limit_bytes=16 * 2**20),
        name="update",
    )(low, grad, grads, wm, wf, wsec, vec_master, vec_first, vec_second)
    block_out, field_grad, norm, w_new, w_f, w_s, w_low, v_new, v_f, v_s = outs
    like = (samples, rows, quads, channels)
    w_new, w_f, w_s, w_low = (jnp.transpose(w, (0, 2, 1)) for w in (w_new, w_f, w_s, w_low))
    return (
        block_out.reshape(like), field_grad.reshape(like), norm.reshape(()),
        w_new, w_f, w_s, w_low, v_new, v_f, v_s,
    )


def solution(mesh):
    tile, kernel = P(None, "lat", "lon", None), P(None, "lat", "lon")
    return jax.shard_map(
        functools.partial(body, mesh.shape["lat"], mesh.shape["lon"]),
        mesh=mesh,
        in_specs=(tile, P(), P(), kernel, kernel, tile, kernel, kernel, kernel, P(), P(), P()),
        out_specs=(tile, tile, P(), kernel, kernel, kernel, kernel, P(), P(), P()),
        check_vma=False,
    )
```

```python
import functools

import jax
import jax.numpy as jnp
from jax import lax
from jax.experimental import pallas as pl
from jax.experimental.pallas import tpu as pltpu
from jax.sharding import PartitionSpec as P

STEP = 10
EPS = 1e-05
MAX_NORM = 1.0
BETA_ONE = 0.9
BETA_TWO = 0.999
ADAM_EPS = 1e-08
RATE_KERNEL = 0.02
RATE_VECTOR = 0.1
DECAY = 0.01

MESH = pl.DeviceIdType.MESH
BF = jnp.bfloat16
F32 = jnp.float32
C = 128
R = 2
W = R * C
FIRST, SECOND = 0, 1


def cols_of(i):
    return slice(i * C, (i + 1) * C)


def twice(row):
    return jnp.concatenate([row, row], axis=1)


def fold(row):
    return row[:, :C] + row[:, C:]


def to_eight(block):
    rows, width = block.shape
    return jnp.sum(block.reshape(rows // 8, 8, width), axis=0)


def total_row(block):
    return jnp.sum(block, axis=0, keepdims=True)


def both_masks(missing, sea):
    have = (1 - missing).astype(F32)
    present = jnp.concatenate([have[0], have[1]], axis=0)
    counted = None
    if sea is not None:
        land = have * sea.astype(F32)
        counted = jnp.concatenate([land[0], land[1]], axis=0)
    return present, counted


def smooth(value):
    small = jnp.exp(-jnp.abs(value))
    one = 1.0 + small
    soft = jnp.maximum(value, 0.0) + jnp.log(one)
    sigmoid = jnp.where(value >= 0.0, 1.0, small) / one
    return 0.3 * value + 0.7 * soft, 0.3 + 0.7 * sigmoid


class Sizes:
    def __init__(self, nla, nlo, samples, quads, wrows, wcols):
        self.nla, self.nlo = nla, nlo
        self.n = nla * nlo
        self.B, self.Q = samples, quads
        self.PX = R * quads
        self.S = samples // nlo
        self.L = quads * nlo
        self.CH = self.S // 4 if self.S % 64 == 0 else 16
        self.nch = self.S // self.CH
        self.wr, self.wc = wrows, wcols
        self.LP = -(-wrows // 128) * 128


def main_kernel(
    z,
    fields, cot, sea_h, missing_h, mean_h, std_h, wt_h, vec_h,
    out_low, out_grad, grads,
    ob, fo, fin, cin, sea, missing, mean, std, wt, vec, fb, pres, cmo, cm, cmn, cnt, sb, cb,
    X, H, G, F, act, slope, sg, ct, pre, bo, fs, red,
    p_o, p_h, sg_o, sg_h, act_h, slope_h, cnt_h,
    w1, w2, t1, t2, acc1, acc2,
    ws, wg, kg_in, kf, kl,
    ca, cr, za, zr, kform, ssum, ts, lb, lr,
    y1, y2, y3,
    load_sem, mask_s, mask_r, f_s, f_r, c_s, c_r, halo_s, halo_r,
    bo_s, bo_r, bo_o, fo_s, fo_r, fo_o, wg_s, wg_r, kz_s, kz_r, kc_s, kc_r,
    rc_s, rc_r, rz_s, rz_r, ro_s, ro_r, y_s, y_r, near_s, near_r,
):
    nla, nlo, n = z.nla, z.nlo, z.n
    S, L, Q, CH, nch = z.S, z.L, z.Q, z.CH, z.nch
    la = lax.axis_index("lat")
    lo = lax.axis_index("lon")
    me = la * nlo + lo

    def remote(src, dst, ss, rs, lat_to, lon_to):
        return pltpu.make_async_remote_copy(
            src, dst, ss, rs, device_id=(lat_to, lon_to), device_id_type=MESH
        )

    def received(ref, sem):
        remote(ref, ref, sem, sem, la, lo).wait_recv()

    def sent(ref, sem):
        remote(ref, ref, sem, sem, la, lo).wait_send()

    def loop(low, high, body):
        def step(k, carry):
            body(k)
            return carry
        lax.fori_loop(low, high, step, 0)

    def others(body):
        upper = la // (nla // 2)

        def row(t):
            i = upper * t + (1 - upper) * (nla - 1 - t)

            def one(j):
                @pl.when(jnp.logical_or(i != la, j != lo))
                def _():
                    body(i, j)
            loop(0, nlo, one)
        loop(0, nla, row)

    own = pl.ds(C, W)

    def chunk(c):
        return pl.ds(pl.multiple_of(c * CH, CH), CH)

    def peer(k):
        return lax.rem(lo + k, nlo)

    barrier = pltpu.get_barrier_semaphore()
    others(lambda i, j: pl.semaphore_signal(barrier, inc=1, device_id=(i, j), device_id_type=MESH))
    pairs = (
        (missing_h, missing), (sea_h, sea), (mean_h, mean), (std_h, std), (wt_h, wt), (vec_h, vec),
        (fields, fin), (cot, cin),
    )
    loads = [pltpu.make_async_copy(src, dst, load_sem.at[i]) for i, (src, dst) in enumerate(pairs)]
    for load in loads:
        load.start()
    for load in loads[:-2]:
        load.wait()
    load_f, load_c = loads[-2:]

    present, counted = both_masks(missing[...], sea[...])
    pres[...] = present.T
    width = min(z.B, 128)

    def for_lon(m):
        return pltpu.roll(counted, lax.rem(z.B - m * S, z.B), 1)[:, :width]

    for k in range(1, nlo):
        cmo[k] = for_lon(peer(k))
    cm[lo] = for_lon(lo)
    pad = z.LP - z.wr
    for k in range(2):
        block = wt[k].astype(BF)
        if pad:
            block = jnp.concatenate([block, jnp.zeros((z.wc, pad), BF)], axis=1)
        ws[k] = block
        wg[k, lo] = block
    north_pole, south_pole = la == 0, la == nla - 1
    for side, pole in enumerate((north_pole, south_pole)):
        @pl.when(pole)
        def _():
            for ref in (X, G):
                ref[:, :, cols_of(3 * side)] = jnp.zeros((L + 2, S, C), BF)
            for ref in (p_h, sg_h):
                ref[:, :, cols_of(side)] = jnp.zeros((L, S, C), BF)
            cmn[side] = jnp.zeros_like(cm)

    def w_copy(kind, k):
        return remote(ws.at[kind], wg.at[kind, lo], wg_s.at[kind], wg_r.at[kind], la, peer(k))

    def mask_copy(k):
        return remote(cmo.at[k], cm.at[lo], mask_s.at[0], mask_r.at[0], la, peer(k))

    load_f.wait()

    rstd = 1.0 / std[...]
    center_in = mean[...]

    def place(src, t, c, put, standardize):
        first = pl.multiple_of((t * S + c * CH) * z.PX, CH * z.PX)
        fb[...] = src[pl.ds(first, CH * z.PX), :].astype(F32)
        here = pres[pl.ds(pl.multiple_of(t * S + c * CH, CH), CH), :]
        for p in range(z.PX):
            value = fb[pl.ds(p, CH, stride=z.PX), :]
            if standardize:
                value = (value - center_in) * rstd * here[:, p : p + 1]
            put(p // Q, p % Q, value.astype(BF))

    def f_copy(c, k):
        return remote(
            sb.at[c, k], X.at[pl.ds(1 + Q * lo, Q), chunk(c), own],
            f_s.at[0], f_r.at[c], la, peer(k),
        )

    def c_copy(c, k):
        return remote(
            cb.at[c, k], ct.at[pl.ds(Q * lo, Q), chunk(c), :],
            c_s.at[0], c_r.at[c], la, peer(k),
        )

    def prep_fields(c):
        def one(k):
            def put(i, q, value):
                sb[c, k, q, :, cols_of(i)] = value
            place(fin, peer(k), c, put, True)
        loop(1, nlo, one)

    def send_fields(c):
        loop(1, nlo, lambda k: f_copy(c, k).start())

    def next_fields(c):
        prep_fields(c)
        send_fields(c)

    def own_fields(c):
        def put(i, q, value):
            X[1 + Q * lo + q, chunk(c), cols_of(i + 1)] = value
        place(fin, lo, c, put, True)

    def own_cot(c):
        def put(i, q, value):
            ct[Q * lo + q, chunk(c), cols_of(i)] = value
        place(cin, lo, c, put, False)

    def prep_cot(c):
        def one(k):
            def put(i, q, value):
                cb[c, k, q, :, cols_of(i)] = value
            place(cin, peer(k), c, put, False)
        loop(1, nlo, one)

    prep_fields(0)
    pl.semaphore_wait(barrier, n - 1)
    loop(1, nlo, lambda k: w_copy(FIRST, k).start())
    loop(1, nlo, lambda k: mask_copy(k).start())
    send_fields(0)
    loop(1, nlo, lambda k: w_copy(SECOND, k).start())
    loop(1, nch, next_fields)

    core = lax.rem(la, 2)
    sibling = la + 1 - 2 * core

    def kz_copy(k, d):
        to = lax.rem(la + 2 * d, nla)
        return remote(kl.at[k], kg_in.at[k, la], kz_s.at[k], kz_r.at[k], to, lo)

    def kc_copy(k, d):
        row = lax.rem(la + nla - 2 * d, nla)
        return remote(kg_in.at[k, row], kg_in.at[k, row], kc_s.at[k], kc_r.at[k], sibling, lo)

    def start_kernel(k):
        received(wg.at[k, pl.ds(0, nlo - 1)], wg_r.at[k])
        gathered = jnp.concatenate([wg[k, m].astype(F32) for m in range(nlo)], axis=0)
        kl[k] = gathered.T[: z.wr].astype(BF)
        kg_in[k, la] = kl[k]
        loop(1, nla // 2, lambda d: kz_copy(k, d).start())
        kc_copy(k, 0).start()

    def forward_kernel(k):
        received(kg_in.at[k, pl.ds(0, nla // 2 - 1)], kz_r.at[k])
        loop(1, nla // 2, lambda d: kc_copy(k, d).start())

    def finish_kernel(k):
        received(kg_in.at[k, pl.ds(0, nla // 2)], kc_r.at[k])
        for i in range(nla):
            kf[pl.ds(i * z.wr, z.wr), :] = kg_in[k, i].astype(F32)

    def tap(a, b):
        return kf[pl.ds((3 * a + b) * C, C), :]

    def build_forward(ref):
        for b in range(3):
            for r in range(4):
                for i in range(R):
                    a = r - i
                    good = 0 <= a <= 2
                    block = tap(a, b).astype(BF) if good else jnp.zeros((C, C), BF)
                    ref[pl.ds((b * 4 + r) * C, C), cols_of(i)] = block

    def build_turned(ref):
        for b in range(3):
            for a in range(3):
                block = tap(2 - a, 2 - b).T.astype(BF)
                for i in range(R):
                    ref[pl.ds((b * 4 + a + i) * C, C), cols_of(i)] = block
            for i, r in ((0, 3), (1, 0)):
                ref[pl.ds((b * 4 + r) * C, C), cols_of(i)] = jnp.zeros((C, C), BF)

    start_kernel(FIRST)

    loop(0, nch, own_fields)
    load_c.wait()
    loop(0, nch, own_cot)
    loop(0, nch, prep_cot)
    start_kernel(SECOND)

    def spread_mask():
        mine = jnp.concatenate([cm[m] for m in range(nlo)], axis=0).T
        for j in range(L):
            for i in range(R):
                col = (j // Q) * z.PX + i * Q + j % Q
                cnt[j, :, cols_of(i)] = jnp.broadcast_to(mine[:S, col : col + 1], (S, C))

    def spread_near():
        for side in range(2):
            theirs = jnp.concatenate([cmn[side, m] for m in range(nlo)], axis=0).T
            for j in range(L):
                col = (j // Q) * z.PX + (1 - side) * Q + j % Q
                cnt_h[j, :, cols_of(side)] = jnp.broadcast_to(theirs[:S, col : col + 1], (S, C))

    def near_copy(side):
        to = jnp.maximum(la - 1, 0) if side == 0 else jnp.minimum(la + 1, nla - 1)
        return remote(cm, cmn.at[1 - side], near_s.at[side], near_r.at[side], to, lo)

    def halo_copies(ref, h, c):
        def lanes(r):
            return ref.at[pl.ds(1, L), chunk(c), pl.ds(r * C, C)]

        return pair(lanes(1), lanes(3), lanes(2), lanes(0), h, c)

    def pair(up_from, up_to, down_from, down_to, h, c):
        north = remote(up_from, up_to, halo_s.at[h], halo_r.at[h, c], jnp.maximum(la - 1, 0), lo)
        south = remote(down_from, down_to, halo_s.at[h], halo_r.at[h, c], jnp.minimum(la + 1, nla - 1), lo)
        return north, south

    def edge_send(src, dst, h, c):
        def lanes(ref, side):
            return ref.at[:, chunk(c), pl.ds(side * C, C)]
        north, south = pair(lanes(src, 0), lanes(dst, 1), lanes(src, 1), lanes(dst, 0), h, c)
        pl.when(la > 0)(north.start)
        pl.when(la < nla - 1)(south.start)

    def edge_wait(ref, h, c):
        pl.when(at_pole)(lambda: received(ref.at[:, chunk(c), pl.ds(0, C)], halo_r.at[h, c]))
        pl.when(jnp.logical_not(at_pole))(lambda: received(ref.at[:, chunk(c), :], halo_r.at[h, c]))

    def edge_done(ref, h):
        pl.when(at_pole)(lambda: sent(ref.at[:, :, pl.ds(0, C)], halo_s.at[h]))
        pl.when(jnp.logical_not(at_pole))(lambda: sent(ref, halo_s.at[h]))

    def halo_send(ref, h, c):
        north, south = halo_copies(ref, h, c)
        pl.when(la > 0)(north.start)
        pl.when(la < nla - 1)(south.start)

    at_pole = jnp.logical_or(north_pole, south_pole)

    def halo_wait(ref, h, c):
        def both(width):
            received(ref.at[pl.ds(1, L), chunk(c), pl.ds(0, width)], halo_r.at[h, c])
        pl.when(at_pole)(lambda: both(C))
        pl.when(jnp.logical_not(at_pole))(lambda: both(W))
        wrap(ref, c)

    def wrap(ref, c):
        ref[0, chunk(c), :] = ref[L, chunk(c), :]
        ref[L + 1, chunk(c), :] = ref[1, chunk(c), :]

    def halo_done(ref, h):
        def both(width):
            sent(ref.at[pl.ds(1, L), :, pl.ds(0, width)], halo_s.at[h])
        pl.when(at_pole)(lambda: both(C))
        pl.when(jnp.logical_not(at_pole))(lambda: both(W))

    def taps(ref, c):
        parts = [ref[b : b + L, chunk(c), :].reshape(L * CH, 4 * C) for b in range(3)]
        return jnp.concatenate(parts, axis=1)

    def conv(lhs, kernel):
        out = jnp.dot(lhs, kernel[...], preferred_element_type=F32)
        pre[...] = out.reshape(L, CH, W)

    def kernel_grad(lhs, grad, acc):
        acc[...] += lax.dot_general(
            lhs, grad, (((0,), (0,)), ((), ())), preferred_element_type=F32
        )

    def columns(body, carry):
        return lax.fori_loop(0, L, body, carry, unroll=min(L, 16))

    zero8 = jnp.zeros((8, W), F32)

    def arrive(c):
        received(X.at[pl.ds(1, Q * (nlo - 1)), chunk(c), own], f_r.at[c])
        halo_send(X, 0, c)

    def first_chunk(c, stats):
        halo_wait(X, 0, c)
        conv(taps(X, c), w1)

        def one(j, carry):
            s, m = carry
            p_o[j, chunk(c), :] = pre[j].astype(BF)
            value, grad = smooth(pre[j])
            act[j, chunk(c), :] = value
            slope[j, chunk(c), :] = grad
            here = cnt[j, chunk(c), :]
            return s + to_eight(here * value), m + to_eight(here)

        s8, n8 = columns(one, (zero8, zero8))
        s_c, n_c = fold(total_row(s8)), fold(total_row(n8))
        mean_c = s_c / jnp.maximum(n_c, 1.0)
        mean_w = twice(mean_c)

        def two(j, m2):
            off = act[j, chunk(c), :] - mean_w
            return m2 + to_eight(cnt[j, chunk(c), :] * off * off)

        m_c = fold(total_row(columns(two, zero8)))
        n_0, s_0, m_0 = stats
        delta = mean_c - s_0 / jnp.maximum(n_0, 1.0)
        n_1 = n_0 + n_c
        m_1 = m_0 + m_c + delta * delta * (n_0 * n_c / jnp.maximum(n_1, 1.0))
        return n_1, s_0 + s_c, m_1

    def first_edge(c):
        edge_wait(p_h, 1, c)

        def one(j, carry):
            act_h[j, chunk(c), :], slope_h[j, chunk(c), :] = smooth(p_h[j, chunk(c), :].astype(F32))
            return carry
        columns(one, 0)

    def send_cot(c):
        loop(1, nlo, lambda k: c_copy(c, k).start())

    arrive(0)
    forward_kernel(FIRST)
    received(cm.at[pl.ds(0, nlo - 1)], mask_r.at[0])
    for side, pole in enumerate((north_pole, south_pole)):
        pl.when(jnp.logical_not(pole))(lambda: near_copy(side).start())
    spread_mask()
    finish_kernel(FIRST)
    build_forward(w1)
    build_turned(t1)
    zero1 = jnp.zeros((1, C), F32)

    def first_step(c, stats):
        pl.when(c + 1 < nch)(lambda: arrive(c + 1))
        pl.when(c + 2 == nch)(lambda: send_cot(0))
        return first_chunk(c, stats)

    n_d, s_d, m_d = lax.fori_loop(0, nch, first_step, (zero1, zero1, zero1))

    def share(buf, which, value):
        buf[me] = value
        others(lambda i, j: remote(buf.at[me], buf.at[me], y_s.at[which], y_r.at[which], i, j).start())

    def shared(buf, which):
        block = remote(buf.at[pl.ds(0, n - 1)], buf.at[pl.ds(0, n - 1)], y_s.at[which], y_r.at[which], la, lo)
        block.wait_recv()
        block.wait_send()
        return buf[...]

    share(y1, 0, jnp.concatenate([n_d, s_d, m_d], axis=1))
    loop(0, nch, lambda c: edge_send(p_o, p_h, 1, c))
    loop(1, nch, send_cot)
    for side, pole in enumerate((south_pole, north_pole)):
        pl.when(jnp.logical_not(pole))(lambda: near_copy(side).wait_recv())
    forward_kernel(SECOND)
    spread_near()
    finish_kernel(SECOND)
    build_forward(w2)
    build_turned(t2)
    acc1[...] = jnp.zeros_like(acc1)
    acc2[...] = jnp.zeros_like(acc2)

    parts = shared(y1, 0)
    n_all, s_all, m_all = parts[:, :, :C], parts[:, :, C : 2 * C], parts[:, :, 2 * C :]
    total = jnp.sum(n_all, axis=0)
    center = jnp.sum(s_all, axis=0) / total
    apart = s_all / jnp.maximum(n_all, 1.0) - center[None]
    spread = jnp.sum(m_all + n_all * apart * apart, axis=0) / total
    inverse = lax.rsqrt(spread + EPS)
    gain, shift, bias = vec[0:1, :], vec[1:2, :], vec[2:3, :]
    center_w, inverse_w = twice(center), twice(inverse)
    gain_w, shift_w, bias_w = twice(gain), twice(shift), twice(bias)
    inside = [jnp.where(pole, 0.0, 1.0) for pole in (north_pole, south_pole)]

    def edges(row):
        return jnp.concatenate([row * inside[0], row * inside[1]], axis=1)

    gain_h, shift_h = edges(gain), edges(shift)

    def put_edges(ref, j, c, value):
        low = value.astype(BF)
        ref[1 + j, chunk(c), cols_of(0)], ref[1 + j, chunk(c), cols_of(3)] = low[:, :C], low[:, C:]

    chip, chips = la // 2, nla // 2

    def rows_of(k, i):
        return kform[k, pl.ds(pl.multiple_of(i * z.wr, 8), z.wr), :]

    def core_copy(k):
        return remote(ca.at[k], cr.at[k], rc_s.at[k], rc_r.at[k], sibling, lo)

    def core_start(k, acc):
        for a in range(3):
            for b in range(3):
                top, low = (b * 4 + a) * C, (b * 4 + a + 1) * C
                kform[k, pl.ds((3 * a + b) * C, C), :] = (
                    acc[pl.ds(top, C), cols_of(0)] + acc[pl.ds(low, C), cols_of(1)]
                )

        def one(t):
            ca[k, t] = rows_of(k, 2 * t + 1 - core).astype(BF)
        loop(0, chips, one)
        core_copy(k).start()

    def chip_copy(k, t, slot):
        return remote(za.at[k, t], zr.at[k, slot], rz_s.at[k], rz_r.at[k], 2 * t + core, lo)

    def chip_start(k):
        core_copy(k).wait_recv()
        ssum[k] = jnp.zeros_like(ssum[k])
        ssum[k, 0 : z.wr, :] = rows_of(k, la) + cr[k, chip].astype(F32)

        def one(t):
            @pl.when(t != chip)
            def _():
                za[k, t] = (rows_of(k, 2 * t + core) + cr[k, t].astype(F32)).astype(BF)
                chip_copy(k, t, chip).start()
        loop(0, chips, one)

    def lon_copy(k, m):
        return remote(lb.at[k, m], lr.at[k, lo], ro_s.at[k], ro_r.at[k], la, m)

    def lon_start(k):
        received(zr.at[k, pl.ds(0, chips - 1)], rz_r.at[k])

        def one(t):
            @pl.when(t != chip)
            def _():
                ssum[k, 0 : z.wr, :] += zr[k, t].astype(F32)
        loop(0, chips, one)
        ts[k] = ssum[k].T

        def two(m):
            lb[k, m] = ts[k, pl.ds(pl.multiple_of(m * z.wc, z.wc), z.wc), :].astype(BF)
            pl.when(m != lo)(lambda: lon_copy(k, m).start())
        loop(0, nlo, two)

    def lon_finish(k):
        received(lr.at[k, pl.ds(0, nlo - 1)], ro_r.at[k])
        grads[k, 0 : z.wc] = ts[k, pl.ds(pl.multiple_of(lo * z.wc, z.wc), z.wc), :]

        def one(m):
            @pl.when(m != lo)
            def _():
                grads[k, 0 : z.wc] += lr[k, m].astype(F32)
        loop(0, nlo, one)

    def hidden(c):
        def one(j, carry):
            normed = (act[j, chunk(c), :] - center_w) * inverse_w
            H[1 + j, chunk(c), own] = (normed * gain_w + shift_w).astype(BF)
            normed = (act_h[j, chunk(c), :] - center_w) * inverse_w
            put_edges(H, j, c, normed * gain_h + shift_h)
            return carry
        columns(one, 0)
        wrap(H, c)

    def out_copy(src, dst, ss, rs, c, k):
        m = peer(k)
        return remote(
            src.at[pl.ds(Q * m, Q), chunk(c), :],
            dst.at[:, pl.ds(pl.multiple_of(lo * S + c * CH, CH), CH), :],
            ss.at[0], rs.at[c], la, m,
        )

    def own_out(src, dst, os, c):
        return pltpu.make_async_copy(
            src.at[pl.ds(Q * lo, Q), chunk(c), :],
            dst.at[:, pl.ds(pl.multiple_of(lo * S + c * CH, CH), CH), :],
            os.at[c],
        )

    def send_out(src, dst, ss, rs, os, c):
        loop(1, nlo, lambda k: out_copy(src, dst, ss, rs, c, k).start())
        own_out(src, dst, os, c).start()

    def out_arrived(src, dst, rs, os, c):
        received(dst.at[:, pl.ds(0, CH * (nlo - 1)), :], rs.at[c])
        pltpu.make_async_copy(src.at[pl.ds(0, Q), chunk(0), :], dst.at[:, chunk(0), :], os.at[c]).wait()

    def native_rows(t, c):
        first = pl.multiple_of((t * S + c * CH) * z.PX, CH * z.PX)
        return pl.ds(first, CH * z.PX), pl.ds(pl.multiple_of(t * S + c * CH, CH), CH)

    def finish_block(c):
        out_arrived(bo, ob, bo_r, bo_o, c)

        def one(t):
            rows, here = native_rows(t, c)
            for p in range(z.PX):
                fb[pl.ds(p, CH, stride=z.PX), :] = ob[p % Q, here, cols_of(p // Q)].astype(F32)
            out_low[rows, :] = fb[...].astype(BF)
        loop(0, nlo, one)

    def finish_field(c):
        out_arrived(fs, fo, fo_r, fo_o, c)

        def one(t):
            rows, here = native_rows(t, c)
            fb[...] = cin[rows, :].astype(F32)
            have = pres[here, :]
            for p in range(z.PX):
                pixel = pl.ds(p, CH, stride=z.PX)
                grad = fb[pixel, :] + fo[p % Q, here, cols_of(p // Q)].astype(F32)
                fb[pixel, :] = grad * have[:, p : p + 1] * rstd
            out_grad[rows, :] = fb[...]
        loop(0, nlo, one)

    block_out = (bo, ob, bo_s, bo_r, bo_o)
    field_out = (fs, fo, fo_s, fo_r, fo_o)
    early = min(1, nch - 1)

    def second_chunk(c):
        first_edge(c)
        hidden(c)
        received(ct.at[pl.ds(0, Q * (nlo - 1)), chunk(c), :], c_r.at[c])
        conv(taps(H, c), w2)

        def one(j, carry):
            value, grad = smooth(pre[j] + bias_w)
            standard = X[1 + j, chunk(c), own].astype(F32)
            bo[j, chunk(c), :] = (standard + value).astype(BF)
            low = (ct[j, chunk(c), :].astype(F32) * grad).astype(BF)
            G[1 + j, chunk(c), own] = low
            return carry + to_eight(low.astype(F32))

        red[0] += columns(one, zero8)
        halo_send(G, 2, c)

    def second_kernel(c):
        grad = G[1 : 1 + L, chunk(c), own].reshape(L * CH, W)
        kernel_grad(taps(H, c), grad, acc2)

    def back_chunk(c):
        halo_wait(G, 2, c)
        conv(taps(G, c), t2)

        def one(j, carry):
            g8, s8 = carry
            value = pre[j]
            sg[j, chunk(c), :] = value
            sg_o[j, chunk(c), :] = value.astype(BF)
            normed = (act[j, chunk(c), :] - center_w) * inverse_w
            return g8 + to_eight(value * normed), s8 + to_eight(value)

        g8, s8 = columns(one, (zero8, zero8))
        red[1] += g8
        red[2] += s8

    def second_step(c):
        second_chunk(c)
        pl.when(c < early)(lambda: send_out(*block_out, c))

    red[...] = jnp.zeros_like(red)
    loop(0, nch, second_step)
    loop(0, nch, second_kernel)
    core_start(SECOND, acc2)
    loop(0, nch, back_chunk)
    sums = [fold(total_row(red[k])) for k in (1, 2, 0)]
    share(y2, 1, jnp.concatenate(sums, axis=1))
    loop(0, nch, lambda c: edge_send(sg_o, sg_h, 3, c))
    loop(early, nch, lambda c: send_out(*block_out, c))

    chip_start(SECOND)
    sums = jnp.sum(shared(y2, 1), axis=0)
    gain_grad, shift_grad = sums[:, :C], sums[:, C : 2 * C]

    scale_w = twice(inverse * gain)
    shift_part = twice(shift_grad / total)
    gain_part = twice(gain_grad / total)

    scale_h = edges(inverse * gain)

    def act_grad(value, activation, here):
        normed = (activation - center_w) * inverse_w
        return value - here * shift_part - here * normed * gain_part

    def first_grad(c):
        def one(j, carry):
            grad = act_grad(sg[j, chunk(c), :], act[j, chunk(c), :], cnt[j, chunk(c), :])
            F[1 + j, chunk(c), own] = (scale_w * grad * slope[j, chunk(c), :]).astype(BF)
            return carry
        columns(one, 0)

    def first_grad_edge(c):
        edge_wait(sg_h, 3, c)

        def one(j, carry):
            theirs = sg_h[j, chunk(c), :].astype(F32)
            grad = act_grad(theirs, act_h[j, chunk(c), :], cnt_h[j, chunk(c), :])
            put_edges(F, j, c, scale_h * grad * slope_h[j, chunk(c), :])
            return carry
        columns(one, 0)
        wrap(F, c)

    def first_kernel(c):
        grad = F[1 : 1 + L, chunk(c), own].reshape(L * CH, W)
        kernel_grad(taps(X, c), grad, acc1)

    def field_chunk(c):
        first_grad_edge(c)
        out = jnp.dot(taps(F, c), t1[...], preferred_element_type=F32)
        fs[:, chunk(c), :] = out.astype(BF).reshape(L, CH, W)

    def send_field(c):
        send_out(*field_out, c)

    held = max(nch - 2, 1)
    def field_step(c):
        field_chunk(c)
        pl.when(c < held)(lambda: send_field(c))
        pl.when(c == 1)(lambda: chip_start(FIRST))

    loop(0, nch, first_grad)
    loop(0, nch, first_kernel)
    core_start(FIRST, acc1)
    loop(0, nch, field_step)
    lon_start(SECOND)
    lon_start(FIRST)
    loop(held, nch - 1, send_field)
    loop(0, nch, finish_block)
    lon_finish(SECOND)
    lon_finish(FIRST)
    first_w, second_w = grads[0, 0 : z.wc], grads[1, 0 : z.wc]
    square = total_row(first_w * first_w + second_w * second_w)
    share(y3, 2, sum(square[:, cols_of(t)] for t in range(z.LP // C)))
    loop(max(held, nch - 1), nch, send_field)
    loop(0, nch - 1, finish_field)
    squares = jnp.sum(shared(y3, 2), axis=0)
    mine2 = sum(sums[:, cols_of(t)] * sums[:, cols_of(t)] for t in range(3))
    norm = jnp.sqrt(jnp.sum(squares + mine2, axis=1, keepdims=True))
    for k in range(3):
        grads[0, z.wc + k : z.wc + k + 1, 0:C] = sums[:, cols_of(k)]
    grads[0, z.wc + 3 : z.wc + 4, 0:C] = jnp.broadcast_to(norm, (1, C))

    finish_field(nch - 1)

    sent(sb.at[:, pl.ds(1, nlo - 1)], f_s.at[0])
    sent(cb.at[:, pl.ds(1, nlo - 1)], c_s.at[0])
    sent(cm.at[pl.ds(0, nlo - 1)], mask_s.at[0])
    halo_done(X, 0)
    edge_done(p_o, 1)
    halo_done(G, 2)
    edge_done(sg_o, 3)
    for side, pole in enumerate((north_pole, south_pole)):
        pl.when(jnp.logical_not(pole))(lambda: near_copy(side).wait_send())
    for k in range(2):
        sent(wg.at[k, pl.ds(0, nlo - 1)], wg_s.at[k])
        sent(kg_in.at[k, pl.ds(0, nla // 2 - 1)], kz_s.at[k])
        sent(kg_in.at[k, pl.ds(0, nla // 2)], kc_s.at[k])
        core_copy(k).wait_send()
        sent(zr.at[k, pl.ds(0, chips - 1)], rz_s.at[k])
        sent(lr.at[k, pl.ds(0, nlo - 1)], ro_s.at[k])
    sent(bo.at[pl.ds(0, Q * (nlo - 1))], bo_s.at[0])
    sent(fs.at[pl.ds(0, Q * (nlo - 1))], fo_s.at[0])


def adam_step(master, first, second, grads, rate, decay):
    first_new = BETA_ONE * first + (1.0 - BETA_ONE) * grads
    second_new = BETA_TWO * second + (1.0 - BETA_TWO) * grads * grads
    first_hat = first_new / (1.0 - BETA_ONE**STEP)
    second_hat = second_new / (1.0 - BETA_TWO**STEP)
    master_new = master - rate * (first_hat / (jnp.sqrt(second_hat) + ADAM_EPS) + decay * master)
    return master_new, first_new, second_new


def last_kernel(
    z,
    low, grad, grads, wm_h, wf_h, ws_h, vm_h, vf_h, vs_h,
    block_out, field_grad, norm_h, w_new_h, w_first_h, w_second_h, w_low_h, v_new_h, v_first_h, v_second_h,
    wm, wf, wsec, vm, vf, vs, norm, w_new, w_first, w_second, w_low, v_new, v_first, v_second,
    in_sem, out_sem,
):
    ins = ((wm_h, wm), (wf_h, wf), (ws_h, wsec), (vm_h, vm), (vf_h, vf), (vs_h, vs))
    loads = [pltpu.make_async_copy(src, dst, in_sem.at[i]) for i, (src, dst) in enumerate(ins)]
    for load in loads:
        load.start()
    outs = (
        (grad, field_grad), (low, block_out), (norm, norm_h), (w_new, w_new_h), (w_first, w_first_h),
        (w_second, w_second_h), (w_low, w_low_h), (v_new, v_new_h), (v_first, v_first_h), (v_second, v_second_h),
    )
    stores = [pltpu.make_async_copy(src, dst, out_sem.at[i]) for i, (src, dst) in enumerate(outs)]
    stores[0].start()
    stores[1].start()
    size = grads[0, z.wc + 3 : z.wc + 4, 0:C]
    norm[...] = size[:, 0:1]
    factor = jnp.minimum(1.0, MAX_NORM / size)
    wide = factor[:, 0:1]
    for load in loads:
        load.wait()
    for k in range(2):
        own = grads[k, 0 : z.wc, 0 : z.wr] * wide
        new, first, second = adam_step(wm[k], wf[k], wsec[k], own, RATE_KERNEL, DECAY)
        w_new[k], w_first[k], w_second[k] = new, first, second
        w_low[k] = new.astype(BF)
    for k in range(3):
        own = grads[0, z.wc + k : z.wc + k + 1, 0:C] * factor
        row = slice(k, k + 1)
        new, first, second = adam_step(vm[row, :], vf[row, :], vs[row, :], own, RATE_VECTOR, 0.0)
        v_new[row, :], v_first[row, :], v_second[row, :] = new, first, second
    for store in stores[2:]:
        store.start()
    for store in stores:
        store.wait()


def body(nla, nlo, fields, chan_mean, chan_std, sea_mask, missing, cotangent,
         w_master, w_first, w_second, vec_master, vec_first, vec_second):
    samples, rows, quads, channels = fields.shape
    z = Sizes(nla, nlo, samples, quads, w_master.shape[1], w_master.shape[2])
    S, L, Q, CH, nch, n, B = z.S, z.L, z.Q, z.CH, z.nch, z.n, z.B
    flat = (samples * rows * quads, channels)
    fields = fields.reshape(flat)
    cotangent = cotangent.reshape(flat)
    sea = jnp.transpose(sea_mask, (1, 2, 0))
    miss = jnp.transpose(missing, (1, 2, 0))
    wm, wf, wsec = (jnp.transpose(w, (0, 2, 1)) for w in (w_master, w_first, w_second))
    mean, std = chan_mean.reshape(1, C), chan_std.reshape(1, C)

    vmem = pl.BlockSpec(memory_space=pltpu.VMEM)
    hbm = pl.BlockSpec(memory_space=pl.ANY)
    V = pltpu.VMEM
    dma = pltpu.SemaphoreType.DMA
    shape = jax.ShapeDtypeStruct
    padded = V((L + 2, S, 2 * W), BF)
    wide = V((L, S, W), F32)
    scratch = [
        V((Q, B, W), BF), V((Q, B, W), BF), V(flat, BF), V(flat, BF), V(sea.shape, sea.dtype), V(miss.shape, miss.dtype),
        V((1, C), F32), V((1, C), F32), V(wm.shape, F32), V((3, C), F32),
        V((CH * z.PX, C), F32), V((B, z.PX), F32),
        V((nlo, z.PX, min(B, 128)), F32), V((nlo, z.PX, min(B, 128)), F32),
        V((2, nlo, z.PX, min(B, 128)), F32), wide,
        V((nch, nlo, Q, CH, W), BF), V((nch, nlo, Q, CH, W), BF),
        padded, padded, padded, padded, wide, wide, wide,
        V((L, S, W), BF), V((L, CH, W), F32), V((L, S, W), BF), V((L, S, W), BF), V((3, 8, W), F32),
        V((L, S, W), BF), V((L, S, W), BF), V((L, S, W), BF), V((L, S, W), BF), wide, wide, wide,
        V((12 * C, W), BF), V((12 * C, W), BF), V((12 * C, W), BF), V((12 * C, W), BF),
        V((12 * C, W), F32), V((12 * C, W), F32),
        V((2, z.wc, z.LP), BF), V((2, nlo, z.wc, z.LP), BF), V((2, nla, z.wr, C), BF),
        V((9 * C, C), F32), V((2, z.wr, C), BF),
        V((2, nla // 2, z.wr, C), BF), V((2, nla // 2, z.wr, C), BF),
        V((2, nla // 2, z.wr, C), BF), V((2, nla // 2, z.wr, C), BF), V((2, 9 * C, C), F32),
        V((2, z.LP, C), F32), V((2, C, z.LP), F32), V((2, nlo, z.wc, z.LP), BF), V((2, nlo, z.wc, z.LP), BF),
        V((n, 1, 3 * C), F32), V((n, 1, 3 * C), F32), V((n, 1, C), F32),
        dma((8,)), dma((1,)), dma((1,)), dma((1,)), dma((nch,)), dma((1,)), dma((nch,)),
        dma((4,)), dma((4, nch)),
        dma((1,)), dma((nch,)), dma((nch,)), dma((1,)), dma((nch,)), dma((nch,)), dma((2,)), dma((2,)),
        dma((2,)), dma((2,)), dma((2,)), dma((2,)),
        dma((2,)), dma((2,)), dma((2,)), dma((2,)), dma((2,)), dma((2,)), dma((3,)), dma((3,)),
        dma((2,)), dma((2,)),
    ]
    low, grad, grads = pl.pallas_call(
        functools.partial(main_kernel, z),
        out_shape=(V(flat, BF), V(flat, F32), V((2, z.wc + 8, z.LP), F32)),
        in_specs=[hbm] * 8,
        out_specs=(vmem, vmem, vmem),
        scratch_shapes=scratch,
        compiler_params=pltpu.CompilerParams(
            collective_id=0, has_side_effects=True, vmem_limit_bytes=59 * 2**20
        ),
        name="block",
    )(fields, cotangent, sea, miss, mean, std, wm, vec_master)

    shapes = [((1, 1), F32)] + [(wm.shape, F32)] * 3 + [(wm.shape, BF)] + [((3, C), F32)] * 3
    outs = pl.pallas_call(
        functools.partial(last_kernel, z),
        out_shape=[shape(flat, BF), shape(flat, F32)] + [shape(*v) for v in shapes],
        in_specs=[vmem] * 3 + [hbm] * 6,
        out_specs=[hbm] * 10,
        scratch_shapes=[V(wm.shape, F32)] * 3 + [V((3, C), F32)] * 3 + [V(*v) for v in shapes]
        + [dma((6,)), dma((10,))],
        compiler_params=pltpu.CompilerParams(vmem_limit_bytes=16 * 2**20),
        name="update",
    )(low, grad, grads, wm, wf, wsec, vec_master, vec_first, vec_second)
    block_out, field_grad, norm, w_new, w_f, w_s, w_low, v_new, v_f, v_s = outs
    like = (samples, rows, quads, channels)
    w_new, w_f, w_s, w_low = (jnp.transpose(w, (0, 2, 1)) for w in (w_new, w_f, w_s, w_low))
    return (
        block_out.reshape(like), field_grad.reshape(like), norm.reshape(()),
        w_new, w_f, w_s, w_low, v_new, v_f, v_s,
    )


def solution(mesh):
    tile, kernel = P(None, "lat", "lon", None), P(None, "lat", "lon")
    return jax.shard_map(
        functools.partial(body, mesh.shape["lat"], mesh.shape["lon"]),
        mesh=mesh,
        in_specs=(tile, P(), P(), kernel, kernel, tile, kernel, kernel, kernel, P(), P(), P()),
        out_specs=(tile, tile, P(), kernel, kernel, kernel, kernel, P(), P(), P()),
        check_vma=False,
    )
```

```python
import functools

import jax
import jax.numpy as jnp
from jax import lax
from jax.experimental import pallas as pl
from jax.experimental.pallas import tpu as pltpu
from jax.sharding import PartitionSpec as P

STEP = 10
EPS = 1e-05
MAX_NORM = 1.0
BETA_ONE = 0.9
BETA_TWO = 0.999
ADAM_EPS = 1e-08
RATE_KERNEL = 0.02
RATE_VECTOR = 0.1
DECAY = 0.01

MESH = pl.DeviceIdType.MESH
BF = jnp.bfloat16
F32 = jnp.float32
C = 128
R = 2
W = R * C
FIRST, SECOND = 0, 1


def cols_of(i):
    return slice(i * C, (i + 1) * C)


def twice(row):
    return jnp.concatenate([row, row], axis=1)


def fold(row):
    return row[:, :C] + row[:, C:]


def to_eight(block):
    rows, width = block.shape
    return jnp.sum(block.reshape(rows // 8, 8, width), axis=0)


def total_row(block):
    return jnp.sum(block, axis=0, keepdims=True)


def both_masks(missing, sea):
    have = (1 - missing).astype(F32)
    present = jnp.concatenate([have[0], have[1]], axis=0)
    counted = None
    if sea is not None:
        land = have * sea.astype(F32)
        counted = jnp.concatenate([land[0], land[1]], axis=0)
    return present, counted


def smooth(value):
    high = 0.5 + 0.5 * jnp.tanh(0.5 * jnp.abs(value))
    soft = jnp.maximum(value, 0.0) - jnp.log(high)
    sigmoid = jnp.where(value >= 0.0, high, 1.0 - high)
    return 0.3 * value + 0.7 * soft, 0.3 + 0.7 * sigmoid


class Sizes:
    def __init__(self, nla, nlo, samples, quads, wrows, wcols):
        self.nla, self.nlo = nla, nlo
        self.n = nla * nlo
        self.B, self.Q = samples, quads
        self.PX = R * quads
        self.S = samples // nlo
        self.L = quads * nlo
        self.CH = self.S // 4 if self.S % 64 == 0 else 16
        self.nch = self.S // self.CH
        self.wr, self.wc = wrows, wcols
        self.LP = -(-wrows // 128) * 128


def main_kernel(
    z,
    fields, cot, sea_h, missing_h, mean_h, std_h, wt_h, vec_h,
    out_low, out_grad, grads,
    ob, fo, fin, cin, sea, missing, mean, std, wt, vec, fb, pres, cmo, cm, cmn, cnt, sb, cb,
    X, H, G, F, act, slope, sg, ct, pre, bo, fs, red,
    p_o, p_h, sg_o, sg_h, act_h, slope_h, cnt_h,
    w1, w2, t1, t2, acc1, acc2,
    ws, wg, kg_in, kf, kl,
    ca, cr, za, zr, kform, ssum, ts, lb, lr,
    y1, y2, y3,
    load_sem, mask_s, mask_r, f_s, f_r, c_s, c_r, halo_s, halo_r,
    bo_s, bo_r, bo_o, fo_s, fo_r, fo_o, wg_s, wg_r, kz_s, kz_r, kc_s, kc_r,
    rc_s, rc_r, rz_s, rz_r, ro_s, ro_r, y_s, y_r, near_s, near_r,
):
    nla, nlo, n = z.nla, z.nlo, z.n
    S, L, Q, CH, nch = z.S, z.L, z.Q, z.CH, z.nch
    la = lax.axis_index("lat")
    lo = lax.axis_index("lon")
    me = la * nlo + lo

    def remote(src, dst, ss, rs, lat_to, lon_to):
        return pltpu.make_async_remote_copy(
            src, dst, ss, rs, device_id=(lat_to, lon_to), device_id_type=MESH
        )

    def received(ref, sem):
        remote(ref, ref, sem, sem, la, lo).wait_recv()

    def sent(ref, sem):
        remote(ref, ref, sem, sem, la, lo).wait_send()

    def loop(low, high, body):
        def step(k, carry):
            body(k)
            return carry
        lax.fori_loop(low, high, step, 0)

    def others(body):
        upper = la // (nla // 2)

        def row(t):
            i = upper * t + (1 - upper) * (nla - 1 - t)

            def one(j):
                @pl.when(jnp.logical_or(i != la, j != lo))
                def _():
                    body(i, j)
            loop(0, nlo, one)
        loop(0, nla, row)

    own = pl.ds(C, W)

    def chunk(c):
        return pl.ds(pl.multiple_of(c * CH, CH), CH)

    def peer(k):
        return lax.rem(lo + k, nlo)

    barrier = pltpu.get_barrier_semaphore()
    others(lambda i, j: pl.semaphore_signal(barrier, inc=1, device_id=(i, j), device_id_type=MESH))
    pairs = (
        (missing_h, missing), (sea_h, sea), (mean_h, mean), (std_h, std), (wt_h, wt), (vec_h, vec),
        (fields, fin), (cot, cin),
    )
    loads = [pltpu.make_async_copy(src, dst, load_sem.at[i]) for i, (src, dst) in enumerate(pairs)]
    for load in loads:
        load.start()
    for load in loads[:-2]:
        load.wait()
    load_f, load_c = loads[-2:]

    present, counted = both_masks(missing[...], sea[...])
    pres[...] = present.T
    width = min(z.B, 128)

    def for_lon(m):
        return pltpu.roll(counted, lax.rem(z.B - m * S, z.B), 1)[:, :width]

    for k in range(1, nlo):
        cmo[k] = for_lon(peer(k))
    cm[lo] = for_lon(lo)
    pad = z.LP - z.wr
    for k in range(2):
        block = wt[k].astype(BF)
        if pad:
            block = jnp.concatenate([block, jnp.zeros((z.wc, pad), BF)], axis=1)
        ws[k] = block
        wg[k, lo] = block
    north_pole, south_pole = la == 0, la == nla - 1
    for side, pole in enumerate((north_pole, south_pole)):
        @pl.when(pole)
        def _():
            for ref in (X, G):
                ref[:, :, cols_of(3 * side)] = jnp.zeros((L + 2, S, C), BF)
            for ref in (p_h, sg_h):
                ref[:, :, cols_of(side)] = jnp.zeros((L, S, C), BF)
            cmn[side] = jnp.zeros_like(cm)

    def w_copy(kind, k):
        return remote(ws.at[kind], wg.at[kind, lo], wg_s.at[kind], wg_r.at[kind], la, peer(k))

    def mask_copy(k):
        return remote(cmo.at[k], cm.at[lo], mask_s.at[0], mask_r.at[0], la, peer(k))

    load_f.wait()

    rstd = 1.0 / std[...]
    center_in = mean[...]

    def place(src, t, c, put, standardize):
        first = pl.multiple_of((t * S + c * CH) * z.PX, CH * z.PX)
        fb[...] = src[pl.ds(first, CH * z.PX), :].astype(F32)
        here = pres[pl.ds(pl.multiple_of(t * S + c * CH, CH), CH), :]
        for p in range(z.PX):
            value = fb[pl.ds(p, CH, stride=z.PX), :]
            if standardize:
                value = (value - center_in) * rstd * here[:, p : p + 1]
            put(p // Q, p % Q, value.astype(BF))

    def f_copy(c, k):
        return remote(
            sb.at[c, k], X.at[pl.ds(1 + Q * lo, Q), chunk(c), own],
            f_s.at[0], f_r.at[c], la, peer(k),
        )

    def c_copy(c, k):
        return remote(
            cb.at[c, k], ct.at[pl.ds(Q * lo, Q), chunk(c), :],
            c_s.at[0], c_r.at[c], la, peer(k),
        )

    def prep_fields(c):
        def one(k):
            def put(i, q, value):
                sb[c, k, q, :, cols_of(i)] = value
            place(fin, peer(k), c, put, True)
        loop(1, nlo, one)

    def send_fields(c):
        loop(1, nlo, lambda k: f_copy(c, k).start())

    def next_fields(c):
        prep_fields(c)
        send_fields(c)

    def own_fields(c):
        def put(i, q, value):
            X[1 + Q * lo + q, chunk(c), cols_of(i + 1)] = value
        place(fin, lo, c, put, True)

    def own_cot(c):
        def put(i, q, value):
            ct[Q * lo + q, chunk(c), cols_of(i)] = value
        place(cin, lo, c, put, False)

    def prep_cot(c):
        def one(k):
            def put(i, q, value):
                cb[c, k, q, :, cols_of(i)] = value
            place(cin, peer(k), c, put, False)
        loop(1, nlo, one)

    prep_fields(0)
    pl.semaphore_wait(barrier, n - 1)
    loop(1, nlo, lambda k: w_copy(FIRST, k).start())
    loop(1, nlo, lambda k: mask_copy(k).start())
    send_fields(0)
    loop(1, nlo, lambda k: w_copy(SECOND, k).start())
    loop(1, nch, next_fields)

    core = lax.rem(la, 2)
    sibling = la + 1 - 2 * core

    def kz_copy(k, d):
        to = lax.rem(la + 2 * d, nla)
        return remote(kl.at[k], kg_in.at[k, la], kz_s.at[k], kz_r.at[k], to, lo)

    def kc_copy(k, d):
        row = lax.rem(la + nla - 2 * d, nla)
        return remote(kg_in.at[k, row], kg_in.at[k, row], kc_s.at[k], kc_r.at[k], sibling, lo)

    def start_kernel(k):
        received(wg.at[k, pl.ds(0, nlo - 1)], wg_r.at[k])
        gathered = jnp.concatenate([wg[k, m].astype(F32) for m in range(nlo)], axis=0)
        kl[k] = gathered.T[: z.wr].astype(BF)
        kg_in[k, la] = kl[k]
        loop(1, nla // 2, lambda d: kz_copy(k, d).start())
        kc_copy(k, 0).start()

    def forward_kernel(k):
        received(kg_in.at[k, pl.ds(0, nla // 2 - 1)], kz_r.at[k])
        loop(1, nla // 2, lambda d: kc_copy(k, d).start())

    def finish_kernel(k):
        received(kg_in.at[k, pl.ds(0, nla // 2)], kc_r.at[k])
        for i in range(nla):
            kf[pl.ds(i * z.wr, z.wr), :] = kg_in[k, i].astype(F32)

    def tap(a, b):
        return kf[pl.ds((3 * a + b) * C, C), :]

    def build_forward(ref):
        for b in range(3):
            for r in range(4):
                for i in range(R):
                    a = r - i
                    good = 0 <= a <= 2
                    block = tap(a, b).astype(BF) if good else jnp.zeros((C, C), BF)
                    ref[pl.ds((b * 4 + r) * C, C), cols_of(i)] = block

    def build_turned(ref):
        for b in range(3):
            for a in range(3):
                block = tap(2 - a, 2 - b).T.astype(BF)
                for i in range(R):
                    ref[pl.ds((b * 4 + a + i) * C, C), cols_of(i)] = block
            for i, r in ((0, 3), (1, 0)):
                ref[pl.ds((b * 4 + r) * C, C), cols_of(i)] = jnp.zeros((C, C), BF)

    start_kernel(FIRST)

    loop(0, nch, own_fields)
    load_c.wait()
    loop(0, nch, own_cot)
    loop(0, nch, prep_cot)
    start_kernel(SECOND)

    def spread_mask():
        mine = jnp.concatenate([cm[m] for m in range(nlo)], axis=0).T
        for j in range(L):
            for i in range(R):
                col = (j // Q) * z.PX + i * Q + j % Q
                cnt[j, :, cols_of(i)] = jnp.broadcast_to(mine[:S, col : col + 1], (S, C))

    def spread_near():
        for side in range(2):
            theirs = jnp.concatenate([cmn[side, m] for m in range(nlo)], axis=0).T
            for j in range(L):
                col = (j // Q) * z.PX + (1 - side) * Q + j % Q
                cnt_h[j, :, cols_of(side)] = jnp.broadcast_to(theirs[:S, col : col + 1], (S, C))

    def near_copy(side):
        to = jnp.maximum(la - 1, 0) if side == 0 else jnp.minimum(la + 1, nla - 1)
        return remote(cm, cmn.at[1 - side], near_s.at[side], near_r.at[side], to, lo)

    def halo_copies(ref, h, c):
        def lanes(r):
            return ref.at[pl.ds(1, L), chunk(c), pl.ds(r * C, C)]

        return pair(lanes(1), lanes(3), lanes(2), lanes(0), h, c)

    def pair(up_from, up_to, down_from, down_to, h, c):
        north = remote(up_from, up_to, halo_s.at[h], halo_r.at[h, c], jnp.maximum(la - 1, 0), lo)
        south = remote(down_from, down_to, halo_s.at[h], halo_r.at[h, c], jnp.minimum(la + 1, nla - 1), lo)
        return north, south

    def edge_send(src, dst, h, c):
        def lanes(ref, side):
            return ref.at[:, chunk(c), pl.ds(side * C, C)]
        north, south = pair(lanes(src, 0), lanes(dst, 1), lanes(src, 1), lanes(dst, 0), h, c)
        pl.when(la > 0)(north.start)
        pl.when(la < nla - 1)(south.start)

    def edge_wait(ref, h, c):
        pl.when(at_pole)(lambda: received(ref.at[:, chunk(c), pl.ds(0, C)], halo_r.at[h, c]))
        pl.when(jnp.logical_not(at_pole))(lambda: received(ref.at[:, chunk(c), :], halo_r.at[h, c]))

    def edge_done(ref, h):
        pl.when(at_pole)(lambda: sent(ref.at[:, :, pl.ds(0, C)], halo_s.at[h]))
        pl.when(jnp.logical_not(at_pole))(lambda: sent(ref, halo_s.at[h]))

    def halo_send(ref, h, c):
        north, south = halo_copies(ref, h, c)
        pl.when(la > 0)(north.start)
        pl.when(la < nla - 1)(south.start)

    at_pole = jnp.logical_or(north_pole, south_pole)

    def halo_wait(ref, h, c):
        def both(width):
            received(ref.at[pl.ds(1, L), chunk(c), pl.ds(0, width)], halo_r.at[h, c])
        pl.when(at_pole)(lambda: both(C))
        pl.when(jnp.logical_not(at_pole))(lambda: both(W))
        wrap(ref, c)

    def wrap(ref, c):
        ref[0, chunk(c), :] = ref[L, chunk(c), :]
        ref[L + 1, chunk(c), :] = ref[1, chunk(c), :]

    def halo_done(ref, h):
        def both(width):
            sent(ref.at[pl.ds(1, L), :, pl.ds(0, width)], halo_s.at[h])
        pl.when(at_pole)(lambda: both(C))
        pl.when(jnp.logical_not(at_pole))(lambda: both(W))

    def taps(ref, c):
        parts = [ref[b : b + L, chunk(c), :].reshape(L * CH, 4 * C) for b in range(3)]
        return jnp.concatenate(parts, axis=1)

    def conv(lhs, kernel):
        out = jnp.dot(lhs, kernel[...], preferred_element_type=F32)
        pre[...] = out.reshape(L, CH, W)

    def kernel_grad(lhs, grad, acc):
        acc[...] += lax.dot_general(
            lhs, grad, (((0,), (0,)), ((), ())), preferred_element_type=F32
        )

    def columns(body, carry):
        return lax.fori_loop(0, L, body, carry, unroll=min(L, 16))

    zero8 = jnp.zeros((8, W), F32)

    def arrive(c):
        received(X.at[pl.ds(1, Q * (nlo - 1)), chunk(c), own], f_r.at[c])
        halo_send(X, 0, c)

    def first_chunk(c, stats):
        halo_wait(X, 0, c)
        conv(taps(X, c), w1)

        def one(j, carry):
            s, m = carry
            p_o[j, chunk(c), :] = pre[j].astype(BF)
            value, grad = smooth(pre[j])
            act[j, chunk(c), :] = value
            slope[j, chunk(c), :] = grad
            here = cnt[j, chunk(c), :]
            return s + to_eight(here * value), m + to_eight(here)

        s8, n8 = columns(one, (zero8, zero8))
        s_c, n_c = fold(total_row(s8)), fold(total_row(n8))
        mean_c = s_c / jnp.maximum(n_c, 1.0)
        mean_w = twice(mean_c)

        def two(j, m2):
            off = act[j, chunk(c), :] - mean_w
            return m2 + to_eight(cnt[j, chunk(c), :] * off * off)

        m_c = fold(total_row(columns(two, zero8)))
        n_0, s_0, m_0 = stats
        delta = mean_c - s_0 / jnp.maximum(n_0, 1.0)
        n_1 = n_0 + n_c
        m_1 = m_0 + m_c + delta * delta * (n_0 * n_c / jnp.maximum(n_1, 1.0))
        return n_1, s_0 + s_c, m_1

    def first_edge(c):
        edge_wait(p_h, 1, c)

        def one(j, carry):
            act_h[j, chunk(c), :], slope_h[j, chunk(c), :] = smooth(p_h[j, chunk(c), :].astype(F32))
            return carry
        columns(one, 0)

    def send_cot(c):
        loop(1, nlo, lambda k: c_copy(c, k).start())

    arrive(0)
    forward_kernel(FIRST)
    received(cm.at[pl.ds(0, nlo - 1)], mask_r.at[0])
    for side, pole in enumerate((north_pole, south_pole)):
        pl.when(jnp.logical_not(pole))(lambda: near_copy(side).start())
    spread_mask()
    finish_kernel(FIRST)
    build_forward(w1)
    build_turned(t1)
    zero1 = jnp.zeros((1, C), F32)

    def first_step(c, stats):
        pl.when(c + 1 < nch)(lambda: arrive(c + 1))
        pl.when(c + 2 == nch)(lambda: loop(0, 2, send_cot))
        return first_chunk(c, stats)

    n_d, s_d, m_d = lax.fori_loop(0, nch, first_step, (zero1, zero1, zero1))

    def share(buf, which, value):
        buf[me] = value
        others(lambda i, j: remote(buf.at[me], buf.at[me], y_s.at[which], y_r.at[which], i, j).start())

    def shared(buf, which):
        block = remote(buf.at[pl.ds(0, n - 1)], buf.at[pl.ds(0, n - 1)], y_s.at[which], y_r.at[which], la, lo)
        block.wait_recv()
        block.wait_send()
        return buf[...]

    share(y1, 0, jnp.concatenate([n_d, s_d, m_d], axis=1))
    loop(0, nch, lambda c: edge_send(p_o, p_h, 1, c))
    loop(2, nch, send_cot)
    for side, pole in enumerate((south_pole, north_pole)):
        pl.when(jnp.logical_not(pole))(lambda: near_copy(side).wait_recv())
    forward_kernel(SECOND)
    spread_near()
    finish_kernel(SECOND)
    build_forward(w2)
    build_turned(t2)
    acc1[...] = jnp.zeros_like(acc1)
    acc2[...] = jnp.zeros_like(acc2)

    parts = shared(y1, 0)
    n_all, s_all, m_all = parts[:, :, :C], parts[:, :, C : 2 * C], parts[:, :, 2 * C :]
    total = jnp.sum(n_all, axis=0)
    center = jnp.sum(s_all, axis=0) / total
    apart = s_all / jnp.maximum(n_all, 1.0) - center[None]
    spread = jnp.sum(m_all + n_all * apart * apart, axis=0) / total
    inverse = lax.rsqrt(spread + EPS)
    gain, shift, bias = vec[0:1, :], vec[1:2, :], vec[2:3, :]
    center_w, inverse_w = twice(center), twice(inverse)
    gain_w, shift_w, bias_w = twice(gain), twice(shift), twice(bias)
    inside = [jnp.where(pole, 0.0, 1.0) for pole in (north_pole, south_pole)]

    def edges(row):
        return jnp.concatenate([row * inside[0], row * inside[1]], axis=1)

    gain_h, shift_h = edges(gain), edges(shift)

    def put_edges(ref, j, c, value):
        low = value.astype(BF)
        ref[1 + j, chunk(c), cols_of(0)], ref[1 + j, chunk(c), cols_of(3)] = low[:, :C], low[:, C:]

    chip, chips = la // 2, nla // 2

    def rows_of(k, i):
        return kform[k, pl.ds(pl.multiple_of(i * z.wr, 8), z.wr), :]

    def core_copy(k):
        return remote(ca.at[k], cr.at[k], rc_s.at[k], rc_r.at[k], sibling, lo)

    def core_start(k, acc):
        for a in range(3):
            for b in range(3):
                top, low = (b * 4 + a) * C, (b * 4 + a + 1) * C
                kform[k, pl.ds((3 * a + b) * C, C), :] = (
                    acc[pl.ds(top, C), cols_of(0)] + acc[pl.ds(low, C), cols_of(1)]
                )

        def one(t):
            ca[k, t] = rows_of(k, 2 * t + 1 - core).astype(BF)
        loop(0, chips, one)
        core_copy(k).start()

    def chip_copy(k, t, slot):
        return remote(za.at[k, t], zr.at[k, slot], rz_s.at[k], rz_r.at[k], 2 * t + core, lo)

    def chip_start(k):
        core_copy(k).wait_recv()
        ssum[k] = jnp.zeros_like(ssum[k])
        ssum[k, 0 : z.wr, :] = rows_of(k, la) + cr[k, chip].astype(F32)

        def one(t):
            @pl.when(t != chip)
            def _():
                za[k, t] = (rows_of(k, 2 * t + core) + cr[k, t].astype(F32)).astype(BF)
                chip_copy(k, t, chip).start()
        loop(0, chips, one)

    def lon_copy(k, m):
        return remote(lb.at[k, m], lr.at[k, lo], ro_s.at[k], ro_r.at[k], la, m)

    def lon_start(k):
        received(zr.at[k, pl.ds(0, chips - 1)], rz_r.at[k])

        def one(t):
            @pl.when(t != chip)
            def _():
                ssum[k, 0 : z.wr, :] += zr[k, t].astype(F32)
        loop(0, chips, one)
        ts[k] = ssum[k].T

        def two(m):
            lb[k, m] = ts[k, pl.ds(pl.multiple_of(m * z.wc, z.wc), z.wc), :].astype(BF)
            pl.when(m != lo)(lambda: lon_copy(k, m).start())
        loop(0, nlo, two)

    def lon_finish(k):
        received(lr.at[k, pl.ds(0, nlo - 1)], ro_r.at[k])
        grads[k, 0 : z.wc] = ts[k, pl.ds(pl.multiple_of(lo * z.wc, z.wc), z.wc), :]

        def one(m):
            @pl.when(m != lo)
            def _():
                grads[k, 0 : z.wc] += lr[k, m].astype(F32)
        loop(0, nlo, one)

    def hidden(c):
        def one(j, carry):
            normed = (act[j, chunk(c), :] - center_w) * inverse_w
            H[1 + j, chunk(c), own] = (normed * gain_w + shift_w).astype(BF)
            normed = (act_h[j, chunk(c), :] - center_w) * inverse_w
            put_edges(H, j, c, normed * gain_h + shift_h)
            return carry
        columns(one, 0)
        wrap(H, c)

    def out_copy(src, dst, ss, rs, c, k):
        m = peer(k)
        return remote(
            src.at[pl.ds(Q * m, Q), chunk(c), :],
            dst.at[:, pl.ds(pl.multiple_of(lo * S + c * CH, CH), CH), :],
            ss.at[0], rs.at[c], la, m,
        )

    def own_out(src, dst, os, c):
        return pltpu.make_async_copy(
            src.at[pl.ds(Q * lo, Q), chunk(c), :],
            dst.at[:, pl.ds(pl.multiple_of(lo * S + c * CH, CH), CH), :],
            os.at[c],
        )

    def send_out(src, dst, ss, rs, os, c):
        loop(1, nlo, lambda k: out_copy(src, dst, ss, rs, c, k).start())
        own_out(src, dst, os, c).start()

    def out_arrived(src, dst, rs, os, c):
        received(dst.at[:, pl.ds(0, CH * (nlo - 1)), :], rs.at[c])
        pltpu.make_async_copy(src.at[pl.ds(0, Q), chunk(0), :], dst.at[:, chunk(0), :], os.at[c]).wait()

    def native_rows(t, c):
        first = pl.multiple_of((t * S + c * CH) * z.PX, CH * z.PX)
        return pl.ds(first, CH * z.PX), pl.ds(pl.multiple_of(t * S + c * CH, CH), CH)

    def finish_block(c):
        out_arrived(bo, ob, bo_r, bo_o, c)

        def one(t):
            rows, here = native_rows(t, c)
            for p in range(z.PX):
                fb[pl.ds(p, CH, stride=z.PX), :] = ob[p % Q, here, cols_of(p // Q)].astype(F32)
            out_low[rows, :] = fb[...].astype(BF)
        loop(0, nlo, one)

    def finish_field(c):
        out_arrived(fs, fo, fo_r, fo_o, c)

        def one(t):
            rows, here = native_rows(t, c)
            fb[...] = cin[rows, :].astype(F32)
            have = pres[here, :]
            for p in range(z.PX):
                pixel = pl.ds(p, CH, stride=z.PX)
                grad = fb[pixel, :] + fo[p % Q, here, cols_of(p // Q)].astype(F32)
                fb[pixel, :] = grad * have[:, p : p + 1] * rstd
            out_grad[rows, :] = fb[...]
        loop(0, nlo, one)

    block_out = (bo, ob, bo_s, bo_r, bo_o)
    field_out = (fs, fo, fo_s, fo_r, fo_o)
    early = 2

    def second_chunk(c):
        first_edge(c)
        hidden(c)
        received(ct.at[pl.ds(0, Q * (nlo - 1)), chunk(c), :], c_r.at[c])
        conv(taps(H, c), w2)

        def one(j, carry):
            value, grad = smooth(pre[j] + bias_w)
            standard = X[1 + j, chunk(c), own].astype(F32)
            bo[j, chunk(c), :] = (standard + value).astype(BF)
            low = (ct[j, chunk(c), :].astype(F32) * grad).astype(BF)
            G[1 + j, chunk(c), own] = low
            return carry + to_eight(low.astype(F32))

        red[0] += columns(one, zero8)
        halo_send(G, 2, c)

    def second_kernel(c):
        grad = G[1 : 1 + L, chunk(c), own].reshape(L * CH, W)
        kernel_grad(taps(H, c), grad, acc2)

    def back_chunk(c):
        halo_wait(G, 2, c)
        conv(taps(G, c), t2)

        def one(j, carry):
            g8, s8 = carry
            value = pre[j]
            sg[j, chunk(c), :] = value
            sg_o[j, chunk(c), :] = value.astype(BF)
            normed = (act[j, chunk(c), :] - center_w) * inverse_w
            return g8 + to_eight(value * normed), s8 + to_eight(value)

        g8, s8 = columns(one, (zero8, zero8))
        red[1] += g8
        red[2] += s8

    def second_step(c):
        second_chunk(c)
        pl.when(c < early)(lambda: send_out(*block_out, c))

    red[...] = jnp.zeros_like(red)
    loop(0, nch, second_step)
    loop(0, nch, second_kernel)
    core_start(SECOND, acc2)
    loop(0, nch, back_chunk)
    sums = [fold(total_row(red[k])) for k in (1, 2, 0)]
    share(y2, 1, jnp.concatenate(sums, axis=1))
    loop(0, nch, lambda c: edge_send(sg_o, sg_h, 3, c))
    loop(early, nch, lambda c: send_out(*block_out, c))

    chip_start(SECOND)
    sums = jnp.sum(shared(y2, 1), axis=0)
    gain_grad, shift_grad = sums[:, :C], sums[:, C : 2 * C]

    scale_w = twice(inverse * gain)
    shift_part = twice(shift_grad / total)
    gain_part = twice(gain_grad / total)

    scale_h = edges(inverse * gain)

    def act_grad(value, activation, here):
        normed = (activation - center_w) * inverse_w
        return value - here * shift_part - here * normed * gain_part

    def first_grad(c):
        def one(j, carry):
            grad = act_grad(sg[j, chunk(c), :], act[j, chunk(c), :], cnt[j, chunk(c), :])
            F[1 + j, chunk(c), own] = (scale_w * grad * slope[j, chunk(c), :]).astype(BF)
            return carry
        columns(one, 0)

    def first_grad_edge(c):
        edge_wait(sg_h, 3, c)

        def one(j, carry):
            theirs = sg_h[j, chunk(c), :].astype(F32)
            grad = act_grad(theirs, act_h[j, chunk(c), :], cnt_h[j, chunk(c), :])
            put_edges(F, j, c, scale_h * grad * slope_h[j, chunk(c), :])
            return carry
        columns(one, 0)
        wrap(F, c)

    def first_kernel(c):
        grad = F[1 : 1 + L, chunk(c), own].reshape(L * CH, W)
        kernel_grad(taps(X, c), grad, acc1)

    def field_chunk(c):
        first_grad_edge(c)
        out = jnp.dot(taps(F, c), t1[...], preferred_element_type=F32)
        fs[:, chunk(c), :] = out.astype(BF).reshape(L, CH, W)

    def send_field(c):
        send_out(*field_out, c)

    held = max(nch - 2, 1)
    def field_step(c):
        field_chunk(c)
        pl.when(c < held)(lambda: send_field(c))
        pl.when(c == 1)(lambda: chip_start(FIRST))

    loop(0, nch, first_grad)
    loop(0, nch, first_kernel)
    core_start(FIRST, acc1)
    loop(0, nch, field_step)
    lon_start(SECOND)
    lon_start(FIRST)
    loop(held, nch - 1, send_field)
    loop(0, nch, finish_block)
    lon_finish(SECOND)
    lon_finish(FIRST)
    first_w, second_w = grads[0, 0 : z.wc], grads[1, 0 : z.wc]
    square = total_row(first_w * first_w + second_w * second_w)
    share(y3, 2, sum(square[:, cols_of(t)] for t in range(z.LP // C)))
    loop(max(held, nch - 1), nch, send_field)
    loop(0, nch - 1, finish_field)
    squares = jnp.sum(shared(y3, 2), axis=0)
    mine2 = sum(sums[:, cols_of(t)] * sums[:, cols_of(t)] for t in range(3))
    norm = jnp.sqrt(jnp.sum(squares + mine2, axis=1, keepdims=True))
    for k in range(3):
        grads[0, z.wc + k : z.wc + k + 1, 0:C] = sums[:, cols_of(k)]
    grads[0, z.wc + 3 : z.wc + 4, 0:C] = jnp.broadcast_to(norm, (1, C))

    finish_field(nch - 1)

    sent(sb.at[:, pl.ds(1, nlo - 1)], f_s.at[0])
    sent(cb.at[:, pl.ds(1, nlo - 1)], c_s.at[0])
    sent(cm.at[pl.ds(0, nlo - 1)], mask_s.at[0])
    halo_done(X, 0)
    edge_done(p_o, 1)
    halo_done(G, 2)
    edge_done(sg_o, 3)
    for side, pole in enumerate((north_pole, south_pole)):
        pl.when(jnp.logical_not(pole))(lambda: near_copy(side).wait_send())
    for k in range(2):
        sent(wg.at[k, pl.ds(0, nlo - 1)], wg_s.at[k])
        sent(kg_in.at[k, pl.ds(0, nla // 2 - 1)], kz_s.at[k])
        sent(kg_in.at[k, pl.ds(0, nla // 2)], kc_s.at[k])
        core_copy(k).wait_send()
        sent(zr.at[k, pl.ds(0, chips - 1)], rz_s.at[k])
        sent(lr.at[k, pl.ds(0, nlo - 1)], ro_s.at[k])
    sent(bo.at[pl.ds(0, Q * (nlo - 1))], bo_s.at[0])
    sent(fs.at[pl.ds(0, Q * (nlo - 1))], fo_s.at[0])


def adam_step(master, first, second, grads, rate, decay):
    first_new = BETA_ONE * first + (1.0 - BETA_ONE) * grads
    second_new = BETA_TWO * second + (1.0 - BETA_TWO) * grads * grads
    first_hat = first_new / (1.0 - BETA_ONE**STEP)
    second_hat = second_new / (1.0 - BETA_TWO**STEP)
    master_new = master - rate * (first_hat / (jnp.sqrt(second_hat) + ADAM_EPS) + decay * master)
    return master_new, first_new, second_new


def last_kernel(
    z,
    low, grad, grads, wm_h, wf_h, ws_h, vm_h, vf_h, vs_h,
    block_out, field_grad, norm_h, w_new_h, w_first_h, w_second_h, w_low_h, v_new_h, v_first_h, v_second_h,
    wm, wf, wsec, vm, vf, vs, norm, w_new, w_first, w_second, w_low, v_new, v_first, v_second,
    in_sem, out_sem,
):
    ins = ((wm_h, wm), (wf_h, wf), (ws_h, wsec), (vm_h, vm), (vf_h, vf), (vs_h, vs))
    loads = [pltpu.make_async_copy(src, dst, in_sem.at[i]) for i, (src, dst) in enumerate(ins)]
    for load in loads:
        load.start()
    outs = (
        (grad, field_grad), (low, block_out), (norm, norm_h), (w_new, w_new_h), (w_first, w_first_h),
        (w_second, w_second_h), (w_low, w_low_h), (v_new, v_new_h), (v_first, v_first_h), (v_second, v_second_h),
    )
    stores = [pltpu.make_async_copy(src, dst, out_sem.at[i]) for i, (src, dst) in enumerate(outs)]
    stores[0].start()
    stores[1].start()
    size = grads[0, z.wc + 3 : z.wc + 4, 0:C]
    norm[...] = size[:, 0:1]
    factor = jnp.minimum(1.0, MAX_NORM / size)
    wide = factor[:, 0:1]
    for load in loads:
        load.wait()
    for k in range(2):
        own = grads[k, 0 : z.wc, 0 : z.wr] * wide
        new, first, second = adam_step(wm[k], wf[k], wsec[k], own, RATE_KERNEL, DECAY)
        w_new[k], w_first[k], w_second[k] = new, first, second
        w_low[k] = new.astype(BF)
    for k in range(3):
        own = grads[0, z.wc + k : z.wc + k + 1, 0:C] * factor
        row = slice(k, k + 1)
        new, first, second = adam_step(vm[row, :], vf[row, :], vs[row, :], own, RATE_VECTOR, 0.0)
        v_new[row, :], v_first[row, :], v_second[row, :] = new, first, second
    for store in stores[2:]:
        store.start()
    for store in stores:
        store.wait()


def body(nla, nlo, fields, chan_mean, chan_std, sea_mask, missing, cotangent,
         w_master, w_first, w_second, vec_master, vec_first, vec_second):
    samples, rows, quads, channels = fields.shape
    z = Sizes(nla, nlo, samples, quads, w_master.shape[1], w_master.shape[2])
    S, L, Q, CH, nch, n, B = z.S, z.L, z.Q, z.CH, z.nch, z.n, z.B
    flat = (samples * rows * quads, channels)
    fields = fields.reshape(flat)
    cotangent = cotangent.reshape(flat)
    sea = jnp.transpose(sea_mask, (1, 2, 0))
    miss = jnp.transpose(missing, (1, 2, 0))
    wm, wf, wsec = (jnp.transpose(w, (0, 2, 1)) for w in (w_master, w_first, w_second))
    mean, std = chan_mean.reshape(1, C), chan_std.reshape(1, C)

    vmem = pl.BlockSpec(memory_space=pltpu.VMEM)
    hbm = pl.BlockSpec(memory_space=pl.ANY)
    V = pltpu.VMEM
    dma = pltpu.SemaphoreType.DMA
    shape = jax.ShapeDtypeStruct
    padded = V((L + 2, S, 2 * W), BF)
    wide = V((L, S, W), F32)
    scratch = [
        V((Q, B, W), BF), V((Q, B, W), BF), V(flat, BF), V(flat, BF), V(sea.shape, sea.dtype), V(miss.shape, miss.dtype),
        V((1, C), F32), V((1, C), F32), V(wm.shape, F32), V((3, C), F32),
        V((CH * z.PX, C), F32), V((B, z.PX), F32),
        V((nlo, z.PX, min(B, 128)), F32), V((nlo, z.PX, min(B, 128)), F32),
        V((2, nlo, z.PX, min(B, 128)), F32), wide,
        V((nch, nlo, Q, CH, W), BF), V((nch, nlo, Q, CH, W), BF),
        padded, padded, padded, padded, wide, wide, wide,
        V((L, S, W), BF), V((L, CH, W), F32), V((L, S, W), BF), V((L, S, W), BF), V((3, 8, W), F32),
        V((L, S, W), BF), V((L, S, W), BF), V((L, S, W), BF), V((L, S, W), BF), wide, wide, wide,
        V((12 * C, W), BF), V((12 * C, W), BF), V((12 * C, W), BF), V((12 * C, W), BF),
        V((12 * C, W), F32), V((12 * C, W), F32),
        V((2, z.wc, z.LP), BF), V((2, nlo, z.wc, z.LP), BF), V((2, nla, z.wr, C), BF),
        V((9 * C, C), F32), V((2, z.wr, C), BF),
        V((2, nla // 2, z.wr, C), BF), V((2, nla // 2, z.wr, C), BF),
        V((2, nla // 2, z.wr, C), BF), V((2, nla // 2, z.wr, C), BF), V((2, 9 * C, C), F32),
        V((2, z.LP, C), F32), V((2, C, z.LP), F32), V((2, nlo, z.wc, z.LP), BF), V((2, nlo, z.wc, z.LP), BF),
        V((n, 1, 3 * C), F32), V((n, 1, 3 * C), F32), V((n, 1, C), F32),
        dma((8,)), dma((1,)), dma((1,)), dma((1,)), dma((nch,)), dma((1,)), dma((nch,)),
        dma((4,)), dma((4, nch)),
        dma((1,)), dma((nch,)), dma((nch,)), dma((1,)), dma((nch,)), dma((nch,)), dma((2,)), dma((2,)),
        dma((2,)), dma((2,)), dma((2,)), dma((2,)),
        dma((2,)), dma((2,)), dma((2,)), dma((2,)), dma((2,)), dma((2,)), dma((3,)), dma((3,)),
        dma((2,)), dma((2,)),
    ]
    low, grad, grads = pl.pallas_call(
        functools.partial(main_kernel, z),
        out_shape=(V(flat, BF), V(flat, F32), V((2, z.wc + 8, z.LP), F32)),
        in_specs=[hbm] * 8,
        out_specs=(vmem, vmem, vmem),
        scratch_shapes=scratch,
        compiler_params=pltpu.CompilerParams(
            collective_id=0, has_side_effects=True, vmem_limit_bytes=59 * 2**20
        ),
        name="block",
    )(fields, cotangent, sea, miss, mean, std, wm, vec_master)

    shapes = [((1, 1), F32)] + [(wm.shape, F32)] * 3 + [(wm.shape, BF)] + [((3, C), F32)] * 3
    outs = pl.pallas_call(
        functools.partial(last_kernel, z),
        out_shape=[shape(flat, BF), shape(flat, F32)] + [shape(*v) for v in shapes],
        in_specs=[vmem] * 3 + [hbm] * 6,
        out_specs=[hbm] * 10,
        scratch_shapes=[V(wm.shape, F32)] * 3 + [V((3, C), F32)] * 3 + [V(*v) for v in shapes]
        + [dma((6,)), dma((10,))],
        compiler_params=pltpu.CompilerParams(vmem_limit_bytes=16 * 2**20),
        name="update",
    )(low, grad, grads, wm, wf, wsec, vec_master, vec_first, vec_second)
    block_out, field_grad, norm, w_new, w_f, w_s, w_low, v_new, v_f, v_s = outs
    like = (samples, rows, quads, channels)
    w_new, w_f, w_s, w_low = (jnp.transpose(w, (0, 2, 1)) for w in (w_new, w_f, w_s, w_low))
    return (
        block_out.reshape(like), field_grad.reshape(like), norm.reshape(()),
        w_new, w_f, w_s, w_low, v_new, v_f, v_s,
    )


def solution(mesh):
    tile, kernel = P(None, "lat", "lon", None), P(None, "lat", "lon")
    return jax.shard_map(
        functools.partial(body, mesh.shape["lat"], mesh.shape["lon"]),
        mesh=mesh,
        in_specs=(tile, P(), P(), kernel, kernel, tile, kernel, kernel, kernel, P(), P(), P()),
        out_specs=(tile, tile, P(), kernel, kernel, kernel, kernel, P(), P(), P()),
        check_vma=False,
    )
```

```python
import functools

import jax
import jax.numpy as jnp
from jax import lax
from jax.experimental import pallas as pl
from jax.experimental.pallas import tpu as pltpu
from jax.sharding import PartitionSpec as P

STEP = 10
EPS = 1e-05
MAX_NORM = 1.0
BETA_ONE = 0.9
BETA_TWO = 0.999
ADAM_EPS = 1e-08
RATE_KERNEL = 0.02
RATE_VECTOR = 0.1
DECAY = 0.01

MESH = pl.DeviceIdType.MESH
BF = jnp.bfloat16
F32 = jnp.float32
C = 128
R = 2
W = R * C
FIRST, SECOND = 0, 1


def cols_of(i):
    return slice(i * C, (i + 1) * C)


def twice(row):
    return jnp.concatenate([row, row], axis=1)


def fold(row):
    return row[:, :C] + row[:, C:]


def to_eight(block):
    rows, width = block.shape
    return jnp.sum(block.reshape(rows // 8, 8, width), axis=0)


def total_row(block):
    return jnp.sum(block, axis=0, keepdims=True)


def both_masks(missing, sea):
    have = (1 - missing).astype(F32)
    present = jnp.concatenate([have[0], have[1]], axis=0)
    counted = None
    if sea is not None:
        land = have * sea.astype(F32)
        counted = jnp.concatenate([land[0], land[1]], axis=0)
    return present, counted


def smooth(value):
    high = 0.5 + 0.5 * jnp.tanh(0.5 * jnp.abs(value))
    soft = jnp.maximum(value, 0.0) - jnp.log(high)
    sigmoid = jnp.where(value >= 0.0, high, 1.0 - high)
    return 0.3 * value + 0.7 * soft, 0.3 + 0.7 * sigmoid


class Sizes:
    def __init__(self, nla, nlo, samples, quads, wrows, wcols):
        self.nla, self.nlo = nla, nlo
        self.n = nla * nlo
        self.B, self.Q = samples, quads
        self.PX = R * quads
        self.S = samples // nlo
        self.L = quads * nlo
        self.CH = self.S // 4 if self.S % 64 == 0 else 16
        self.nch = self.S // self.CH
        self.wr, self.wc = wrows, wcols
        self.LP = -(-wrows // 128) * 128


def main_kernel(
    z,
    fields, cot, sea_h, missing_h, mean_h, std_h, wt_h, vec_h,
    out_low, out_grad, grads,
    ob, fo, fin, cin, sea, missing, mean, std, wt, vec, fb, pres, cmo, cm, cmn, cnt, sb, cb,
    X, H, G, F, act, slope, sg, ct, pre, bo, fs, red,
    p_o, p_h, sg_o, sg_h, act_h, slope_h, cnt_h,
    w1, w2, t1, t2, acc1, acc2,
    ws, wg, kg_in, kf, kl,
    ca, cr, za, zr, kform, ssum, ts, lb, lr,
    y1, y2, y3,
    load_sem, mask_s, mask_r, f_s, f_r, c_s, c_r, halo_s, halo_r,
    bo_s, bo_r, bo_o, fo_s, fo_r, fo_o, wg_s, wg_r, kz_s, kz_r, kc_s, kc_r,
    rc_s, rc_r, rz_s, rz_r, ro_s, ro_r, y_s, y_r, near_s, near_r,
):
    nla, nlo, n = z.nla, z.nlo, z.n
    S, L, Q, CH, nch = z.S, z.L, z.Q, z.CH, z.nch
    la = lax.axis_index("lat")
    lo = lax.axis_index("lon")
    me = la * nlo + lo

    def remote(src, dst, ss, rs, lat_to, lon_to):
        return pltpu.make_async_remote_copy(
            src, dst, ss, rs, device_id=(lat_to, lon_to), device_id_type=MESH
        )

    def received(ref, sem):
        remote(ref, ref, sem, sem, la, lo).wait_recv()

    def sent(ref, sem):
        remote(ref, ref, sem, sem, la, lo).wait_send()

    def loop(low, high, body):
        def step(k, carry):
            body(k)
            return carry
        lax.fori_loop(low, high, step, 0)

    def others(body):
        upper = la // (nla // 2)

        def row(t):
            i = upper * t + (1 - upper) * (nla - 1 - t)

            def one(j):
                @pl.when(jnp.logical_or(i != la, j != lo))
                def _():
                    body(i, j)
            loop(0, nlo, one)
        loop(0, nla, row)

    own = pl.ds(C, W)

    def chunk(c):
        return pl.ds(pl.multiple_of(c * CH, CH), CH)

    def peer(k):
        return lax.rem(lo + k, nlo)

    barrier = pltpu.get_barrier_semaphore()
    others(lambda i, j: pl.semaphore_signal(barrier, inc=1, device_id=(i, j), device_id_type=MESH))
    pairs = (
        (missing_h, missing), (sea_h, sea), (mean_h, mean), (std_h, std), (wt_h, wt), (vec_h, vec),
        (fields, fin), (cot, cin),
    )
    loads = [pltpu.make_async_copy(src, dst, load_sem.at[i]) for i, (src, dst) in enumerate(pairs)]
    for load in loads:
        load.start()
    for load in loads[:-2]:
        load.wait()
    load_f, load_c = loads[-2:]

    present, counted = both_masks(missing[...], sea[...])
    pres[...] = present.T
    width = min(z.B, 128)

    def for_lon(m):
        return pltpu.roll(counted, lax.rem(z.B - m * S, z.B), 1)[:, :width]

    for k in range(1, nlo):
        cmo[k] = for_lon(peer(k))
    cm[lo] = for_lon(lo)
    pad = z.LP - z.wr
    for k in range(2):
        block = wt[k].astype(BF)
        if pad:
            block = jnp.concatenate([block, jnp.zeros((z.wc, pad), BF)], axis=1)
        ws[k] = block
        wg[k, lo] = block
    north_pole, south_pole = la == 0, la == nla - 1
    for side, pole in enumerate((north_pole, south_pole)):
        @pl.when(pole)
        def _():
            for ref in (X, G):
                ref[:, :, cols_of(3 * side)] = jnp.zeros((L + 2, S, C), BF)
            for ref in (p_h, sg_h):
                ref[:, :, cols_of(side)] = jnp.zeros((L, S, C), BF)
            cmn[side] = jnp.zeros_like(cm)

    def w_copy(kind, k):
        return remote(ws.at[kind], wg.at[kind, lo], wg_s.at[kind], wg_r.at[kind], la, peer(k))

    def mask_copy(k):
        return remote(cmo.at[k], cm.at[lo], mask_s.at[0], mask_r.at[0], la, peer(k))

    load_f.wait()

    rstd = 1.0 / std[...]
    center_in = mean[...]

    def place(src, t, c, put, standardize):
        first = pl.multiple_of((t * S + c * CH) * z.PX, CH * z.PX)
        fb[...] = src[pl.ds(first, CH * z.PX), :].astype(F32)
        here = pres[pl.ds(pl.multiple_of(t * S + c * CH, CH), CH), :]
        for p in range(z.PX):
            value = fb[pl.ds(p, CH, stride=z.PX), :]
            if standardize:
                value = (value - center_in) * rstd * here[:, p : p + 1]
            put(p // Q, p % Q, value.astype(BF))

    def f_copy(c, k):
        return remote(
            sb.at[c, k], X.at[pl.ds(1 + Q * lo, Q), chunk(c), own],
            f_s.at[0], f_r.at[c], la, peer(k),
        )

    def c_copy(c, k):
        return remote(
            cb.at[c, k], ct.at[pl.ds(Q * lo, Q), chunk(c), :],
            c_s.at[0], c_r.at[c], la, peer(k),
        )

    def prep_fields(c):
        def one(k):
            def put(i, q, value):
                sb[c, k, q, :, cols_of(i)] = value
            place(fin, peer(k), c, put, True)
        loop(1, nlo, one)

    def send_fields(c):
        loop(1, nlo, lambda k: f_copy(c, k).start())

    def next_fields(c):
        prep_fields(c)
        send_fields(c)

    def own_fields(c):
        def put(i, q, value):
            X[1 + Q * lo + q, chunk(c), cols_of(i + 1)] = value
        place(fin, lo, c, put, True)

    def own_cot(c):
        def put(i, q, value):
            ct[Q * lo + q, chunk(c), cols_of(i)] = value
        place(cin, lo, c, put, False)

    def prep_cot(c):
        def one(k):
            def put(i, q, value):
                cb[c, k, q, :, cols_of(i)] = value
            place(cin, peer(k), c, put, False)
        loop(1, nlo, one)

    prep_fields(0)
    pl.semaphore_wait(barrier, n - 1)
    loop(1, nlo, lambda k: w_copy(FIRST, k).start())
    loop(1, nlo, lambda k: mask_copy(k).start())
    send_fields(0)
    loop(1, nlo, lambda k: w_copy(SECOND, k).start())
    loop(1, nch, next_fields)

    core = lax.rem(la, 2)
    sibling = la + 1 - 2 * core

    def kz_copy(k, d):
        to = lax.rem(la + 2 * d, nla)
        return remote(kl.at[k], kg_in.at[k, la], kz_s.at[k], kz_r.at[k], to, lo)

    def kc_copy(k, d):
        row = lax.rem(la + nla - 2 * d, nla)
        return remote(kg_in.at[k, row], kg_in.at[k, row], kc_s.at[k], kc_r.at[k], sibling, lo)

    def start_kernel(k):
        received(wg.at[k, pl.ds(0, nlo - 1)], wg_r.at[k])
        gathered = jnp.concatenate([wg[k, m].astype(F32) for m in range(nlo)], axis=0)
        kl[k] = gathered.T[: z.wr].astype(BF)
        kg_in[k, la] = kl[k]
        loop(1, nla // 2, lambda d: kz_copy(k, d).start())
        kc_copy(k, 0).start()

    def forward_kernel(k):
        received(kg_in.at[k, pl.ds(0, nla // 2 - 1)], kz_r.at[k])
        loop(1, nla // 2, lambda d: kc_copy(k, d).start())

    def finish_kernel(k):
        received(kg_in.at[k, pl.ds(0, nla // 2)], kc_r.at[k])
        for i in range(nla):
            kf[pl.ds(i * z.wr, z.wr), :] = kg_in[k, i].astype(F32)

    def tap(a, b):
        return kf[pl.ds((3 * a + b) * C, C), :]

    def build_forward(ref):
        for b in range(3):
            for r in range(4):
                for i in range(R):
                    a = r - i
                    good = 0 <= a <= 2
                    block = tap(a, b).astype(BF) if good else jnp.zeros((C, C), BF)
                    ref[pl.ds((b * 4 + r) * C, C), cols_of(i)] = block

    def build_turned(ref):
        for b in range(3):
            for a in range(3):
                block = tap(2 - a, 2 - b).T.astype(BF)
                for i in range(R):
                    ref[pl.ds((b * 4 + a + i) * C, C), cols_of(i)] = block
            for i, r in ((0, 3), (1, 0)):
                ref[pl.ds((b * 4 + r) * C, C), cols_of(i)] = jnp.zeros((C, C), BF)

    start_kernel(FIRST)

    loop(0, nch, own_fields)
    load_c.wait()
    loop(0, nch, own_cot)
    loop(0, nch, prep_cot)
    start_kernel(SECOND)

    def spread_mask():
        mine = jnp.concatenate([cm[m] for m in range(nlo)], axis=0).T
        for j in range(L):
            for i in range(R):
                col = (j // Q) * z.PX + i * Q + j % Q
                cnt[j, :, cols_of(i)] = jnp.broadcast_to(mine[:S, col : col + 1], (S, C))

    def spread_near():
        for side in range(2):
            theirs = jnp.concatenate([cmn[side, m] for m in range(nlo)], axis=0).T
            for j in range(L):
                col = (j // Q) * z.PX + (1 - side) * Q + j % Q
                cnt_h[j, :, cols_of(side)] = jnp.broadcast_to(theirs[:S, col : col + 1], (S, C))

    def near_copy(side):
        to = jnp.maximum(la - 1, 0) if side == 0 else jnp.minimum(la + 1, nla - 1)
        return remote(cm, cmn.at[1 - side], near_s.at[side], near_r.at[side], to, lo)

    def halo_copies(ref, h, c):
        def lanes(r):
            return ref.at[pl.ds(1, L), chunk(c), pl.ds(r * C, C)]

        return pair(lanes(1), lanes(3), lanes(2), lanes(0), h, c)

    def pair(up_from, up_to, down_from, down_to, h, c):
        north = remote(up_from, up_to, halo_s.at[h], halo_r.at[h, c], jnp.maximum(la - 1, 0), lo)
        south = remote(down_from, down_to, halo_s.at[h], halo_r.at[h, c], jnp.minimum(la + 1, nla - 1), lo)
        return north, south

    def edge_send(src, dst, h, c):
        def lanes(ref, side):
            return ref.at[:, chunk(c), pl.ds(side * C, C)]
        north, south = pair(lanes(src, 0), lanes(dst, 1), lanes(src, 1), lanes(dst, 0), h, c)
        pl.when(la > 0)(north.start)
        pl.when(la < nla - 1)(south.start)

    def edge_wait(ref, h, c):
        pl.when(at_pole)(lambda: received(ref.at[:, chunk(c), pl.ds(0, C)], halo_r.at[h, c]))
        pl.when(jnp.logical_not(at_pole))(lambda: received(ref.at[:, chunk(c), :], halo_r.at[h, c]))

    def edge_done(ref, h):
        pl.when(at_pole)(lambda: sent(ref.at[:, :, pl.ds(0, C)], halo_s.at[h]))
        pl.when(jnp.logical_not(at_pole))(lambda: sent(ref, halo_s.at[h]))

    def halo_send(ref, h, c):
        north, south = halo_copies(ref, h, c)
        pl.when(la > 0)(north.start)
        pl.when(la < nla - 1)(south.start)

    at_pole = jnp.logical_or(north_pole, south_pole)

    def halo_wait(ref, h, c):
        def both(width):
            received(ref.at[pl.ds(1, L), chunk(c), pl.ds(0, width)], halo_r.at[h, c])
        pl.when(at_pole)(lambda: both(C))
        pl.when(jnp.logical_not(at_pole))(lambda: both(W))
        wrap(ref, c)

    def wrap(ref, c):
        ref[0, chunk(c), :] = ref[L, chunk(c), :]
        ref[L + 1, chunk(c), :] = ref[1, chunk(c), :]

    def halo_done(ref, h):
        def both(width):
            sent(ref.at[pl.ds(1, L), :, pl.ds(0, width)], halo_s.at[h])
        pl.when(at_pole)(lambda: both(C))
        pl.when(jnp.logical_not(at_pole))(lambda: both(W))

    def taps(ref, c):
        parts = [ref[b : b + L, chunk(c), :].reshape(L * CH, 4 * C) for b in range(3)]
        return jnp.concatenate(parts, axis=1)

    def conv(lhs, kernel):
        out = jnp.dot(lhs, kernel[...], preferred_element_type=F32)
        pre[...] = out.reshape(L, CH, W)

    def kernel_grad(lhs, grad, acc):
        acc[...] += lax.dot_general(
            lhs, grad, (((0,), (0,)), ((), ())), preferred_element_type=F32
        )

    def columns(body, carry):
        return lax.fori_loop(0, L, body, carry, unroll=min(L, 16))

    zero8 = jnp.zeros((8, W), F32)

    def arrive(c):
        received(X.at[pl.ds(1, Q * (nlo - 1)), chunk(c), own], f_r.at[c])
        halo_send(X, 0, c)

    def first_chunk(c, stats):
        halo_wait(X, 0, c)
        conv(taps(X, c), w1)

        def one(j, carry):
            s, m = carry
            p_o[j, chunk(c), :] = pre[j].astype(BF)
            value, grad = smooth(pre[j])
            act[j, chunk(c), :] = value
            slope[j, chunk(c), :] = grad
            here = cnt[j, chunk(c), :]
            return s + to_eight(here * value), m + to_eight(here)

        s8, n8 = columns(one, (zero8, zero8))
        s_c, n_c = fold(total_row(s8)), fold(total_row(n8))
        mean_c = s_c / jnp.maximum(n_c, 1.0)
        mean_w = twice(mean_c)

        def two(j, m2):
            off = act[j, chunk(c), :] - mean_w
            return m2 + to_eight(cnt[j, chunk(c), :] * off * off)

        m_c = fold(total_row(columns(two, zero8)))
        n_0, s_0, m_0 = stats
        delta = mean_c - s_0 / jnp.maximum(n_0, 1.0)
        n_1 = n_0 + n_c
        m_1 = m_0 + m_c + delta * delta * (n_0 * n_c / jnp.maximum(n_1, 1.0))
        return n_1, s_0 + s_c, m_1

    def first_edge(c):
        edge_wait(p_h, 1, c)

        def one(j, carry):
            act_h[j, chunk(c), :], slope_h[j, chunk(c), :] = smooth(p_h[j, chunk(c), :].astype(F32))
            return carry
        columns(one, 0)

    def send_cot(c):
        loop(1, nlo, lambda k: c_copy(c, k).start())

    arrive(0)
    forward_kernel(FIRST)
    received(cm.at[pl.ds(0, nlo - 1)], mask_r.at[0])
    for side, pole in enumerate((north_pole, south_pole)):
        pl.when(jnp.logical_not(pole))(lambda: near_copy(side).start())
    spread_mask()
    finish_kernel(FIRST)
    build_forward(w1)
    build_turned(t1)
    zero1 = jnp.zeros((1, C), F32)

    def first_step(c, stats):
        pl.when(c + 1 < nch)(lambda: arrive(c + 1))
        pl.when(c + 2 == nch)(lambda: loop(0, 2, send_cot))
        return first_chunk(c, stats)

    n_d, s_d, m_d = lax.fori_loop(0, nch, first_step, (zero1, zero1, zero1))

    def share(buf, which, value):
        buf[me] = value
        others(lambda i, j: remote(buf.at[me], buf.at[me], y_s.at[which], y_r.at[which], i, j).start())

    def shared(buf, which):
        block = remote(buf.at[pl.ds(0, n - 1)], buf.at[pl.ds(0, n - 1)], y_s.at[which], y_r.at[which], la, lo)
        block.wait_recv()
        block.wait_send()
        return buf[...]

    share(y1, 0, jnp.concatenate([n_d, s_d, m_d], axis=1))
    loop(0, nch, lambda c: edge_send(p_o, p_h, 1, c))
    loop(2, nch, send_cot)
    for side, pole in enumerate((south_pole, north_pole)):
        pl.when(jnp.logical_not(pole))(lambda: near_copy(side).wait_recv())
    forward_kernel(SECOND)
    spread_near()
    finish_kernel(SECOND)
    build_forward(w2)
    build_turned(t2)
    acc1[...] = jnp.zeros_like(acc1)
    acc2[...] = jnp.zeros_like(acc2)

    parts = shared(y1, 0)
    n_all, s_all, m_all = parts[:, :, :C], parts[:, :, C : 2 * C], parts[:, :, 2 * C :]
    total = jnp.sum(n_all, axis=0)
    center = jnp.sum(s_all, axis=0) / total
    apart = s_all / jnp.maximum(n_all, 1.0) - center[None]
    spread = jnp.sum(m_all + n_all * apart * apart, axis=0) / total
    inverse = lax.rsqrt(spread + EPS)
    gain, shift, bias = vec[0:1, :], vec[1:2, :], vec[2:3, :]
    center_w, inverse_w = twice(center), twice(inverse)
    gain_w, shift_w, bias_w = twice(gain), twice(shift), twice(bias)
    inside = [jnp.where(pole, 0.0, 1.0) for pole in (north_pole, south_pole)]

    def edges(row):
        return jnp.concatenate([row * inside[0], row * inside[1]], axis=1)

    gain_h, shift_h = edges(gain), edges(shift)

    def put_edges(ref, j, c, value):
        low = value.astype(BF)
        ref[1 + j, chunk(c), cols_of(0)], ref[1 + j, chunk(c), cols_of(3)] = low[:, :C], low[:, C:]

    chip, chips = la // 2, nla // 2

    def rows_of(k, i):
        return kform[k, pl.ds(pl.multiple_of(i * z.wr, 8), z.wr), :]

    def core_copy(k):
        return remote(ca.at[k], cr.at[k], rc_s.at[k], rc_r.at[k], sibling, lo)

    def core_start(k, acc):
        for a in range(3):
            for b in range(3):
                top, low = (b * 4 + a) * C, (b * 4 + a + 1) * C
                kform[k, pl.ds((3 * a + b) * C, C), :] = (
                    acc[pl.ds(top, C), cols_of(0)] + acc[pl.ds(low, C), cols_of(1)]
                )

        def one(t):
            ca[k, t] = rows_of(k, 2 * t + 1 - core).astype(BF)
        loop(0, chips, one)
        core_copy(k).start()

    def chip_copy(k, t, slot):
        return remote(za.at[k, t], zr.at[k, slot], rz_s.at[k], rz_r.at[k], 2 * t + core, lo)

    def chip_start(k):
        core_copy(k).wait_recv()
        ssum[k] = jnp.zeros_like(ssum[k])
        ssum[k, 0 : z.wr, :] = rows_of(k, la) + cr[k, chip].astype(F32)

        def one(t):
            @pl.when(t != chip)
            def _():
                za[k, t] = (rows_of(k, 2 * t + core) + cr[k, t].astype(F32)).astype(BF)
                chip_copy(k, t, chip).start()
        loop(0, chips, one)

    def lon_copy(k, m):
        return remote(lb.at[k, m], lr.at[k, lo], ro_s.at[k], ro_r.at[k], la, m)

    def lon_start(k):
        received(zr.at[k, pl.ds(0, chips - 1)], rz_r.at[k])

        def one(t):
            @pl.when(t != chip)
            def _():
                ssum[k, 0 : z.wr, :] += zr[k, t].astype(F32)
        loop(0, chips, one)
        ts[k] = ssum[k].T

        def two(m):
            lb[k, m] = ts[k, pl.ds(pl.multiple_of(m * z.wc, z.wc), z.wc), :].astype(BF)
            pl.when(m != lo)(lambda: lon_copy(k, m).start())
        loop(0, nlo, two)

    def lon_finish(k):
        received(lr.at[k, pl.ds(0, nlo - 1)], ro_r.at[k])
        grads[k, 0 : z.wc] = ts[k, pl.ds(pl.multiple_of(lo * z.wc, z.wc), z.wc), :]

        def one(m):
            @pl.when(m != lo)
            def _():
                grads[k, 0 : z.wc] += lr[k, m].astype(F32)
        loop(0, nlo, one)

    def hidden(c):
        def one(j, carry):
            normed = (act[j, chunk(c), :] - center_w) * inverse_w
            H[1 + j, chunk(c), own] = (normed * gain_w + shift_w).astype(BF)
            normed = (act_h[j, chunk(c), :] - center_w) * inverse_w
            put_edges(H, j, c, normed * gain_h + shift_h)
            return carry
        columns(one, 0)
        wrap(H, c)

    def out_copy(src, dst, ss, rs, c, k):
        m = peer(k)
        return remote(
            src.at[pl.ds(Q * m, Q), chunk(c), :],
            dst.at[:, pl.ds(pl.multiple_of(lo * S + c * CH, CH), CH), :],
            ss.at[0], rs.at[c], la, m,
        )

    def own_out(src, dst, os, c):
        return pltpu.make_async_copy(
            src.at[pl.ds(Q * lo, Q), chunk(c), :],
            dst.at[:, pl.ds(pl.multiple_of(lo * S + c * CH, CH), CH), :],
            os.at[c],
        )

    def send_out(src, dst, ss, rs, os, c):
        loop(1, nlo, lambda k: out_copy(src, dst, ss, rs, c, k).start())
        own_out(src, dst, os, c).start()

    def out_arrived(src, dst, rs, os, c):
        received(dst.at[:, pl.ds(0, CH * (nlo - 1)), :], rs.at[c])
        pltpu.make_async_copy(src.at[pl.ds(0, Q), chunk(0), :], dst.at[:, chunk(0), :], os.at[c]).wait()

    def native_rows(t, c):
        first = pl.multiple_of((t * S + c * CH) * z.PX, CH * z.PX)
        return pl.ds(first, CH * z.PX), pl.ds(pl.multiple_of(t * S + c * CH, CH), CH)

    def finish_block(c):
        out_arrived(bo, ob, bo_r, bo_o, c)

        def one(t):
            rows, here = native_rows(t, c)
            for p in range(z.PX):
                fb[pl.ds(p, CH, stride=z.PX), :] = ob[p % Q, here, cols_of(p // Q)].astype(F32)
            out_low[rows, :] = fb[...].astype(BF)
        loop(0, nlo, one)

    def finish_field(c):
        out_arrived(fs, fo, fo_r, fo_o, c)

        def one(t):
            rows, here = native_rows(t, c)
            fb[...] = cin[rows, :].astype(F32)
            have = pres[here, :]
            for p in range(z.PX):
                pixel = pl.ds(p, CH, stride=z.PX)
                grad = fb[pixel, :] + fo[p % Q, here, cols_of(p // Q)].astype(F32)
                fb[pixel, :] = grad * have[:, p : p + 1] * rstd
            out_grad[rows, :] = fb[...]
        loop(0, nlo, one)

    block_out = (bo, ob, bo_s, bo_r, bo_o)
    field_out = (fs, fo, fo_s, fo_r, fo_o)
    early = 2

    def second_chunk(c):
        first_edge(c)
        hidden(c)
        conv(taps(H, c), w2)
        received(ct.at[pl.ds(0, Q * (nlo - 1)), chunk(c), :], c_r.at[c])

        def one(j, carry):
            value, grad = smooth(pre[j] + bias_w)
            standard = X[1 + j, chunk(c), own].astype(F32)
            bo[j, chunk(c), :] = (standard + value).astype(BF)
            low = (ct[j, chunk(c), :].astype(F32) * grad).astype(BF)
            G[1 + j, chunk(c), own] = low
            return carry + to_eight(low.astype(F32))

        red[0] += columns(one, zero8)
        halo_send(G, 2, c)

    def second_kernel(c):
        grad = G[1 : 1 + L, chunk(c), own].reshape(L * CH, W)
        kernel_grad(taps(H, c), grad, acc2)

    def back_chunk(c):
        halo_wait(G, 2, c)
        conv(taps(G, c), t2)

        def one(j, carry):
            g8, s8 = carry
            value = pre[j]
            sg[j, chunk(c), :] = value
            sg_o[j, chunk(c), :] = value.astype(BF)
            normed = (act[j, chunk(c), :] - center_w) * inverse_w
            return g8 + to_eight(value * normed), s8 + to_eight(value)

        g8, s8 = columns(one, (zero8, zero8))
        red[1] += g8
        red[2] += s8

    def second_step(c):
        second_chunk(c)
        pl.when(c < early)(lambda: send_out(*block_out, c))

    red[...] = jnp.zeros_like(red)
    loop(0, nch, second_step)
    loop(0, nch, second_kernel)
    core_start(SECOND, acc2)
    loop(0, nch, back_chunk)
    sums = [fold(total_row(red[k])) for k in (1, 2, 0)]
    share(y2, 1, jnp.concatenate(sums, axis=1))
    loop(0, nch, lambda c: edge_send(sg_o, sg_h, 3, c))
    loop(early, nch, lambda c: send_out(*block_out, c))

    chip_start(SECOND)
    sums = jnp.sum(shared(y2, 1), axis=0)
    gain_grad, shift_grad = sums[:, :C], sums[:, C : 2 * C]

    scale_w = twice(inverse * gain)
    shift_part = twice(shift_grad / total)
    gain_part = twice(gain_grad / total)

    scale_h = edges(inverse * gain)

    def act_grad(value, activation, here):
        normed = (activation - center_w) * inverse_w
        return value - here * shift_part - here * normed * gain_part

    def first_grad(c):
        def one(j, carry):
            grad = act_grad(sg[j, chunk(c), :], act[j, chunk(c), :], cnt[j, chunk(c), :])
            F[1 + j, chunk(c), own] = (scale_w * grad * slope[j, chunk(c), :]).astype(BF)
            return carry
        columns(one, 0)

    def first_grad_edge(c):
        edge_wait(sg_h, 3, c)

        def one(j, carry):
            theirs = sg_h[j, chunk(c), :].astype(F32)
            grad = act_grad(theirs, act_h[j, chunk(c), :], cnt_h[j, chunk(c), :])
            put_edges(F, j, c, scale_h * grad * slope_h[j, chunk(c), :])
            return carry
        columns(one, 0)
        wrap(F, c)

    def first_kernel(c):
        grad = F[1 : 1 + L, chunk(c), own].reshape(L * CH, W)
        kernel_grad(taps(X, c), grad, acc1)

    def field_chunk(c):
        first_grad_edge(c)
        out = jnp.dot(taps(F, c), t1[...], preferred_element_type=F32)
        fs[:, chunk(c), :] = out.astype(BF).reshape(L, CH, W)

    def send_field(c):
        send_out(*field_out, c)

    held = max(nch - 2, 1)
    def field_step(c):
        field_chunk(c)
        pl.when(c < held)(lambda: send_field(c))
        pl.when(c == 0)(lambda: chip_start(FIRST))

    loop(0, nch, first_grad)
    rows_x = jnp.concatenate([X[b : b + L].reshape(L * S, 4 * C) for b in range(3)], axis=1)
    acc1[...] = lax.dot_general(
        rows_x, F[1 : 1 + L, :, own].reshape(L * S, W), (((0,), (0,)), ((), ())), preferred_element_type=F32
    )
    core_start(FIRST, acc1)
    loop(0, nch, field_step)
    lon_start(SECOND)
    lon_start(FIRST)
    loop(held, nch - 1, send_field)
    loop(0, nch, finish_block)
    lon_finish(SECOND)
    lon_finish(FIRST)
    first_w, second_w = grads[0, 0 : z.wc], grads[1, 0 : z.wc]
    square = total_row(first_w * first_w + second_w * second_w)
    share(y3, 2, sum(square[:, cols_of(t)] for t in range(z.LP // C)))
    loop(max(held, nch - 1), nch, send_field)
    loop(0, nch - 1, finish_field)
    squares = jnp.sum(shared(y3, 2), axis=0)
    mine2 = sum(sums[:, cols_of(t)] * sums[:, cols_of(t)] for t in range(3))
    norm = jnp.sqrt(jnp.sum(squares + mine2, axis=1, keepdims=True))
    for k in range(3):
        grads[0, z.wc + k : z.wc + k + 1, 0:C] = sums[:, cols_of(k)]
    grads[0, z.wc + 3 : z.wc + 4, 0:C] = jnp.broadcast_to(norm, (1, C))

    finish_field(nch - 1)

    sent(sb.at[:, pl.ds(1, nlo - 1)], f_s.at[0])
    sent(cb.at[:, pl.ds(1, nlo - 1)], c_s.at[0])
    sent(cm.at[pl.ds(0, nlo - 1)], mask_s.at[0])
    halo_done(X, 0)
    edge_done(p_o, 1)
    halo_done(G, 2)
    edge_done(sg_o, 3)
    for side, pole in enumerate((north_pole, south_pole)):
        pl.when(jnp.logical_not(pole))(lambda: near_copy(side).wait_send())
    for k in range(2):
        sent(wg.at[k, pl.ds(0, nlo - 1)], wg_s.at[k])
        sent(kg_in.at[k, pl.ds(0, nla // 2 - 1)], kz_s.at[k])
        sent(kg_in.at[k, pl.ds(0, nla // 2)], kc_s.at[k])
        core_copy(k).wait_send()
        sent(zr.at[k, pl.ds(0, chips - 1)], rz_s.at[k])
        sent(lr.at[k, pl.ds(0, nlo - 1)], ro_s.at[k])
    sent(bo.at[pl.ds(0, Q * (nlo - 1))], bo_s.at[0])
    sent(fs.at[pl.ds(0, Q * (nlo - 1))], fo_s.at[0])


def adam_step(master, first, second, grads, rate, decay):
    first_new = BETA_ONE * first + (1.0 - BETA_ONE) * grads
    second_new = BETA_TWO * second + (1.0 - BETA_TWO) * grads * grads
    first_hat = first_new / (1.0 - BETA_ONE**STEP)
    second_hat = second_new / (1.0 - BETA_TWO**STEP)
    master_new = master - rate * (first_hat / (jnp.sqrt(second_hat) + ADAM_EPS) + decay * master)
    return master_new, first_new, second_new


def last_kernel(
    z,
    low, grad, grads, wm_h, wf_h, ws_h, vm_h, vf_h, vs_h,
    block_out, field_grad, norm_h, w_new_h, w_first_h, w_second_h, w_low_h, v_new_h, v_first_h, v_second_h,
    wm, wf, wsec, vm, vf, vs, norm, w_new, w_first, w_second, w_low, v_new, v_first, v_second,
    in_sem, out_sem,
):
    ins = ((wm_h, wm), (wf_h, wf), (ws_h, wsec), (vm_h, vm), (vf_h, vf), (vs_h, vs))
    loads = [pltpu.make_async_copy(src, dst, in_sem.at[i]) for i, (src, dst) in enumerate(ins)]
    for load in loads:
        load.start()
    outs = (
        (grad, field_grad), (low, block_out), (norm, norm_h), (w_new, w_new_h), (w_first, w_first_h),
        (w_second, w_second_h), (w_low, w_low_h), (v_new, v_new_h), (v_first, v_first_h), (v_second, v_second_h),
    )
    stores = [pltpu.make_async_copy(src, dst, out_sem.at[i]) for i, (src, dst) in enumerate(outs)]
    stores[0].start()
    stores[1].start()
    size = grads[0, z.wc + 3 : z.wc + 4, 0:C]
    norm[...] = size[:, 0:1]
    factor = jnp.minimum(1.0, MAX_NORM / size)
    wide = factor[:, 0:1]
    for load in loads:
        load.wait()
    for k in range(2):
        own = grads[k, 0 : z.wc, 0 : z.wr] * wide
        new, first, second = adam_step(wm[k], wf[k], wsec[k], own, RATE_KERNEL, DECAY)
        w_new[k], w_first[k], w_second[k] = new, first, second
        w_low[k] = new.astype(BF)
    for k in range(3):
        own = grads[0, z.wc + k : z.wc + k + 1, 0:C] * factor
        row = slice(k, k + 1)
        new, first, second = adam_step(vm[row, :], vf[row, :], vs[row, :], own, RATE_VECTOR, 0.0)
        v_new[row, :], v_first[row, :], v_second[row, :] = new, first, second
    for store in stores[2:]:
        store.start()
    for store in stores:
        store.wait()


def body(nla, nlo, fields, chan_mean, chan_std, sea_mask, missing, cotangent,
         w_master, w_first, w_second, vec_master, vec_first, vec_second):
    samples, rows, quads, channels = fields.shape
    z = Sizes(nla, nlo, samples, quads, w_master.shape[1], w_master.shape[2])
    S, L, Q, CH, nch, n, B = z.S, z.L, z.Q, z.CH, z.nch, z.n, z.B
    flat = (samples * rows * quads, channels)
    fields = fields.reshape(flat)
    cotangent = cotangent.reshape(flat)
    sea = jnp.transpose(sea_mask, (1, 2, 0))
    miss = jnp.transpose(missing, (1, 2, 0))
    wm, wf, wsec = (jnp.transpose(w, (0, 2, 1)) for w in (w_master, w_first, w_second))
    mean, std = chan_mean.reshape(1, C), chan_std.reshape(1, C)

    vmem = pl.BlockSpec(memory_space=pltpu.VMEM)
    hbm = pl.BlockSpec(memory_space=pl.ANY)
    V = pltpu.VMEM
    dma = pltpu.SemaphoreType.DMA
    shape = jax.ShapeDtypeStruct
    padded = V((L + 2, S, 2 * W), BF)
    wide = V((L, S, W), F32)
    scratch = [
        V((Q, B, W), BF), V((Q, B, W), BF), V(flat, BF), V(flat, BF), V(sea.shape, sea.dtype), V(miss.shape, miss.dtype),
        V((1, C), F32), V((1, C), F32), V(wm.shape, F32), V((3, C), F32),
        V((CH * z.PX, C), F32), V((B, z.PX), F32),
        V((nlo, z.PX, min(B, 128)), F32), V((nlo, z.PX, min(B, 128)), F32),
        V((2, nlo, z.PX, min(B, 128)), F32), wide,
        V((nch, nlo, Q, CH, W), BF), V((nch, nlo, Q, CH, W), BF),
        padded, padded, padded, padded, wide, wide, wide,
        V((L, S, W), BF), V((L, CH, W), F32), V((L, S, W), BF), V((L, S, W), BF), V((3, 8, W), F32),
        V((L, S, W), BF), V((L, S, W), BF), V((L, S, W), BF), V((L, S, W), BF), wide, wide, wide,
        V((12 * C, W), BF), V((12 * C, W), BF), V((12 * C, W), BF), V((12 * C, W), BF),
        V((12 * C, W), F32), V((12 * C, W), F32),
        V((2, z.wc, z.LP), BF), V((2, nlo, z.wc, z.LP), BF), V((2, nla, z.wr, C), BF),
        V((9 * C, C), F32), V((2, z.wr, C), BF),
        V((2, nla // 2, z.wr, C), BF), V((2, nla // 2, z.wr, C), BF),
        V((2, nla // 2, z.wr, C), BF), V((2, nla // 2, z.wr, C), BF), V((2, 9 * C, C), F32),
        V((2, z.LP, C), F32), V((2, C, z.LP), F32), V((2, nlo, z.wc, z.LP), BF), V((2, nlo, z.wc, z.LP), BF),
        V((n, 1, 3 * C), F32), V((n, 1, 3 * C), F32), V((n, 1, C), F32),
        dma((8,)), dma((1,)), dma((1,)), dma((1,)), dma((nch,)), dma((1,)), dma((nch,)),
        dma((4,)), dma((4, nch)),
        dma((1,)), dma((nch,)), dma((nch,)), dma((1,)), dma((nch,)), dma((nch,)), dma((2,)), dma((2,)),
        dma((2,)), dma((2,)), dma((2,)), dma((2,)),
        dma((2,)), dma((2,)), dma((2,)), dma((2,)), dma((2,)), dma((2,)), dma((3,)), dma((3,)),
        dma((2,)), dma((2,)),
    ]
    low, grad, grads = pl.pallas_call(
        functools.partial(main_kernel, z),
        out_shape=(V(flat, BF), V(flat, F32), V((2, z.wc + 8, z.LP), F32)),
        in_specs=[hbm] * 8,
        out_specs=(vmem, vmem, vmem),
        scratch_shapes=scratch,
        compiler_params=pltpu.CompilerParams(
            collective_id=0, has_side_effects=True, vmem_limit_bytes=59 * 2**20
        ),
        name="block",
    )(fields, cotangent, sea, miss, mean, std, wm, vec_master)

    shapes = [((1, 1), F32)] + [(wm.shape, F32)] * 3 + [(wm.shape, BF)] + [((3, C), F32)] * 3
    outs = pl.pallas_call(
        functools.partial(last_kernel, z),
        out_shape=[shape(flat, BF), shape(flat, F32)] + [shape(*v) for v in shapes],
        in_specs=[vmem] * 3 + [hbm] * 6,
        out_specs=[hbm] * 10,
        scratch_shapes=[V(wm.shape, F32)] * 3 + [V((3, C), F32)] * 3 + [V(*v) for v in shapes]
        + [dma((6,)), dma((10,))],
        compiler_params=pltpu.CompilerParams(vmem_limit_bytes=16 * 2**20),
        name="update",
    )(low, grad, grads, wm, wf, wsec, vec_master, vec_first, vec_second)
    block_out, field_grad, norm, w_new, w_f, w_s, w_low, v_new, v_f, v_s = outs
    like = (samples, rows, quads, channels)
    w_new, w_f, w_s, w_low = (jnp.transpose(w, (0, 2, 1)) for w in (w_new, w_f, w_s, w_low))
    return (
        block_out.reshape(like), field_grad.reshape(like), norm.reshape(()),
        w_new, w_f, w_s, w_low, v_new, v_f, v_s,
    )


def solution(mesh):
    tile, kernel = P(None, "lat", "lon", None), P(None, "lat", "lon")
    return jax.shard_map(
        functools.partial(body, mesh.shape["lat"], mesh.shape["lon"]),
        mesh=mesh,
        in_specs=(tile, P(), P(), kernel, kernel, tile, kernel, kernel, kernel, P(), P(), P()),
        out_specs=(tile, tile, P(), kernel, kernel, kernel, kernel, P(), P(), P()),
        check_vma=False,
    )
```

```python
import functools

import jax
import jax.numpy as jnp
from jax import lax
from jax.experimental import pallas as pl
from jax.experimental.pallas import tpu as pltpu
from jax.sharding import PartitionSpec as P

STEP = 10
EPS = 1e-05
MAX_NORM = 1.0
BETA_ONE = 0.9
BETA_TWO = 0.999
ADAM_EPS = 1e-08
RATE_KERNEL = 0.02
RATE_VECTOR = 0.1
DECAY = 0.01

MESH = pl.DeviceIdType.MESH
BF = jnp.bfloat16
F32 = jnp.float32
C = 128
R = 2
W = R * C
FIRST, SECOND = 0, 1


def cols_of(i):
    return slice(i * C, (i + 1) * C)


def twice(row):
    return jnp.concatenate([row, row], axis=1)


def fold(row):
    return row[:, :C] + row[:, C:]


def to_eight(block):
    rows, width = block.shape
    return jnp.sum(block.reshape(rows // 8, 8, width), axis=0)


def total_row(block):
    return jnp.sum(block, axis=0, keepdims=True)


def both_masks(missing, sea):
    have = (1 - missing).astype(F32)
    present = jnp.concatenate([have[0], have[1]], axis=0)
    counted = None
    if sea is not None:
        land = have * sea.astype(F32)
        counted = jnp.concatenate([land[0], land[1]], axis=0)
    return present, counted


def smooth(value):
    high = 0.5 + 0.5 * jnp.tanh(0.5 * jnp.abs(value))
    soft = jnp.maximum(value, 0.0) - jnp.log(high)
    sigmoid = jnp.where(value >= 0.0, high, 1.0 - high)
    return 0.3 * value + 0.7 * soft, 0.3 + 0.7 * sigmoid


class Sizes:
    def __init__(self, nla, nlo, samples, quads, wrows, wcols):
        self.nla, self.nlo = nla, nlo
        self.n = nla * nlo
        self.B, self.Q = samples, quads
        self.PX = R * quads
        self.S = samples // nlo
        self.L = quads * nlo
        self.CH = self.S // 4 if self.S % 64 == 0 else 16
        self.nch = self.S // self.CH
        self.wr, self.wc = wrows, wcols
        self.LP = -(-wrows // 128) * 128
        self.full, self.rest = divmod(wrows, 128)
        self.shared = self.full > 0 and 0 < 2 * self.rest <= 128
        each = self.full + (self.rest > 0)
        self.first = (0, each)
        self.count = (each, self.full if self.shared else each)
        self.pieces = sum(self.count)


def main_kernel(
    z,
    fields, cot, sea_h, missing_h, mean_h, std_h, wt_h, vec_h,
    out_low, out_grad, grads,
    ob, fo, fin, cin, sea, missing, mean, std, wt, vec, fb, pres, cmo, cm, cmn, cnt, sb, cb,
    X, H, G, F, act, slope, sg, ct, pre, bo, fs, red,
    p_o, p_h, sg_o, sg_h, act_h, slope_h, cnt_h,
    w1, w2, t1, t2, acc1, acc2,
    ws, wg, kg_in, kf, kl,
    ca, cr, za, zr, kform, ssum, ts, lb, lr,
    y1, y2, y3,
    load_sem, mask_s, mask_r, f_s, f_r, c_s, c_r, halo_s, halo_r,
    bo_s, bo_r, bo_o, fo_s, fo_r, fo_o, wg_s, wg_r, kz_s, kz_r, kc_s, kc_r,
    rc_s, rc_r, rz_s, rz_r, ro_s, ro_r, y_s, y_r, near_s, near_r,
):
    nla, nlo, n = z.nla, z.nlo, z.n
    S, L, Q, CH, nch = z.S, z.L, z.Q, z.CH, z.nch
    la = lax.axis_index("lat")
    lo = lax.axis_index("lon")
    me = la * nlo + lo

    def remote(src, dst, ss, rs, lat_to, lon_to):
        return pltpu.make_async_remote_copy(
            src, dst, ss, rs, device_id=(lat_to, lon_to), device_id_type=MESH
        )

    def received(ref, sem):
        remote(ref, ref, sem, sem, la, lo).wait_recv()

    def sent(ref, sem):
        remote(ref, ref, sem, sem, la, lo).wait_send()

    def loop(low, high, body):
        def step(k, carry):
            body(k)
            return carry
        lax.fori_loop(low, high, step, 0)

    def others(body):
        upper = la // (nla // 2)

        def row(t):
            i = upper * t + (1 - upper) * (nla - 1 - t)

            def one(j):
                @pl.when(jnp.logical_or(i != la, j != lo))
                def _():
                    body(i, j)
            loop(0, nlo, one)
        loop(0, nla, row)

    own = pl.ds(C, W)

    def chunk(c):
        return pl.ds(pl.multiple_of(c * CH, CH), CH)

    def peer(k):
        return lax.rem(lo + k, nlo)

    barrier = pltpu.get_barrier_semaphore()
    others(lambda i, j: pl.semaphore_signal(barrier, inc=1, device_id=(i, j), device_id_type=MESH))
    pairs = (
        (missing_h, missing), (sea_h, sea), (mean_h, mean), (std_h, std), (wt_h, wt), (vec_h, vec),
        (fields, fin), (cot, cin),
    )
    loads = [pltpu.make_async_copy(src, dst, load_sem.at[i]) for i, (src, dst) in enumerate(pairs)]
    for load in loads:
        load.start()
    for load in loads[:-2]:
        load.wait()
    load_f, load_c = loads[-2:]

    present, counted = both_masks(missing[...], sea[...])
    pres[...] = present.T
    width = min(z.B, 128)

    def for_lon(m):
        return pltpu.roll(counted, lax.rem(z.B - m * S, z.B), 1)[:, :width]

    for k in range(1, nlo):
        cmo[k] = for_lon(peer(k))
    cm[lo] = for_lon(lo)
    tails = []
    for k in range(2):
        block = wt[k].astype(BF)
        for f in range(z.full):
            ws[z.first[k] + f] = block[:, f * 128 : (f + 1) * 128]
        tails.append(block[:, z.full * 128 :])
    if z.rest:
        groups = [(z.full, tails)] if z.shared else [(z.first[k] + z.full, tails[k : k + 1]) for k in range(2)]
        for slot, parts in groups:
            empty = 128 - z.rest * len(parts)
            if empty:
                parts = parts + [jnp.zeros((z.wc, empty), BF)]
            ws[slot] = jnp.concatenate(parts, axis=1)
    wg[lo] = ws[...]
    north_pole, south_pole = la == 0, la == nla - 1
    for side, pole in enumerate((north_pole, south_pole)):
        @pl.when(pole)
        def _():
            for ref in (X, G):
                ref[:, :, cols_of(3 * side)] = jnp.zeros((L + 2, S, C), BF)
            for ref in (p_h, sg_h):
                ref[:, :, cols_of(side)] = jnp.zeros((L, S, C), BF)
            cmn[side] = jnp.zeros_like(cm)

    def w_copy(kind, k):
        part = pl.ds(z.first[kind], z.count[kind])
        return remote(ws.at[part], wg.at[lo, part], wg_s.at[kind], wg_r.at[kind], la, peer(k))

    def mask_copy(k):
        return remote(cmo.at[k], cm.at[lo], mask_s.at[0], mask_r.at[0], la, peer(k))

    load_f.wait()

    rstd = 1.0 / std[...]
    center_in = mean[...]

    def place(src, t, c, put, standardize):
        first = pl.multiple_of((t * S + c * CH) * z.PX, CH * z.PX)
        fb[...] = src[pl.ds(first, CH * z.PX), :].astype(F32)
        here = pres[pl.ds(pl.multiple_of(t * S + c * CH, CH), CH), :]
        for p in range(z.PX):
            value = fb[pl.ds(p, CH, stride=z.PX), :]
            if standardize:
                value = (value - center_in) * rstd * here[:, p : p + 1]
            put(p // Q, p % Q, value.astype(BF))

    def f_copy(c, k):
        return remote(
            sb.at[c, k], X.at[pl.ds(1 + Q * lo, Q), chunk(c), own],
            f_s.at[0], f_r.at[c], la, peer(k),
        )

    def c_copy(c, k):
        return remote(
            cb.at[c, k], ct.at[pl.ds(Q * lo, Q), chunk(c), :],
            c_s.at[0], c_r.at[c], la, peer(k),
        )

    def prep_fields(c):
        def one(k):
            def put(i, q, value):
                sb[c, k, q, :, cols_of(i)] = value
            place(fin, peer(k), c, put, True)
        loop(1, nlo, one)

    def send_fields(c):
        loop(1, nlo, lambda k: f_copy(c, k).start())

    def next_fields(c):
        prep_fields(c)
        send_fields(c)

    def own_fields(c):
        def put(i, q, value):
            X[1 + Q * lo + q, chunk(c), cols_of(i + 1)] = value
        place(fin, lo, c, put, True)

    def own_cot(c):
        def put(i, q, value):
            ct[Q * lo + q, chunk(c), cols_of(i)] = value
        place(cin, lo, c, put, False)

    def prep_cot(c):
        def one(k):
            def put(i, q, value):
                cb[c, k, q, :, cols_of(i)] = value
            place(cin, peer(k), c, put, False)
        loop(1, nlo, one)

    prep_fields(0)
    pl.semaphore_wait(barrier, n - 1)
    loop(1, nlo, lambda k: w_copy(FIRST, k).start())
    loop(1, nlo, lambda k: mask_copy(k).start())
    send_fields(0)
    loop(1, nlo, lambda k: w_copy(SECOND, k).start())
    loop(1, nch, next_fields)

    core = lax.rem(la, 2)
    sibling = la + 1 - 2 * core

    def kz_copy(k, d):
        to = lax.rem(la + 2 * d, nla)
        return remote(kl.at[k], kg_in.at[k, la], kz_s.at[k], kz_r.at[k], to, lo)

    def kc_copy(k, d):
        row = lax.rem(la + nla - 2 * d, nla)
        return remote(kg_in.at[k, row], kg_in.at[k, row], kc_s.at[k], kc_r.at[k], sibling, lo)

    def start_kernel(k):
        received(wg.at[pl.ds(0, nlo - 1), pl.ds(z.first[k], z.count[k])], wg_r.at[k])

        def turned_block(slot):
            return jnp.concatenate([wg[m, slot].astype(F32) for m in range(nlo)], axis=0).T.astype(BF)

        for f in range(z.full):
            kl[k, f * 128 : (f + 1) * 128] = turned_block(z.first[k] + f)
        if z.rest:
            slot, start = (z.full, k * z.rest) if z.shared else (z.first[k] + z.full, 0)
            kl[k, z.full * 128 : z.wr] = turned_block(slot)[start : start + z.rest]
        kg_in[k, la] = kl[k]
        loop(1, nla // 2, lambda d: kz_copy(k, d).start())
        kc_copy(k, 0).start()

    def forward_kernel(k):
        received(kg_in.at[k, pl.ds(0, nla // 2 - 1)], kz_r.at[k])
        loop(1, nla // 2, lambda d: kc_copy(k, d).start())

    def finish_kernel(k):
        received(kg_in.at[k, pl.ds(0, nla // 2)], kc_r.at[k])
        for i in range(nla):
            kf[pl.ds(i * z.wr, z.wr), :] = kg_in[k, i].astype(F32)

    def tap(a, b):
        return kf[pl.ds((3 * a + b) * C, C), :]

    def build_forward(ref):
        for b in range(3):
            for r in range(4):
                for i in range(R):
                    a = r - i
                    good = 0 <= a <= 2
                    block = tap(a, b).astype(BF) if good else jnp.zeros((C, C), BF)
                    ref[pl.ds((b * 4 + r) * C, C), cols_of(i)] = block

    def build_turned(ref):
        for b in range(3):
            for a in range(3):
                block = tap(2 - a, 2 - b).T.astype(BF)
                for i in range(R):
                    ref[pl.ds((b * 4 + a + i) * C, C), cols_of(i)] = block
            for i, r in ((0, 3), (1, 0)):
                ref[pl.ds((b * 4 + r) * C, C), cols_of(i)] = jnp.zeros((C, C), BF)

    start_kernel(FIRST)

    loop(0, nch, own_fields)
    load_c.wait()
    loop(0, nch, own_cot)
    loop(0, nch, prep_cot)
    start_kernel(SECOND)

    def spread_mask():
        mine = jnp.concatenate([cm[m] for m in range(nlo)], axis=0).T
        for j in range(L):
            for i in range(R):
                col = (j // Q) * z.PX + i * Q + j % Q
                cnt[j, :, cols_of(i)] = jnp.broadcast_to(mine[:S, col : col + 1], (S, C))

    def spread_near():
        for side in range(2):
            theirs = jnp.concatenate([cmn[side, m] for m in range(nlo)], axis=0).T
            for j in range(L):
                col = (j // Q) * z.PX + (1 - side) * Q + j % Q
                cnt_h[j, :, cols_of(side)] = jnp.broadcast_to(theirs[:S, col : col + 1], (S, C))

    def near_copy(side):
        to = jnp.maximum(la - 1, 0) if side == 0 else jnp.minimum(la + 1, nla - 1)
        return remote(cm, cmn.at[1 - side], near_s.at[side], near_r.at[side], to, lo)

    def halo_copies(ref, h, c):
        def lanes(r):
            return ref.at[pl.ds(1, L), chunk(c), pl.ds(r * C, C)]

        return pair(lanes(1), lanes(3), lanes(2), lanes(0), h, c)

    def pair(up_from, up_to, down_from, down_to, h, c):
        north = remote(up_from, up_to, halo_s.at[h], halo_r.at[h, c], jnp.maximum(la - 1, 0), lo)
        south = remote(down_from, down_to, halo_s.at[h], halo_r.at[h, c], jnp.minimum(la + 1, nla - 1), lo)
        return north, south

    def edge_send(src, dst, h, c):
        def lanes(ref, side):
            return ref.at[:, chunk(c), pl.ds(side * C, C)]
        north, south = pair(lanes(src, 0), lanes(dst, 1), lanes(src, 1), lanes(dst, 0), h, c)
        pl.when(la > 0)(north.start)
        pl.when(la < nla - 1)(south.start)

    def edge_wait(ref, h, c):
        pl.when(at_pole)(lambda: received(ref.at[:, chunk(c), pl.ds(0, C)], halo_r.at[h, c]))
        pl.when(jnp.logical_not(at_pole))(lambda: received(ref.at[:, chunk(c), :], halo_r.at[h, c]))

    def edge_done(ref, h):
        pl.when(at_pole)(lambda: sent(ref.at[:, :, pl.ds(0, C)], halo_s.at[h]))
        pl.when(jnp.logical_not(at_pole))(lambda: sent(ref, halo_s.at[h]))

    def halo_send(ref, h, c):
        north, south = halo_copies(ref, h, c)
        pl.when(la > 0)(north.start)
        pl.when(la < nla - 1)(south.start)

    at_pole = jnp.logical_or(north_pole, south_pole)

    def halo_wait(ref, h, c):
        def both(width):
            received(ref.at[pl.ds(1, L), chunk(c), pl.ds(0, width)], halo_r.at[h, c])
        pl.when(at_pole)(lambda: both(C))
        pl.when(jnp.logical_not(at_pole))(lambda: both(W))
        wrap(ref, c)

    def wrap(ref, c):
        ref[0, chunk(c), :] = ref[L, chunk(c), :]
        ref[L + 1, chunk(c), :] = ref[1, chunk(c), :]

    def halo_done(ref, h):
        def both(width):
            sent(ref.at[pl.ds(1, L), :, pl.ds(0, width)], halo_s.at[h])
        pl.when(at_pole)(lambda: both(C))
        pl.when(jnp.logical_not(at_pole))(lambda: both(W))

    def taps(ref, c):
        parts = [ref[b : b + L, chunk(c), :].reshape(L * CH, 4 * C) for b in range(3)]
        return jnp.concatenate(parts, axis=1)

    def conv(lhs, kernel):
        out = jnp.dot(lhs, kernel[...], preferred_element_type=F32)
        pre[...] = out.reshape(L, CH, W)

    def kernel_grad(lhs, grad, acc):
        acc[...] += lax.dot_general(
            lhs, grad, (((0,), (0,)), ((), ())), preferred_element_type=F32
        )

    def columns(body, carry):
        return lax.fori_loop(0, L, body, carry, unroll=min(L, 16))

    zero8 = jnp.zeros((8, W), F32)

    def arrive(c):
        received(X.at[pl.ds(1, Q * (nlo - 1)), chunk(c), own], f_r.at[c])
        halo_send(X, 0, c)

    def first_chunk(c, stats):
        halo_wait(X, 0, c)
        conv(taps(X, c), w1)

        def one(j, carry):
            s, m = carry
            p_o[j, chunk(c), :] = pre[j].astype(BF)
            value, grad = smooth(pre[j])
            act[j, chunk(c), :] = value
            slope[j, chunk(c), :] = grad
            here = cnt[j, chunk(c), :]
            return s + to_eight(here * value), m + to_eight(here)

        s8, n8 = columns(one, (zero8, zero8))
        s_c, n_c = fold(total_row(s8)), fold(total_row(n8))
        mean_c = s_c / jnp.maximum(n_c, 1.0)
        mean_w = twice(mean_c)

        def two(j, m2):
            off = act[j, chunk(c), :] - mean_w
            return m2 + to_eight(cnt[j, chunk(c), :] * off * off)

        m_c = fold(total_row(columns(two, zero8)))
        n_0, s_0, m_0 = stats
        delta = mean_c - s_0 / jnp.maximum(n_0, 1.0)
        n_1 = n_0 + n_c
        m_1 = m_0 + m_c + delta * delta * (n_0 * n_c / jnp.maximum(n_1, 1.0))
        return n_1, s_0 + s_c, m_1

    def first_edge(c):
        edge_wait(p_h, 1, c)

        def one(j, carry):
            act_h[j, chunk(c), :], slope_h[j, chunk(c), :] = smooth(p_h[j, chunk(c), :].astype(F32))
            return carry
        columns(one, 0)

    def send_cot(c):
        loop(1, nlo, lambda k: c_copy(c, k).start())

    arrive(0)
    forward_kernel(FIRST)
    received(cm.at[pl.ds(0, nlo - 1)], mask_r.at[0])
    for side, pole in enumerate((north_pole, south_pole)):
        pl.when(jnp.logical_not(pole))(lambda: near_copy(side).start())
    spread_mask()
    finish_kernel(FIRST)
    build_forward(w1)
    build_turned(t1)
    zero1 = jnp.zeros((1, C), F32)

    def first_step(c, stats):
        pl.when(c + 1 < nch)(lambda: arrive(c + 1))
        pl.when(c + 2 == nch)(lambda: loop(0, 2, send_cot))
        return first_chunk(c, stats)

    n_d, s_d, m_d = lax.fori_loop(0, nch, first_step, (zero1, zero1, zero1))

    def share(buf, which, value):
        buf[me] = value
        others(lambda i, j: remote(buf.at[me], buf.at[me], y_s.at[which], y_r.at[which], i, j).start())

    def shared(buf, which):
        block = remote(buf.at[pl.ds(0, n - 1)], buf.at[pl.ds(0, n - 1)], y_s.at[which], y_r.at[which], la, lo)
        block.wait_recv()
        block.wait_send()
        return buf[...]

    share(y1, 0, jnp.concatenate([n_d, s_d, m_d], axis=1))
    loop(0, nch, lambda c: edge_send(p_o, p_h, 1, c))
    loop(2, nch, send_cot)
    for side, pole in enumerate((south_pole, north_pole)):
        pl.when(jnp.logical_not(pole))(lambda: near_copy(side).wait_recv())
    forward_kernel(SECOND)
    spread_near()
    finish_kernel(SECOND)
    build_forward(w2)
    build_turned(t2)
    acc1[...] = jnp.zeros_like(acc1)
    acc2[...] = jnp.zeros_like(acc2)

    parts = shared(y1, 0)
    n_all, s_all, m_all = parts[:, :, :C], parts[:, :, C : 2 * C], parts[:, :, 2 * C :]
    total = jnp.sum(n_all, axis=0)
    center = jnp.sum(s_all, axis=0) / total
    apart = s_all / jnp.maximum(n_all, 1.0) - center[None]
    spread = jnp.sum(m_all + n_all * apart * apart, axis=0) / total
    inverse = lax.rsqrt(spread + EPS)
    gain, shift, bias = vec[0:1, :], vec[1:2, :], vec[2:3, :]
    center_w, inverse_w = twice(center), twice(inverse)
    gain_w, shift_w, bias_w = twice(gain), twice(shift), twice(bias)
    inside = [jnp.where(pole, 0.0, 1.0) for pole in (north_pole, south_pole)]

    def edges(row):
        return jnp.concatenate([row * inside[0], row * inside[1]], axis=1)

    gain_h, shift_h = edges(gain), edges(shift)

    def put_edges(ref, j, c, value):
        low = value.astype(BF)
        ref[1 + j, chunk(c), cols_of(0)], ref[1 + j, chunk(c), cols_of(3)] = low[:, :C], low[:, C:]

    chip, chips = la // 2, nla // 2

    def rows_of(k, i):
        return kform[k, pl.ds(pl.multiple_of(i * z.wr, 8), z.wr), :]

    def core_copy(k):
        return remote(ca.at[k], cr.at[k], rc_s.at[k], rc_r.at[k], sibling, lo)

    def core_start(k, acc):
        for a in range(3):
            for b in range(3):
                top, low = (b * 4 + a) * C, (b * 4 + a + 1) * C
                kform[k, pl.ds((3 * a + b) * C, C), :] = (
                    acc[pl.ds(top, C), cols_of(0)] + acc[pl.ds(low, C), cols_of(1)]
                )

        def one(t):
            ca[k, t] = rows_of(k, 2 * t + 1 - core).astype(BF)
        loop(0, chips, one)
        core_copy(k).start()

    def chip_copy(k, t, slot):
        return remote(za.at[k, t], zr.at[k, slot], rz_s.at[k], rz_r.at[k], 2 * t + core, lo)

    def chip_start(k):
        core_copy(k).wait_recv()
        ssum[k] = jnp.zeros_like(ssum[k])
        ssum[k, 0 : z.wr, :] = rows_of(k, la) + cr[k, chip].astype(F32)

        def one(t):
            @pl.when(t != chip)
            def _():
                za[k, t] = (rows_of(k, 2 * t + core) + cr[k, t].astype(F32)).astype(BF)
                chip_copy(k, t, chip).start()
        loop(0, chips, one)

    def lon_copy(k, m):
        return remote(lb.at[k, m], lr.at[k, lo], ro_s.at[k], ro_r.at[k], la, m)

    def lon_start(k):
        received(zr.at[k, pl.ds(0, chips - 1)], rz_r.at[k])

        def one(t):
            @pl.when(t != chip)
            def _():
                ssum[k, 0 : z.wr, :] += zr[k, t].astype(F32)
        loop(0, chips, one)
        ts[k] = ssum[k].T

        def two(m):
            lb[k, m] = ts[k, pl.ds(pl.multiple_of(m * z.wc, z.wc), z.wc), :].astype(BF)
            pl.when(m != lo)(lambda: lon_copy(k, m).start())
        loop(0, nlo, two)

    def lon_finish(k):
        received(lr.at[k, pl.ds(0, nlo - 1)], ro_r.at[k])
        grads[k, 0 : z.wc] = ts[k, pl.ds(pl.multiple_of(lo * z.wc, z.wc), z.wc), :]

        def one(m):
            @pl.when(m != lo)
            def _():
                grads[k, 0 : z.wc] += lr[k, m].astype(F32)
        loop(0, nlo, one)

    def hidden(c):
        def one(j, carry):
            normed = (act[j, chunk(c), :] - center_w) * inverse_w
            H[1 + j, chunk(c), own] = (normed * gain_w + shift_w).astype(BF)
            normed = (act_h[j, chunk(c), :] - center_w) * inverse_w
            put_edges(H, j, c, normed * gain_h + shift_h)
            return carry
        columns(one, 0)
        wrap(H, c)

    def out_copy(src, dst, ss, rs, c, k):
        m = peer(k)
        return remote(
            src.at[pl.ds(Q * m, Q), chunk(c), :],
            dst.at[:, pl.ds(pl.multiple_of(lo * S + c * CH, CH), CH), :],
            ss.at[0], rs.at[c], la, m,
        )

    def own_out(src, dst, os, c):
        return pltpu.make_async_copy(
            src.at[pl.ds(Q * lo, Q), chunk(c), :],
            dst.at[:, pl.ds(pl.multiple_of(lo * S + c * CH, CH), CH), :],
            os.at[c],
        )

    def send_out(src, dst, ss, rs, os, c):
        loop(1, nlo, lambda k: out_copy(src, dst, ss, rs, c, k).start())
        own_out(src, dst, os, c).start()

    def out_arrived(src, dst, rs, os, c):
        received(dst.at[:, pl.ds(0, CH * (nlo - 1)), :], rs.at[c])
        pltpu.make_async_copy(src.at[pl.ds(0, Q), chunk(0), :], dst.at[:, chunk(0), :], os.at[c]).wait()

    def native_rows(t, c):
        first = pl.multiple_of((t * S + c * CH) * z.PX, CH * z.PX)
        return pl.ds(first, CH * z.PX), pl.ds(pl.multiple_of(t * S + c * CH, CH), CH)

    def finish_block(c):
        out_arrived(bo, ob, bo_r, bo_o, c)

        def one(t):
            rows, here = native_rows(t, c)
            for p in range(z.PX):
                fb[pl.ds(p, CH, stride=z.PX), :] = ob[p % Q, here, cols_of(p // Q)].astype(F32)
            out_low[rows, :] = fb[...].astype(BF)
        loop(0, nlo, one)

    def finish_field(c):
        out_arrived(fs, fo, fo_r, fo_o, c)

        def one(t):
            rows, here = native_rows(t, c)
            fb[...] = cin[rows, :].astype(F32)
            have = pres[here, :]
            for p in range(z.PX):
                pixel = pl.ds(p, CH, stride=z.PX)
                grad = fb[pixel, :] + fo[p % Q, here, cols_of(p // Q)].astype(F32)
                fb[pixel, :] = grad * have[:, p : p + 1] * rstd
            out_grad[rows, :] = fb[...]
        loop(0, nlo, one)

    block_out = (bo, ob, bo_s, bo_r, bo_o)
    field_out = (fs, fo, fo_s, fo_r, fo_o)
    early = 2

    def second_chunk(c):
        first_edge(c)
        hidden(c)
        conv(taps(H, c), w2)
        received(ct.at[pl.ds(0, Q * (nlo - 1)), chunk(c), :], c_r.at[c])

        def one(j, carry):
            value, grad = smooth(pre[j] + bias_w)
            standard = X[1 + j, chunk(c), own].astype(F32)
            bo[j, chunk(c), :] = (standard + value).astype(BF)
            low = (ct[j, chunk(c), :].astype(F32) * grad).astype(BF)
            G[1 + j, chunk(c), own] = low
            return carry + to_eight(low.astype(F32))

        red[0] += columns(one, zero8)
        halo_send(G, 2, c)

    def second_kernel(c):
        grad = G[1 : 1 + L, chunk(c), own].reshape(L * CH, W)
        kernel_grad(taps(H, c), grad, acc2)

    def back_chunk(c):
        halo_wait(G, 2, c)
        conv(taps(G, c), t2)

        def one(j, carry):
            g8, s8 = carry
            value = pre[j]
            sg[j, chunk(c), :] = value
            sg_o[j, chunk(c), :] = value.astype(BF)
            normed = (act[j, chunk(c), :] - center_w) * inverse_w
            return g8 + to_eight(value * normed), s8 + to_eight(value)

        g8, s8 = columns(one, (zero8, zero8))
        red[1] += g8
        red[2] += s8

    def second_step(c):
        second_chunk(c)
        pl.when(c < early)(lambda: send_out(*block_out, c))

    red[...] = jnp.zeros_like(red)
    loop(0, nch, second_step)
    loop(0, nch, second_kernel)
    core_start(SECOND, acc2)
    loop(0, nch, back_chunk)
    sums = [fold(total_row(red[k])) for k in (1, 2, 0)]
    share(y2, 1, jnp.concatenate(sums, axis=1))
    loop(0, nch, lambda c: edge_send(sg_o, sg_h, 3, c))
    loop(early, nch, lambda c: send_out(*block_out, c))

    chip_start(SECOND)
    sums = jnp.sum(shared(y2, 1), axis=0)
    gain_grad, shift_grad = sums[:, :C], sums[:, C : 2 * C]

    scale_w = twice(inverse * gain)
    shift_part = twice(shift_grad / total)
    gain_part = twice(gain_grad / total)

    scale_h = edges(inverse * gain)

    def act_grad(value, activation, here):
        normed = (activation - center_w) * inverse_w
        return value - here * shift_part - here * normed * gain_part

    def first_grad(c):
        def one(j, carry):
            grad = act_grad(sg[j, chunk(c), :], act[j, chunk(c), :], cnt[j, chunk(c), :])
            F[1 + j, chunk(c), own] = (scale_w * grad * slope[j, chunk(c), :]).astype(BF)
            return carry
        columns(one, 0)

    def first_grad_edge(c):
        edge_wait(sg_h, 3, c)

        def one(j, carry):
            theirs = sg_h[j, chunk(c), :].astype(F32)
            grad = act_grad(theirs, act_h[j, chunk(c), :], cnt_h[j, chunk(c), :])
            put_edges(F, j, c, scale_h * grad * slope_h[j, chunk(c), :])
            return carry
        columns(one, 0)
        wrap(F, c)

    def first_kernel(c):
        grad = F[1 : 1 + L, chunk(c), own].reshape(L * CH, W)
        kernel_grad(taps(X, c), grad, acc1)

    def field_chunk(c):
        first_grad_edge(c)
        out = jnp.dot(taps(F, c), t1[...], preferred_element_type=F32)
        fs[:, chunk(c), :] = out.astype(BF).reshape(L, CH, W)

    def send_field(c):
        send_out(*field_out, c)

    held = max(nch - 2, 1)
    def field_step(c):
        field_chunk(c)
        pl.when(c < held)(lambda: send_field(c))
        pl.when(c == 0)(lambda: chip_start(FIRST))

    loop(0, nch, first_grad)
    rows_x = jnp.concatenate([X[b : b + L].reshape(L * S, 4 * C) for b in range(3)], axis=1)
    acc1[...] = lax.dot_general(
        rows_x, F[1 : 1 + L, :, own].reshape(L * S, W), (((0,), (0,)), ((), ())), preferred_element_type=F32
    )
    core_start(FIRST, acc1)
    loop(0, nch, field_step)
    lon_start(SECOND)
    lon_start(FIRST)
    loop(held, nch - 1, send_field)
    loop(0, nch, finish_block)
    lon_finish(SECOND)
    lon_finish(FIRST)
    first_w, second_w = grads[0, 0 : z.wc], grads[1, 0 : z.wc]
    square = total_row(first_w * first_w + second_w * second_w)
    share(y3, 2, sum(square[:, cols_of(t)] for t in range(z.LP // C)))
    loop(max(held, nch - 1), nch, send_field)
    loop(0, nch - 1, finish_field)
    squares = jnp.sum(shared(y3, 2), axis=0)
    mine2 = sum(sums[:, cols_of(t)] * sums[:, cols_of(t)] for t in range(3))
    norm = jnp.sqrt(jnp.sum(squares + mine2, axis=1, keepdims=True))
    for k in range(3):
        grads[0, z.wc + k : z.wc + k + 1, 0:C] = sums[:, cols_of(k)]
    grads[0, z.wc + 3 : z.wc + 4, 0:C] = jnp.broadcast_to(norm, (1, C))

    finish_field(nch - 1)

    sent(sb.at[:, pl.ds(1, nlo - 1)], f_s.at[0])
    sent(cb.at[:, pl.ds(1, nlo - 1)], c_s.at[0])
    sent(cm.at[pl.ds(0, nlo - 1)], mask_s.at[0])
    halo_done(X, 0)
    edge_done(p_o, 1)
    halo_done(G, 2)
    edge_done(sg_o, 3)
    for side, pole in enumerate((north_pole, south_pole)):
        pl.when(jnp.logical_not(pole))(lambda: near_copy(side).wait_send())
    for k in range(2):
        sent(wg.at[pl.ds(0, nlo - 1), pl.ds(z.first[k], z.count[k])], wg_s.at[k])
        sent(kg_in.at[k, pl.ds(0, nla // 2 - 1)], kz_s.at[k])
        sent(kg_in.at[k, pl.ds(0, nla // 2)], kc_s.at[k])
        core_copy(k).wait_send()
        sent(zr.at[k, pl.ds(0, chips - 1)], rz_s.at[k])
        sent(lr.at[k, pl.ds(0, nlo - 1)], ro_s.at[k])
    sent(bo.at[pl.ds(0, Q * (nlo - 1))], bo_s.at[0])
    sent(fs.at[pl.ds(0, Q * (nlo - 1))], fo_s.at[0])


def adam_step(master, first, second, grads, rate, decay):
    first_new = BETA_ONE * first + (1.0 - BETA_ONE) * grads
    second_new = BETA_TWO * second + (1.0 - BETA_TWO) * grads * grads
    first_hat = first_new / (1.0 - BETA_ONE**STEP)
    second_hat = second_new / (1.0 - BETA_TWO**STEP)
    master_new = master - rate * (first_hat / (jnp.sqrt(second_hat) + ADAM_EPS) + decay * master)
    return master_new, first_new, second_new


def last_kernel(
    z,
    low, grad, grads, wm_h, wf_h, ws_h, vm_h, vf_h, vs_h,
    block_out, field_grad, norm_h, w_new_h, w_first_h, w_second_h, w_low_h, v_new_h, v_first_h, v_second_h,
    wm, wf, wsec, vm, vf, vs, norm, w_new, w_first, w_second, w_low, v_new, v_first, v_second,
    in_sem, out_sem,
):
    ins = ((wm_h, wm), (wf_h, wf), (ws_h, wsec), (vm_h, vm), (vf_h, vf), (vs_h, vs))
    loads = [pltpu.make_async_copy(src, dst, in_sem.at[i]) for i, (src, dst) in enumerate(ins)]
    for load in loads:
        load.start()
    outs = (
        (grad, field_grad), (low, block_out), (norm, norm_h), (w_new, w_new_h), (w_first, w_first_h),
        (w_second, w_second_h), (w_low, w_low_h), (v_new, v_new_h), (v_first, v_first_h), (v_second, v_second_h),
    )
    stores = [pltpu.make_async_copy(src, dst, out_sem.at[i]) for i, (src, dst) in enumerate(outs)]
    stores[0].start()
    stores[1].start()
    size = grads[0, z.wc + 3 : z.wc + 4, 0:C]
    norm[...] = size[:, 0:1]
    factor = jnp.minimum(1.0, MAX_NORM / size)
    wide = factor[:, 0:1]
    for load in loads:
        load.wait()
    for k in range(2):
        own = grads[k, 0 : z.wc, 0 : z.wr] * wide
        new, first, second = adam_step(wm[k], wf[k], wsec[k], own, RATE_KERNEL, DECAY)
        w_new[k], w_first[k], w_second[k] = new, first, second
        w_low[k] = new.astype(BF)
    for k in range(3):
        own = grads[0, z.wc + k : z.wc + k + 1, 0:C] * factor
        row = slice(k, k + 1)
        new, first, second = adam_step(vm[row, :], vf[row, :], vs[row, :], own, RATE_VECTOR, 0.0)
        v_new[row, :], v_first[row, :], v_second[row, :] = new, first, second
    for store in stores[2:]:
        store.start()
    for store in stores:
        store.wait()


def body(nla, nlo, fields, chan_mean, chan_std, sea_mask, missing, cotangent,
         w_master, w_first, w_second, vec_master, vec_first, vec_second):
    samples, rows, quads, channels = fields.shape
    z = Sizes(nla, nlo, samples, quads, w_master.shape[1], w_master.shape[2])
    S, L, Q, CH, nch, n, B = z.S, z.L, z.Q, z.CH, z.nch, z.n, z.B
    flat = (samples * rows * quads, channels)
    fields = fields.reshape(flat)
    cotangent = cotangent.reshape(flat)
    sea = jnp.transpose(sea_mask, (1, 2, 0))
    miss = jnp.transpose(missing, (1, 2, 0))
    wm, wf, wsec = (jnp.transpose(w, (0, 2, 1)) for w in (w_master, w_first, w_second))
    mean, std = chan_mean.reshape(1, C), chan_std.reshape(1, C)

    vmem = pl.BlockSpec(memory_space=pltpu.VMEM)
    hbm = pl.BlockSpec(memory_space=pl.ANY)
    V = pltpu.VMEM
    dma = pltpu.SemaphoreType.DMA
    shape = jax.ShapeDtypeStruct
    padded = V((L + 2, S, 2 * W), BF)
    wide = V((L, S, W), F32)
    scratch = [
        V((Q, B, W), BF), V((Q, B, W), BF), V(flat, BF), V(flat, BF), V(sea.shape, sea.dtype), V(miss.shape, miss.dtype),
        V((1, C), F32), V((1, C), F32), V(wm.shape, F32), V((3, C), F32),
        V((CH * z.PX, C), F32), V((B, z.PX), F32),
        V((nlo, z.PX, min(B, 128)), F32), V((nlo, z.PX, min(B, 128)), F32),
        V((2, nlo, z.PX, min(B, 128)), F32), wide,
        V((nch, nlo, Q, CH, W), BF), V((nch, nlo, Q, CH, W), BF),
        padded, padded, padded, padded, wide, wide, wide,
        V((L, S, W), BF), V((L, CH, W), F32), V((L, S, W), BF), V((L, S, W), BF), V((3, 8, W), F32),
        V((L, S, W), BF), V((L, S, W), BF), V((L, S, W), BF), V((L, S, W), BF), wide, wide, wide,
        V((12 * C, W), BF), V((12 * C, W), BF), V((12 * C, W), BF), V((12 * C, W), BF),
        V((12 * C, W), F32), V((12 * C, W), F32),
        V((z.pieces, z.wc, 128), BF), V((nlo, z.pieces, z.wc, 128), BF), V((2, nla, z.wr, C), BF),
        V((9 * C, C), F32), V((2, z.wr, C), BF),
        V((2, nla // 2, z.wr, C), BF), V((2, nla // 2, z.wr, C), BF),
        V((2, nla // 2, z.wr, C), BF), V((2, nla // 2, z.wr, C), BF), V((2, 9 * C, C), F32),
        V((2, z.LP, C), F32), V((2, C, z.LP), F32), V((2, nlo, z.wc, z.LP), BF), V((2, nlo, z.wc, z.LP), BF),
        V((n, 1, 3 * C), F32), V((n, 1, 3 * C), F32), V((n, 1, C), F32),
        dma((8,)), dma((1,)), dma((1,)), dma((1,)), dma((nch,)), dma((1,)), dma((nch,)),
        dma((4,)), dma((4, nch)),
        dma((1,)), dma((nch,)), dma((nch,)), dma((1,)), dma((nch,)), dma((nch,)), dma((2,)), dma((2,)),
        dma((2,)), dma((2,)), dma((2,)), dma((2,)),
        dma((2,)), dma((2,)), dma((2,)), dma((2,)), dma((2,)), dma((2,)), dma((3,)), dma((3,)),
        dma((2,)), dma((2,)),
    ]
    low, grad, grads = pl.pallas_call(
        functools.partial(main_kernel, z),
        out_shape=(V(flat, BF), V(flat, F32), V((2, z.wc + 8, z.LP), F32)),
        in_specs=[hbm] * 8,
        out_specs=(vmem, vmem, vmem),
        scratch_shapes=scratch,
        compiler_params=pltpu.CompilerParams(
            collective_id=0, has_side_effects=True, vmem_limit_bytes=59 * 2**20
        ),
        name="block",
    )(fields, cotangent, sea, miss, mean, std, wm, vec_master)

    shapes = [((1, 1), F32)] + [(wm.shape, F32)] * 3 + [(wm.shape, BF)] + [((3, C), F32)] * 3
    outs = pl.pallas_call(
        functools.partial(last_kernel, z),
        out_shape=[shape(flat, BF), shape(flat, F32)] + [shape(*v) for v in shapes],
        in_specs=[vmem] * 3 + [hbm] * 6,
        out_specs=[hbm] * 10,
        scratch_shapes=[V(wm.shape, F32)] * 3 + [V((3, C), F32)] * 3 + [V(*v) for v in shapes]
        + [dma((6,)), dma((10,))],
        compiler_params=pltpu.CompilerParams(vmem_limit_bytes=16 * 2**20),
        name="update",
    )(low, grad, grads, wm, wf, wsec, vec_master, vec_first, vec_second)
    block_out, field_grad, norm, w_new, w_f, w_s, w_low, v_new, v_f, v_s = outs
    like = (samples, rows, quads, channels)
    w_new, w_f, w_s, w_low = (jnp.transpose(w, (0, 2, 1)) for w in (w_new, w_f, w_s, w_low))
    return (
        block_out.reshape(like), field_grad.reshape(like), norm.reshape(()),
        w_new, w_f, w_s, w_low, v_new, v_f, v_s,
    )


def solution(mesh):
    tile, kernel = P(None, "lat", "lon", None), P(None, "lat", "lon")
    return jax.shard_map(
        functools.partial(body, mesh.shape["lat"], mesh.shape["lon"]),
        mesh=mesh,
        in_specs=(tile, P(), P(), kernel, kernel, tile, kernel, kernel, kernel, P(), P(), P()),
        out_specs=(tile, tile, P(), kernel, kernel, kernel, kernel, P(), P(), P()),
        check_vma=False,
    )
```

```python
import functools

import jax
import jax.numpy as jnp
from jax import lax
from jax.experimental import pallas as pl
from jax.experimental.pallas import tpu as pltpu
from jax.sharding import PartitionSpec as P

STEP = 10
EPS = 1e-05
MAX_NORM = 1.0
BETA_ONE = 0.9
BETA_TWO = 0.999
ADAM_EPS = 1e-08
RATE_KERNEL = 0.02
RATE_VECTOR = 0.1
DECAY = 0.01

MESH = pl.DeviceIdType.MESH
BF = jnp.bfloat16
F32 = jnp.float32
C = 128
R = 2
W = R * C
FIRST, SECOND = 0, 1


def cols_of(i):
    return slice(i * C, (i + 1) * C)


def twice(row):
    return jnp.concatenate([row, row], axis=1)


def fold(row):
    return row[:, :C] + row[:, C:]


def to_eight(block):
    rows, width = block.shape
    return jnp.sum(block.reshape(rows // 8, 8, width), axis=0)


def total_row(block):
    return jnp.sum(block, axis=0, keepdims=True)


def both_masks(missing, sea):
    have = (1 - missing).astype(F32)
    present = jnp.concatenate([have[0], have[1]], axis=0)
    counted = None
    if sea is not None:
        land = have * sea.astype(F32)
        counted = jnp.concatenate([land[0], land[1]], axis=0)
    return present, counted


def smooth(value):
    high = 0.5 + 0.5 * jnp.tanh(0.5 * jnp.abs(value))
    soft = jnp.maximum(value, 0.0) - jnp.log(high)
    sigmoid = jnp.where(value >= 0.0, high, 1.0 - high)
    return 0.3 * value + 0.7 * soft, 0.3 + 0.7 * sigmoid


class Sizes:
    def __init__(self, nla, nlo, samples, quads, wrows, wcols):
        self.nla, self.nlo = nla, nlo
        self.n = nla * nlo
        self.B, self.Q = samples, quads
        self.PX = R * quads
        self.S = samples // nlo
        self.L = quads * nlo
        self.CH = self.S // 4 if self.S % 64 == 0 else 16
        self.nch = self.S // self.CH
        self.wr, self.wc = wrows, wcols
        self.LP = -(-wrows // 128) * 128
        self.full, self.rest = divmod(wrows, 128)
        self.shared = self.full > 0 and 0 < 2 * self.rest <= 128
        each = self.full + (self.rest > 0)
        self.first = (0, each)
        self.count = (each, self.full if self.shared else each)
        self.pieces = sum(self.count)


def main_kernel(
    z,
    fields, cot, sea_h, missing_h, mean_h, std_h, wt_h, vec_h,
    out_low, out_grad, grads,
    ob, fo, fin, cin, sea, missing, mean, std, wt, vec, fb, pres, cmo, cm, cmn, cnt, sb, cb,
    X, H, G, F, act, slope, sg, ct, pre, bo, fs, red,
    p_o, p_h, sg_o, sg_h, act_h, slope_h, cnt_h,
    w1, w2, t1, t2, acc1, acc2,
    ws, wg, kg_in, kf, kl,
    ca, cr, za, zr, kform, ssum, ts, lb, lr,
    y1, y2, y3,
    load_sem, mask_s, mask_r, f_s, f_r, c_s, c_r, halo_s, halo_r,
    bo_s, bo_r, bo_o, fo_s, fo_r, fo_o, wg_s, wg_r, kz_s, kz_r, kc_s, kc_r,
    rc_s, rc_r, rz_s, rz_r, ro_s, ro_r, y_s, y_r, near_s, near_r,
):
    nla, nlo, n = z.nla, z.nlo, z.n
    S, L, Q, CH, nch = z.S, z.L, z.Q, z.CH, z.nch
    la = lax.axis_index("lat")
    lo = lax.axis_index("lon")
    me = la * nlo + lo

    def remote(src, dst, ss, rs, lat_to, lon_to):
        return pltpu.make_async_remote_copy(
            src, dst, ss, rs, device_id=(lat_to, lon_to), device_id_type=MESH
        )

    def received(ref, sem):
        remote(ref, ref, sem, sem, la, lo).wait_recv()

    def sent(ref, sem):
        remote(ref, ref, sem, sem, la, lo).wait_send()

    def loop(low, high, body):
        def step(k, carry):
            body(k)
            return carry
        lax.fori_loop(low, high, step, 0)

    def others(body):
        upper = la // (nla // 2)

        def row(t):
            i = upper * t + (1 - upper) * (nla - 1 - t)

            def one(j):
                @pl.when(jnp.logical_or(i != la, j != lo))
                def _():
                    body(i, j)
            loop(0, nlo, one)
        loop(0, nla, row)

    own = pl.ds(C, W)

    def chunk(c):
        return pl.ds(pl.multiple_of(c * CH, CH), CH)

    def peer(k):
        return lax.rem(lo + k, nlo)

    barrier = pltpu.get_barrier_semaphore()
    others(lambda i, j: pl.semaphore_signal(barrier, inc=1, device_id=(i, j), device_id_type=MESH))
    pairs = (
        (missing_h, missing), (sea_h, sea), (mean_h, mean), (std_h, std), (wt_h, wt), (vec_h, vec),
        (fields, fin), (cot, cin),
    )
    loads = [pltpu.make_async_copy(src, dst, load_sem.at[i]) for i, (src, dst) in enumerate(pairs)]
    for load in loads:
        load.start()
    for load in loads[:-2]:
        load.wait()
    load_f, load_c = loads[-2:]

    present, counted = both_masks(missing[...], sea[...])
    pres[...] = present.T
    width = min(z.B, 128)

    def for_lon(m):
        return pltpu.roll(counted, lax.rem(z.B - m * S, z.B), 1)[:, :width]

    for k in range(1, nlo):
        cmo[k] = for_lon(peer(k))
    cm[lo] = for_lon(lo)
    tails = []
    for k in range(2):
        block = wt[k].astype(BF)
        for f in range(z.full):
            ws[z.first[k] + f] = block[:, f * 128 : (f + 1) * 128]
        tails.append(block[:, z.full * 128 :])
    if z.rest:
        groups = [(z.full, tails)] if z.shared else [(z.first[k] + z.full, tails[k : k + 1]) for k in range(2)]
        for slot, parts in groups:
            empty = 128 - z.rest * len(parts)
            if empty:
                parts = parts + [jnp.zeros((z.wc, empty), BF)]
            ws[slot] = jnp.concatenate(parts, axis=1)
    wg[lo] = ws[...]
    north_pole, south_pole = la == 0, la == nla - 1
    for side, pole in enumerate((north_pole, south_pole)):
        @pl.when(pole)
        def _():
            for ref in (X, G):
                ref[:, :, cols_of(3 * side)] = jnp.zeros((L + 2, S, C), BF)
            for ref in (p_h, sg_h):
                ref[:, :, cols_of(side)] = jnp.zeros((L, S, C), BF)
            cmn[side] = jnp.zeros_like(cm)

    def w_copy(kind, k):
        part = pl.ds(z.first[kind], z.count[kind])
        return remote(ws.at[part], wg.at[lo, part], wg_s.at[kind], wg_r.at[kind], la, peer(k))

    def mask_copy(k):
        return remote(cmo.at[k], cm.at[lo], mask_s.at[0], mask_r.at[0], la, peer(k))

    load_f.wait()

    rstd = 1.0 / std[...]
    center_in = mean[...]

    def place(src, t, c, put, standardize):
        first = pl.multiple_of((t * S + c * CH) * z.PX, CH * z.PX)
        fb[...] = src[pl.ds(first, CH * z.PX), :].astype(F32)
        here = pres[pl.ds(pl.multiple_of(t * S + c * CH, CH), CH), :]
        for p in range(z.PX):
            value = fb[pl.ds(p, CH, stride=z.PX), :]
            if standardize:
                value = (value - center_in) * rstd * here[:, p : p + 1]
            put(p // Q, p % Q, value.astype(BF))

    def f_copy(c, k):
        return remote(
            sb.at[c, k], X.at[pl.ds(1 + Q * lo, Q), chunk(c), own],
            f_s.at[0], f_r.at[c], la, peer(k),
        )

    def c_copy(c, k):
        return remote(
            cb.at[c, k], ct.at[pl.ds(Q * lo, Q), chunk(c), :],
            c_s.at[0], c_r.at[c], la, peer(k),
        )

    def prep_fields(c):
        def one(k):
            def put(i, q, value):
                sb[c, k, q, :, cols_of(i)] = value
            place(fin, peer(k), c, put, True)
        loop(1, nlo, one)

    def send_fields(c):
        loop(1, nlo, lambda k: f_copy(c, k).start())

    def next_fields(c):
        prep_fields(c)
        send_fields(c)

    def own_fields(c):
        def put(i, q, value):
            X[1 + Q * lo + q, chunk(c), cols_of(i + 1)] = value
        place(fin, lo, c, put, True)

    def own_cot(c):
        def put(i, q, value):
            ct[Q * lo + q, chunk(c), cols_of(i)] = value
        place(cin, lo, c, put, False)

    def prep_cot(c):
        def one(k):
            def put(i, q, value):
                cb[c, k, q, :, cols_of(i)] = value
            place(cin, peer(k), c, put, False)
        loop(1, nlo, one)

    prep_fields(0)
    pl.semaphore_wait(barrier, n - 1)
    loop(1, nlo, lambda k: w_copy(FIRST, k).start())
    loop(1, nlo, lambda k: mask_copy(k).start())
    send_fields(0)
    loop(1, nlo, lambda k: w_copy(SECOND, k).start())
    loop(1, nch, next_fields)

    core = lax.rem(la, 2)
    sibling = la + 1 - 2 * core

    def kz_copy(k, d):
        to = lax.rem(la + 2 * d, nla)
        return remote(kl.at[k], kg_in.at[k, la], kz_s.at[k], kz_r.at[k], to, lo)

    def kc_copy(k, d):
        row = lax.rem(la + nla - 2 * d, nla)
        return remote(kg_in.at[k, row], kg_in.at[k, row], kc_s.at[k], kc_r.at[k], sibling, lo)

    def start_kernel(k):
        received(wg.at[pl.ds(0, nlo - 1), pl.ds(z.first[k], z.count[k])], wg_r.at[k])

        def turned_block(slot):
            return jnp.concatenate([wg[m, slot].astype(F32) for m in range(nlo)], axis=0).T.astype(BF)

        for f in range(z.full):
            kl[k, f * 128 : (f + 1) * 128] = turned_block(z.first[k] + f)
        if z.rest:
            slot, start = (z.full, k * z.rest) if z.shared else (z.first[k] + z.full, 0)
            kl[k, z.full * 128 : z.wr] = turned_block(slot)[start : start + z.rest]
        kg_in[k, la] = kl[k]
        loop(1, nla // 2, lambda d: kz_copy(k, d).start())
        kc_copy(k, 0).start()

    def forward_kernel(k):
        received(kg_in.at[k, pl.ds(0, nla // 2 - 1)], kz_r.at[k])
        loop(1, nla // 2, lambda d: kc_copy(k, d).start())

    def finish_kernel(k):
        received(kg_in.at[k, pl.ds(0, nla // 2)], kc_r.at[k])
        for i in range(nla):
            kf[pl.ds(i * z.wr, z.wr), :] = kg_in[k, i].astype(F32)

    def tap(a, b):
        return kf[pl.ds((3 * a + b) * C, C), :]

    def build_forward(ref):
        for b in range(3):
            for r in range(4):
                for i in range(R):
                    a = r - i
                    good = 0 <= a <= 2
                    block = tap(a, b).astype(BF) if good else jnp.zeros((C, C), BF)
                    ref[pl.ds((b * 4 + r) * C, C), cols_of(i)] = block

    def build_turned(ref):
        for b in range(3):
            for a in range(3):
                block = tap(2 - a, 2 - b).T.astype(BF)
                for i in range(R):
                    ref[pl.ds((b * 4 + a + i) * C, C), cols_of(i)] = block
            for i, r in ((0, 3), (1, 0)):
                ref[pl.ds((b * 4 + r) * C, C), cols_of(i)] = jnp.zeros((C, C), BF)

    start_kernel(FIRST)

    loop(0, nch, own_fields)
    load_c.wait()
    loop(0, nch, own_cot)
    loop(0, nch, prep_cot)
    start_kernel(SECOND)

    def spread_mask():
        mine = jnp.concatenate([cm[m] for m in range(nlo)], axis=0).T
        for j in range(L):
            for i in range(R):
                col = (j // Q) * z.PX + i * Q + j % Q
                cnt[j, :, cols_of(i)] = jnp.broadcast_to(mine[:S, col : col + 1], (S, C))

    def spread_near():
        for side in range(2):
            theirs = jnp.concatenate([cmn[side, m] for m in range(nlo)], axis=0).T
            for j in range(L):
                col = (j // Q) * z.PX + (1 - side) * Q + j % Q
                cnt_h[j, :, cols_of(side)] = jnp.broadcast_to(theirs[:S, col : col + 1], (S, C))

    def near_copy(side):
        to = jnp.maximum(la - 1, 0) if side == 0 else jnp.minimum(la + 1, nla - 1)
        return remote(cm, cmn.at[1 - side], near_s.at[side], near_r.at[side], to, lo)

    def halo_copies(ref, h, c):
        def lanes(r):
            return ref.at[pl.ds(1, L), chunk(c), pl.ds(r * C, C)]

        return pair(lanes(1), lanes(3), lanes(2), lanes(0), h, c)

    def pair(up_from, up_to, down_from, down_to, h, c):
        north = remote(up_from, up_to, halo_s.at[h], halo_r.at[h, c], jnp.maximum(la - 1, 0), lo)
        south = remote(down_from, down_to, halo_s.at[h], halo_r.at[h, c], jnp.minimum(la + 1, nla - 1), lo)
        return north, south

    def edge_send(src, dst, h, c):
        def lanes(ref, side):
            return ref.at[:, chunk(c), pl.ds(side * C, C)]
        north, south = pair(lanes(src, 0), lanes(dst, 1), lanes(src, 1), lanes(dst, 0), h, c)
        pl.when(la > 0)(north.start)
        pl.when(la < nla - 1)(south.start)

    def edge_wait(ref, h, c):
        pl.when(at_pole)(lambda: received(ref.at[:, chunk(c), pl.ds(0, C)], halo_r.at[h, c]))
        pl.when(jnp.logical_not(at_pole))(lambda: received(ref.at[:, chunk(c), :], halo_r.at[h, c]))

    def edge_done(ref, h):
        pl.when(at_pole)(lambda: sent(ref.at[:, :, pl.ds(0, C)], halo_s.at[h]))
        pl.when(jnp.logical_not(at_pole))(lambda: sent(ref, halo_s.at[h]))

    def halo_send(ref, h, c):
        north, south = halo_copies(ref, h, c)
        pl.when(la > 0)(north.start)
        pl.when(la < nla - 1)(south.start)

    at_pole = jnp.logical_or(north_pole, south_pole)

    def halo_wait(ref, h, c):
        def both(width):
            received(ref.at[pl.ds(1, L), chunk(c), pl.ds(0, width)], halo_r.at[h, c])
        pl.when(at_pole)(lambda: both(C))
        pl.when(jnp.logical_not(at_pole))(lambda: both(W))
        wrap(ref, c)

    def wrap(ref, c):
        ref[0, chunk(c), :] = ref[L, chunk(c), :]
        ref[L + 1, chunk(c), :] = ref[1, chunk(c), :]

    def halo_done(ref, h):
        def both(width):
            sent(ref.at[pl.ds(1, L), :, pl.ds(0, width)], halo_s.at[h])
        pl.when(at_pole)(lambda: both(C))
        pl.when(jnp.logical_not(at_pole))(lambda: both(W))

    def taps(ref, c):
        parts = [ref[b : b + L, chunk(c), :].reshape(L * CH, 4 * C) for b in range(3)]
        return jnp.concatenate(parts, axis=1)

    def conv(lhs, kernel):
        out = jnp.dot(lhs, kernel[...], preferred_element_type=F32)
        pre[...] = out.reshape(L, CH, W)

    def kernel_grad(lhs, grad, acc):
        acc[...] += lax.dot_general(
            lhs, grad, (((0,), (0,)), ((), ())), preferred_element_type=F32
        )

    def columns(body, carry):
        return lax.fori_loop(0, L, body, carry, unroll=min(L, 16))

    zero8 = jnp.zeros((8, W), F32)

    def arrive(c):
        received(X.at[pl.ds(1, Q * (nlo - 1)), chunk(c), own], f_r.at[c])
        halo_send(X, 0, c)

    def first_chunk(c, stats):
        halo_wait(X, 0, c)
        conv(taps(X, c), w1)

        def one(j, carry):
            s, m = carry
            p_o[j, chunk(c), :] = pre[j].astype(BF)
            value, grad = smooth(pre[j])
            act[j, chunk(c), :] = value
            slope[j, chunk(c), :] = grad
            here = cnt[j, chunk(c), :]
            return s + to_eight(here * value), m + to_eight(here)

        s8, n8 = columns(one, (zero8, zero8))
        s_c, n_c = fold(total_row(s8)), fold(total_row(n8))
        mean_c = s_c / jnp.maximum(n_c, 1.0)
        mean_w = twice(mean_c)

        def two(j, m2):
            off = act[j, chunk(c), :] - mean_w
            return m2 + to_eight(cnt[j, chunk(c), :] * off * off)

        m_c = fold(total_row(columns(two, zero8)))
        n_0, s_0, m_0 = stats
        delta = mean_c - s_0 / jnp.maximum(n_0, 1.0)
        n_1 = n_0 + n_c
        m_1 = m_0 + m_c + delta * delta * (n_0 * n_c / jnp.maximum(n_1, 1.0))
        return n_1, s_0 + s_c, m_1

    def first_edge(c):
        edge_wait(p_h, 1, c)

        def one(j, carry):
            act_h[j, chunk(c), :], slope_h[j, chunk(c), :] = smooth(p_h[j, chunk(c), :].astype(F32))
            return carry
        columns(one, 0)

    def send_cot(c):
        loop(1, nlo, lambda k: c_copy(c, k).start())

    arrive(0)
    forward_kernel(FIRST)
    received(cm.at[pl.ds(0, nlo - 1)], mask_r.at[0])
    for side, pole in enumerate((north_pole, south_pole)):
        pl.when(jnp.logical_not(pole))(lambda: near_copy(side).start())
    spread_mask()
    finish_kernel(FIRST)
    build_forward(w1)
    build_turned(t1)
    zero1 = jnp.zeros((1, C), F32)

    def first_step(c, stats):
        pl.when(c + 1 < nch)(lambda: arrive(c + 1))
        pl.when(c + 2 == nch)(lambda: loop(0, 2, send_cot))
        return first_chunk(c, stats)

    n_d, s_d, m_d = lax.fori_loop(0, nch, first_step, (zero1, zero1, zero1))

    def share(buf, which, value):
        buf[me] = value
        others(lambda i, j: remote(buf.at[me], buf.at[me], y_s.at[which], y_r.at[which], i, j).start())

    def shared(buf, which):
        block = remote(buf.at[pl.ds(0, n - 1)], buf.at[pl.ds(0, n - 1)], y_s.at[which], y_r.at[which], la, lo)
        block.wait_recv()
        block.wait_send()
        return buf[...]

    share(y1, 0, jnp.concatenate([n_d, s_d, m_d], axis=1))
    loop(0, nch, lambda c: edge_send(p_o, p_h, 1, c))
    loop(2, nch, send_cot)
    for side, pole in enumerate((south_pole, north_pole)):
        pl.when(jnp.logical_not(pole))(lambda: near_copy(side).wait_recv())
    forward_kernel(SECOND)
    spread_near()
    finish_kernel(SECOND)
    build_forward(w2)
    build_turned(t2)
    acc1[...] = jnp.zeros_like(acc1)
    acc2[...] = jnp.zeros_like(acc2)

    parts = shared(y1, 0)
    n_all, s_all, m_all = parts[:, :, :C], parts[:, :, C : 2 * C], parts[:, :, 2 * C :]
    total = jnp.sum(n_all, axis=0)
    center = jnp.sum(s_all, axis=0) / total
    apart = s_all / jnp.maximum(n_all, 1.0) - center[None]
    spread = jnp.sum(m_all + n_all * apart * apart, axis=0) / total
    inverse = lax.rsqrt(spread + EPS)
    gain, shift, bias = vec[0:1, :], vec[1:2, :], vec[2:3, :]
    center_w, inverse_w = twice(center), twice(inverse)
    gain_w, shift_w, bias_w = twice(gain), twice(shift), twice(bias)
    inside = [jnp.where(pole, 0.0, 1.0) for pole in (north_pole, south_pole)]

    def edges(row):
        return jnp.concatenate([row * inside[0], row * inside[1]], axis=1)

    gain_h, shift_h = edges(gain), edges(shift)

    def put_edges(ref, j, c, value):
        low = value.astype(BF)
        ref[1 + j, chunk(c), cols_of(0)], ref[1 + j, chunk(c), cols_of(3)] = low[:, :C], low[:, C:]

    chip, chips = la // 2, nla // 2

    def rows_of(k, i):
        return kform[k, pl.ds(pl.multiple_of(i * z.wr, 8), z.wr), :]

    def core_copy(k):
        return remote(ca.at[k], cr.at[k], rc_s.at[k], rc_r.at[k], sibling, lo)

    def core_start(k, acc):
        for a in range(3):
            for b in range(3):
                top, low = (b * 4 + a) * C, (b * 4 + a + 1) * C
                kform[k, pl.ds((3 * a + b) * C, C), :] = (
                    acc[pl.ds(top, C), cols_of(0)] + acc[pl.ds(low, C), cols_of(1)]
                )

        def one(t):
            ca[k, t] = rows_of(k, 2 * t + 1 - core).astype(BF)
        loop(0, chips, one)
        core_copy(k).start()

    def chip_copy(k, t, slot):
        return remote(za.at[k, t], zr.at[k, slot], rz_s.at[k], rz_r.at[k], 2 * t + core, lo)

    def chip_start(k):
        core_copy(k).wait_recv()
        ssum[k] = jnp.zeros_like(ssum[k])
        ssum[k, 0 : z.wr, :] = rows_of(k, la) + cr[k, chip].astype(F32)

        def one(t):
            @pl.when(t != chip)
            def _():
                za[k, t] = (rows_of(k, 2 * t + core) + cr[k, t].astype(F32)).astype(BF)
                chip_copy(k, t, chip).start()
        loop(0, chips, one)

    def lon_copy(k, m):
        return remote(lb.at[k, m], lr.at[k, lo], ro_s.at[k], ro_r.at[k], la, m)

    def lon_start(k):
        received(zr.at[k, pl.ds(0, chips - 1)], rz_r.at[k])

        def one(t):
            @pl.when(t != chip)
            def _():
                ssum[k, 0 : z.wr, :] += zr[k, t].astype(F32)
        loop(0, chips, one)
        ts[k] = ssum[k].T

        def two(m):
            lb[k, m] = ts[k, pl.ds(pl.multiple_of(m * z.wc, z.wc), z.wc), :].astype(BF)
            pl.when(m != lo)(lambda: lon_copy(k, m).start())
        loop(0, nlo, two)

    def lon_finish(k):
        received(lr.at[k, pl.ds(0, nlo - 1)], ro_r.at[k])
        grads[k, 0 : z.wc] = ts[k, pl.ds(pl.multiple_of(lo * z.wc, z.wc), z.wc), :]

        def one(m):
            @pl.when(m != lo)
            def _():
                grads[k, 0 : z.wc] += lr[k, m].astype(F32)
        loop(0, nlo, one)

    def hidden(c):
        def one(j, carry):
            normed = (act[j, chunk(c), :] - center_w) * inverse_w
            H[1 + j, chunk(c), own] = (normed * gain_w + shift_w).astype(BF)
            normed = (act_h[j, chunk(c), :] - center_w) * inverse_w
            put_edges(H, j, c, normed * gain_h + shift_h)
            return carry
        columns(one, 0)
        wrap(H, c)

    def out_copy(src, dst, ss, rs, c, k):
        m = peer(k)
        return remote(
            src.at[pl.ds(Q * m, Q), chunk(c), :],
            dst.at[:, pl.ds(pl.multiple_of(lo * S + c * CH, CH), CH), :],
            ss.at[0], rs.at[c], la, m,
        )

    def own_out(src, dst, os, c):
        return pltpu.make_async_copy(
            src.at[pl.ds(Q * lo, Q), chunk(c), :],
            dst.at[:, pl.ds(pl.multiple_of(lo * S + c * CH, CH), CH), :],
            os.at[c],
        )

    def send_out(src, dst, ss, rs, os, c):
        loop(1, nlo, lambda k: out_copy(src, dst, ss, rs, c, k).start())
        own_out(src, dst, os, c).start()

    def out_arrived(src, dst, rs, os, c):
        received(dst.at[:, pl.ds(0, CH * (nlo - 1)), :], rs.at[c])
        pltpu.make_async_copy(src.at[pl.ds(0, Q), chunk(0), :], dst.at[:, chunk(0), :], os.at[c]).wait()

    def native_rows(t, c):
        first = pl.multiple_of((t * S + c * CH) * z.PX, CH * z.PX)
        return pl.ds(first, CH * z.PX), pl.ds(pl.multiple_of(t * S + c * CH, CH), CH)

    def finish_block(c):
        out_arrived(bo, ob, bo_r, bo_o, c)

        def one(t):
            rows, here = native_rows(t, c)
            for p in range(z.PX):
                fb[pl.ds(p, CH, stride=z.PX), :] = ob[p % Q, here, cols_of(p // Q)].astype(F32)
            out_low[rows, :] = fb[...].astype(BF)
        loop(0, nlo, one)

    def finish_field(c):
        out_arrived(fs, fo, fo_r, fo_o, c)

        def one(t):
            rows, here = native_rows(t, c)
            fb[...] = cin[rows, :].astype(F32)
            have = pres[here, :]
            for p in range(z.PX):
                pixel = pl.ds(p, CH, stride=z.PX)
                grad = fb[pixel, :] + fo[p % Q, here, cols_of(p // Q)].astype(F32)
                fb[pixel, :] = grad * have[:, p : p + 1] * rstd
            out_grad[rows, :] = fb[...]
        loop(0, nlo, one)

    block_out = (bo, ob, bo_s, bo_r, bo_o)
    field_out = (fs, fo, fo_s, fo_r, fo_o)
    early = 3

    def second_chunk(c):
        first_edge(c)
        hidden(c)
        conv(taps(H, c), w2)
        received(ct.at[pl.ds(0, Q * (nlo - 1)), chunk(c), :], c_r.at[c])

        def one(j, carry):
            value, grad = smooth(pre[j] + bias_w)
            standard = X[1 + j, chunk(c), own].astype(F32)
            bo[j, chunk(c), :] = (standard + value).astype(BF)
            low = (ct[j, chunk(c), :].astype(F32) * grad).astype(BF)
            G[1 + j, chunk(c), own] = low
            return carry + to_eight(low.astype(F32))

        red[0] += columns(one, zero8)
        halo_send(G, 2, c)

    def second_kernel(c):
        grad = G[1 : 1 + L, chunk(c), own].reshape(L * CH, W)
        kernel_grad(taps(H, c), grad, acc2)

    def back_chunk(c):
        halo_wait(G, 2, c)
        conv(taps(G, c), t2)

        def one(j, carry):
            g8, s8 = carry
            value = pre[j]
            sg[j, chunk(c), :] = value
            sg_o[j, chunk(c), :] = value.astype(BF)
            normed = (act[j, chunk(c), :] - center_w) * inverse_w
            return g8 + to_eight(value * normed), s8 + to_eight(value)

        g8, s8 = columns(one, (zero8, zero8))
        red[1] += g8
        red[2] += s8

    def second_step(c):
        second_chunk(c)
        pl.when(c < early)(lambda: send_out(*block_out, c))

    red[...] = jnp.zeros_like(red)
    loop(0, nch, second_step)
    loop(0, nch, second_kernel)
    core_start(SECOND, acc2)
    loop(0, nch, back_chunk)
    sums = [fold(total_row(red[k])) for k in (1, 2, 0)]
    share(y2, 1, jnp.concatenate(sums, axis=1))
    loop(0, nch, lambda c: edge_send(sg_o, sg_h, 3, c))
    loop(early, nch, lambda c: send_out(*block_out, c))

    chip_start(SECOND)
    sums = jnp.sum(shared(y2, 1), axis=0)
    gain_grad, shift_grad = sums[:, :C], sums[:, C : 2 * C]

    scale_w = twice(inverse * gain)
    shift_part = twice(shift_grad / total)
    gain_part = twice(gain_grad / total)

    scale_h = edges(inverse * gain)

    def act_grad(value, activation, here):
        normed = (activation - center_w) * inverse_w
        return value - here * shift_part - here * normed * gain_part

    def first_grad(c):
        def one(j, carry):
            grad = act_grad(sg[j, chunk(c), :], act[j, chunk(c), :], cnt[j, chunk(c), :])
            F[1 + j, chunk(c), own] = (scale_w * grad * slope[j, chunk(c), :]).astype(BF)
            return carry
        columns(one, 0)

    def first_grad_edge(c):
        edge_wait(sg_h, 3, c)

        def one(j, carry):
            theirs = sg_h[j, chunk(c), :].astype(F32)
            grad = act_grad(theirs, act_h[j, chunk(c), :], cnt_h[j, chunk(c), :])
            put_edges(F, j, c, scale_h * grad * slope_h[j, chunk(c), :])
            return carry
        columns(one, 0)
        wrap(F, c)

    def first_kernel(c):
        grad = F[1 : 1 + L, chunk(c), own].reshape(L * CH, W)
        kernel_grad(taps(X, c), grad, acc1)

    def field_chunk(c):
        first_grad_edge(c)
        out = jnp.dot(taps(F, c), t1[...], preferred_element_type=F32)
        fs[:, chunk(c), :] = out.astype(BF).reshape(L, CH, W)

    def send_field(c):
        send_out(*field_out, c)

    held = max(nch - 2, 1)
    def field_step(c):
        field_chunk(c)
        pl.when(c < held)(lambda: send_field(c))
        pl.when(c == 0)(lambda: chip_start(FIRST))

    loop(0, nch, first_grad)
    rows_x = jnp.concatenate([X[b : b + L].reshape(L * S, 4 * C) for b in range(3)], axis=1)
    acc1[...] = lax.dot_general(
        rows_x, F[1 : 1 + L, :, own].reshape(L * S, W), (((0,), (0,)), ((), ())), preferred_element_type=F32
    )
    core_start(FIRST, acc1)
    loop(0, nch, field_step)
    lon_start(SECOND)
    lon_start(FIRST)
    loop(held, nch - 1, send_field)
    loop(0, nch, finish_block)
    lon_finish(SECOND)
    lon_finish(FIRST)
    first_w, second_w = grads[0, 0 : z.wc], grads[1, 0 : z.wc]
    square = total_row(first_w * first_w + second_w * second_w)
    share(y3, 2, sum(square[:, cols_of(t)] for t in range(z.LP // C)))
    loop(max(held, nch - 1), nch, send_field)
    loop(0, nch - 1, finish_field)
    squares = jnp.sum(shared(y3, 2), axis=0)
    mine2 = sum(sums[:, cols_of(t)] * sums[:, cols_of(t)] for t in range(3))
    norm = jnp.sqrt(jnp.sum(squares + mine2, axis=1, keepdims=True))
    for k in range(3):
        grads[0, z.wc + k : z.wc + k + 1, 0:C] = sums[:, cols_of(k)]
    grads[0, z.wc + 3 : z.wc + 4, 0:C] = jnp.broadcast_to(norm, (1, C))

    finish_field(nch - 1)

    sent(sb.at[:, pl.ds(1, nlo - 1)], f_s.at[0])
    sent(cb.at[:, pl.ds(1, nlo - 1)], c_s.at[0])
    sent(cm.at[pl.ds(0, nlo - 1)], mask_s.at[0])
    halo_done(X, 0)
    edge_done(p_o, 1)
    halo_done(G, 2)
    edge_done(sg_o, 3)
    for side, pole in enumerate((north_pole, south_pole)):
        pl.when(jnp.logical_not(pole))(lambda: near_copy(side).wait_send())
    for k in range(2):
        sent(wg.at[pl.ds(0, nlo - 1), pl.ds(z.first[k], z.count[k])], wg_s.at[k])
        sent(kg_in.at[k, pl.ds(0, nla // 2 - 1)], kz_s.at[k])
        sent(kg_in.at[k, pl.ds(0, nla // 2)], kc_s.at[k])
        core_copy(k).wait_send()
        sent(zr.at[k, pl.ds(0, chips - 1)], rz_s.at[k])
        sent(lr.at[k, pl.ds(0, nlo - 1)], ro_s.at[k])
    sent(bo.at[pl.ds(0, Q * (nlo - 1))], bo_s.at[0])
    sent(fs.at[pl.ds(0, Q * (nlo - 1))], fo_s.at[0])


def adam_step(master, first, second, grads, rate, decay):
    first_new = BETA_ONE * first + (1.0 - BETA_ONE) * grads
    second_new = BETA_TWO * second + (1.0 - BETA_TWO) * grads * grads
    first_hat = first_new / (1.0 - BETA_ONE**STEP)
    second_hat = second_new / (1.0 - BETA_TWO**STEP)
    master_new = master - rate * (first_hat / (jnp.sqrt(second_hat) + ADAM_EPS) + decay * master)
    return master_new, first_new, second_new


def last_kernel(
    z,
    low, grad, grads, wm_h, wf_h, ws_h, vm_h, vf_h, vs_h,
    block_out, field_grad, norm_h, w_new_h, w_first_h, w_second_h, w_low_h, v_new_h, v_first_h, v_second_h,
    wm, wf, wsec, vm, vf, vs, norm, w_new, w_first, w_second, w_low, v_new, v_first, v_second,
    in_sem, out_sem,
):
    ins = ((wm_h, wm), (wf_h, wf), (ws_h, wsec), (vm_h, vm), (vf_h, vf), (vs_h, vs))
    loads = [pltpu.make_async_copy(src, dst, in_sem.at[i]) for i, (src, dst) in enumerate(ins)]
    for load in loads:
        load.start()
    outs = (
        (grad, field_grad), (low, block_out), (norm, norm_h), (w_new, w_new_h), (w_first, w_first_h),
        (w_second, w_second_h), (w_low, w_low_h), (v_new, v_new_h), (v_first, v_first_h), (v_second, v_second_h),
    )
    stores = [pltpu.make_async_copy(src, dst, out_sem.at[i]) for i, (src, dst) in enumerate(outs)]
    stores[0].start()
    stores[1].start()
    size = grads[0, z.wc + 3 : z.wc + 4, 0:C]
    norm[...] = size[:, 0:1]
    factor = jnp.minimum(1.0, MAX_NORM / size)
    wide = factor[:, 0:1]
    for load in loads:
        load.wait()
    for k in range(2):
        own = grads[k, 0 : z.wc, 0 : z.wr] * wide
        new, first, second = adam_step(wm[k], wf[k], wsec[k], own, RATE_KERNEL, DECAY)
        w_new[k], w_first[k], w_second[k] = new, first, second
        w_low[k] = new.astype(BF)
    for k in range(3):
        own = grads[0, z.wc + k : z.wc + k + 1, 0:C] * factor
        row = slice(k, k + 1)
        new, first, second = adam_step(vm[row, :], vf[row, :], vs[row, :], own, RATE_VECTOR, 0.0)
        v_new[row, :], v_first[row, :], v_second[row, :] = new, first, second
    for store in stores[2:]:
        store.start()
    for store in stores:
        store.wait()


def body(nla, nlo, fields, chan_mean, chan_std, sea_mask, missing, cotangent,
         w_master, w_first, w_second, vec_master, vec_first, vec_second):
    samples, rows, quads, channels = fields.shape
    z = Sizes(nla, nlo, samples, quads, w_master.shape[1], w_master.shape[2])
    S, L, Q, CH, nch, n, B = z.S, z.L, z.Q, z.CH, z.nch, z.n, z.B
    flat = (samples * rows * quads, channels)
    fields = fields.reshape(flat)
    cotangent = cotangent.reshape(flat)
    sea = jnp.transpose(sea_mask, (1, 2, 0))
    miss = jnp.transpose(missing, (1, 2, 0))
    wm, wf, wsec = (jnp.transpose(w, (0, 2, 1)) for w in (w_master, w_first, w_second))
    mean, std = chan_mean.reshape(1, C), chan_std.reshape(1, C)

    vmem = pl.BlockSpec(memory_space=pltpu.VMEM)
    hbm = pl.BlockSpec(memory_space=pl.ANY)
    V = pltpu.VMEM
    dma = pltpu.SemaphoreType.DMA
    shape = jax.ShapeDtypeStruct
    padded = V((L + 2, S, 2 * W), BF)
    wide = V((L, S, W), F32)
    scratch = [
        V((Q, B, W), BF), V((Q, B, W), BF), V(flat, BF), V(flat, BF), V(sea.shape, sea.dtype), V(miss.shape, miss.dtype),
        V((1, C), F32), V((1, C), F32), V(wm.shape, F32), V((3, C), F32),
        V((CH * z.PX, C), F32), V((B, z.PX), F32),
        V((nlo, z.PX, min(B, 128)), F32), V((nlo, z.PX, min(B, 128)), F32),
        V((2, nlo, z.PX, min(B, 128)), F32), wide,
        V((nch, nlo, Q, CH, W), BF), V((nch, nlo, Q, CH, W), BF),
        padded, padded, padded, padded, wide, wide, wide,
        V((L, S, W), BF), V((L, CH, W), F32), V((L, S, W), BF), V((L, S, W), BF), V((3, 8, W), F32),
        V((L, S, W), BF), V((L, S, W), BF), V((L, S, W), BF), V((L, S, W), BF), wide, wide, wide,
        V((12 * C, W), BF), V((12 * C, W), BF), V((12 * C, W), BF), V((12 * C, W), BF),
        V((12 * C, W), F32), V((12 * C, W), F32),
        V((z.pieces, z.wc, 128), BF), V((nlo, z.pieces, z.wc, 128), BF), V((2, nla, z.wr, C), BF),
        V((9 * C, C), F32), V((2, z.wr, C), BF),
        V((2, nla // 2, z.wr, C), BF), V((2, nla // 2, z.wr, C), BF),
        V((2, nla // 2, z.wr, C), BF), V((2, nla // 2, z.wr, C), BF), V((2, 9 * C, C), F32),
        V((2, z.LP, C), F32), V((2, C, z.LP), F32), V((2, nlo, z.wc, z.LP), BF), V((2, nlo, z.wc, z.LP), BF),
        V((n, 1, 3 * C), F32), V((n, 1, 3 * C), F32), V((n, 1, C), F32),
        dma((8,)), dma((1,)), dma((1,)), dma((1,)), dma((nch,)), dma((1,)), dma((nch,)),
        dma((4,)), dma((4, nch)),
        dma((1,)), dma((nch,)), dma((nch,)), dma((1,)), dma((nch,)), dma((nch,)), dma((2,)), dma((2,)),
        dma((2,)), dma((2,)), dma((2,)), dma((2,)),
        dma((2,)), dma((2,)), dma((2,)), dma((2,)), dma((2,)), dma((2,)), dma((3,)), dma((3,)),
        dma((2,)), dma((2,)),
    ]
    low, grad, grads = pl.pallas_call(
        functools.partial(main_kernel, z),
        out_shape=(V(flat, BF), V(flat, F32), V((2, z.wc + 8, z.LP), F32)),
        in_specs=[hbm] * 8,
        out_specs=(vmem, vmem, vmem),
        scratch_shapes=scratch,
        compiler_params=pltpu.CompilerParams(
            collective_id=0, has_side_effects=True, vmem_limit_bytes=59 * 2**20
        ),
        name="block",
    )(fields, cotangent, sea, miss, mean, std, wm, vec_master)

    shapes = [((1, 1), F32)] + [(wm.shape, F32)] * 3 + [(wm.shape, BF)] + [((3, C), F32)] * 3
    outs = pl.pallas_call(
        functools.partial(last_kernel, z),
        out_shape=[shape(flat, BF), shape(flat, F32)] + [shape(*v) for v in shapes],
        in_specs=[vmem] * 3 + [hbm] * 6,
        out_specs=[hbm] * 10,
        scratch_shapes=[V(wm.shape, F32)] * 3 + [V((3, C), F32)] * 3 + [V(*v) for v in shapes]
        + [dma((6,)), dma((10,))],
        compiler_params=pltpu.CompilerParams(vmem_limit_bytes=16 * 2**20),
        name="update",
    )(low, grad, grads, wm, wf, wsec, vec_master, vec_first, vec_second)
    block_out, field_grad, norm, w_new, w_f, w_s, w_low, v_new, v_f, v_s = outs
    like = (samples, rows, quads, channels)
    w_new, w_f, w_s, w_low = (jnp.transpose(w, (0, 2, 1)) for w in (w_new, w_f, w_s, w_low))
    return (
        block_out.reshape(like), field_grad.reshape(like), norm.reshape(()),
        w_new, w_f, w_s, w_low, v_new, v_f, v_s,
    )


def solution(mesh):
    tile, kernel = P(None, "lat", "lon", None), P(None, "lat", "lon")
    return jax.shard_map(
        functools.partial(body, mesh.shape["lat"], mesh.shape["lon"]),
        mesh=mesh,
        in_specs=(tile, P(), P(), kernel, kernel, tile, kernel, kernel, kernel, P(), P(), P()),
        out_specs=(tile, tile, P(), kernel, kernel, kernel, kernel, P(), P(), P()),
        check_vma=False,
    )
```
